32 devices in a mesh: groups: 2 (over x), pool: 16 (over z, y, core).
Axes of the slice: x: 2, y: 2, z: 4, core: 2. Of those that a mesh axis runs over, the one named last changes fastest.
Arguments:
- hidden: bfloat16 [64, 8192], P(('groups', 'pool')), parts along dimension 0, may hold values from -6 to 6
- gain: float32 [8192], replicated, may hold values from 0.1 to 1.9
- query_weight: bfloat16 [8192, 8192], P(None, 'pool'), may hold values from -0.0625 to 0.0625
- key_value_weight: bfloat16 [8192, 2048], P(None, 'pool'), may hold values from -0.0625 to 0.0625
- output_weight: bfloat16 [8192, 8192], P('pool'), may hold values from -0.5 to 0.5
- query_down_factor: bfloat16 [128, 8192, 16], P(('groups', 'pool')), parts along dimension 0, may hold values from -0.0625 to 0.0625
- query_up_factor: bfloat16 [128, 16, 8192], P(('groups', 'pool')), parts along dimension 0, may hold values from -1.5 to 1.5
- output_down_factor: bfloat16 [128, 8192, 16], P(('groups', 'pool')), parts along dimension 0, may hold values from -0.5 to 0.5
- output_up_factor: bfloat16 [128, 16, 8192], P(('groups', 'pool')), parts along dimension 0, may hold values from -1.5 to 1.5
- key_cache: bfloat16 [64, 512, 1024], P(('groups', 'pool')), parts along dimension 0, may hold values from -400 to 400
- value_cache: bfloat16 [64, 512, 1024], P(('groups', 'pool')), parts along dimension 0, may hold values from -6 to 6
- lengths: int32 [64], P(('groups', 'pool')), parts along dimension 0, may hold values from 1 to 512, as said below
- request_adapter: int32 [64], P(('groups', 'pool')), parts along dimension 0, may hold values from 0 to 63
- adapter_slot: int32 [128], P('groups'), parts along dimension 0, may hold values from 0 to 63, each once
Outputs:
- attn_out: bfloat16 [64, 8192], P(('groups', 'pool')), parts along dimension 0
The draws below stay inside these ranges and needn't reach their ends.
There are 2 independent parts, one for each index of `groups`. The reference program is written for one: setup_inputs(seed, part) draws one part's arguments, and reference() takes and returns one part's arrays. A program takes and returns all parts, laid end to end along the dimension named above; an argument that names none is the same for every part. Nothing has to cross between parts.
Inputs may be any that keep to these rules, and one draw needn't show every extreme that they name: `lengths`: some request of every replica holds exactly 512 positions. `adapter_slot`: each slot holds exactly one adapter; the slot s lies on the device of pool index s // 4.
All inputs are finite; a program needn't handle non-finite values.
Results may differ from the reference program's by a relative error of at most 0.007.
The reference program's roundings to bfloat16 on the way count: a program that leaves them out, or rounds other values in their place, can miss the bound.
Values may be sent and summed in bfloat16 or wider, within the bound.
No kernel may reach another device: no remote copies, remote signals or barrier semaphores. Data moves between devices by JAX's collectives and lax.ppermute only.
A program may use at most 128 MiB of HBM per device.

```python
import math
import jax
import jax.numpy as jnp
import numpy as np
from jax import lax

MODEL_WIDTH = 8192
H = 64
KVH = 8
HEAD_WIDTH = 128
ADAPTER_RANK = 16
CACHE = 512
QUERY_WIDTH = 8192
DKV = 1024
REQ = 32
POOL_SLOTS = 64


def draw_key_cache(key, part):
    key = jax.random.fold_in(key, 11)
    values = jnp.clip(jax.random.normal(key, (REQ, CACHE, DKV), jnp.float32), -5.0, 5.0)
    return values.astype(jnp.bfloat16)


def draw_lengths(key, part):
    key = jax.random.fold_in(key, 12)
    drawn = jax.random.randint(key, (REQ,), 1, CACHE + 1, dtype=jnp.int32)
    where_full = jax.random.randint(jax.random.fold_in(key, 1), (), 0, REQ, dtype=jnp.int32)
    return drawn.at[where_full].set(CACHE)


def with_ends(entries, key, smallest, high):
    longest = entries.shape.index(max(entries.shape))
    spots = []
    for shift in (0, 1):
        where = [jax.random.randint(jax.random.fold_in(key, axis), (), 0, length) for axis, length in enumerate(entries.shape)]
        where[longest] = (where[longest] + shift) % entries.shape[longest]
        spots.append(tuple(where))
    return entries.at[spots[0]].set(smallest).at[spots[1]].set(high)


def levels(key, shape, shards, least, top_value):
    loudness = 1.0
    for dim, blocks in shards:
        steps = jax.random.uniform(jax.random.fold_in(jax.random.fold_in(key, 6), dim), (blocks,), jnp.float32, least / len(shards), top_value / len(shards))
        loudness = loudness * jnp.repeat(jnp.exp(steps), shape[dim] // blocks).reshape((-1,) + (1,) * (len(shape) - 1 - dim))
    return loudness


def cumulative_ranks(number_of, slope):
    loads = [(1 << 20) // math.isqrt(standing ** slope) + 1 for standing in range(1, number_of + 1)]
    scale = 1 + sum(loads) // (1 << 30)
    return np.cumsum(np.array([max(1, weight // scale) for weight in loads]))


def skewed_ids(stream_key, shape, count, skew):
    listing = cumulative_ranks(count, skew)
    lot = jax.random.randint(jax.random.fold_in(stream_key, 1), shape, 0, int(listing[count - 1]))
    standing = jnp.searchsorted(jnp.asarray(listing, jnp.int32), lot, side="right")
    return jax.random.permutation(jax.random.fold_in(stream_key, 2), count)[standing].astype(jnp.int32)


def gaussian(rng, dims, scale, limit, shards=(), kind=jnp.bfloat16):
    values = jax.random.normal(rng, dims, jnp.float32) * scale
    if len(shards) > 0:
        values = levels(rng, dims, shards, -0.22, 0.18) * values
    return jnp.clip(values, min=-limit, max=limit).astype(kind)


def setup_inputs(seed: int = 0, part: int = 0) -> dict:
    splits = jax.random.split(jax.random.key(seed), 15)
    part_keys = jax.random.split(jax.random.fold_in(splits[14], part), 15)
    return {
        "hidden": gaussian(part_keys[0], (REQ, MODEL_WIDTH), 1.0, 6.0, ((0, 16),)),
        "gain": jnp.clip(1.0 + 0.18 * jax.random.normal(splits[1], (MODEL_WIDTH,), jnp.float32), 0.1, 1.9),
        "query_weight": gaussian(splits[2], (MODEL_WIDTH, QUERY_WIDTH), MODEL_WIDTH ** -0.5, 0.0625, ((1, 16),)),
        "key_value_weight": gaussian(splits[3], (MODEL_WIDTH, 2 * DKV), MODEL_WIDTH ** -0.5, 0.0625, ((1, 16),)),
        "output_weight": gaussian(splits[4], (QUERY_WIDTH, MODEL_WIDTH), HEAD_WIDTH ** -0.5, 0.5, ((0, 16),)),
        "query_down_factor": gaussian(part_keys[5], (POOL_SLOTS, MODEL_WIDTH, ADAPTER_RANK), MODEL_WIDTH ** -0.5, 0.0625, ((0, 16),)),
        "query_up_factor": gaussian(part_keys[6], (POOL_SLOTS, ADAPTER_RANK, QUERY_WIDTH), ADAPTER_RANK ** -0.5, 1.5, ((0, 16),)),
        "output_down_factor": gaussian(part_keys[7], (POOL_SLOTS, QUERY_WIDTH, ADAPTER_RANK), HEAD_WIDTH ** -0.5, 0.5, ((0, 16),)),
        "output_up_factor": gaussian(part_keys[8], (POOL_SLOTS, ADAPTER_RANK, MODEL_WIDTH), ADAPTER_RANK ** -0.5, 1.5, ((0, 16),)),
        "key_cache": draw_key_cache(jax.random.fold_in(jax.random.fold_in(splits[14], part), 71), part),
        "value_cache": gaussian(part_keys[10], (REQ, CACHE, DKV), 1.0, 6.0, ((0, 16),)),
        "lengths": draw_lengths(jax.random.fold_in(jax.random.fold_in(splits[14], part), 71), part),
        "request_adapter": with_ends(skewed_ids(part_keys[12], (REQ,), POOL_SLOTS, 2), jax.random.fold_in(part_keys[12], 3), 0, POOL_SLOTS - 1).astype(jnp.int32),
        "adapter_slot": jax.random.permutation(part_keys[13], POOL_SLOTS).astype(jnp.int32),
    }


adapter_scale = 0.5
norm_eps = 1e-05

def norm_rows(hidden, gain):
    values = hidden.astype(jnp.float32)
    factor = lax.rsqrt(lax.optimization_barrier(jnp.mean(values * values, axis=-1, keepdims=True)) + norm_eps)
    return (values * factor * gain).astype(jnp.bfloat16)

def attend_one(operands):
    query_row, keyval_row, cached_keys, cached_values, length = operands
    group_size = H // KVH
    heads_q = query_row.astype(jnp.float32).reshape(KVH, group_size, HEAD_WIDTH)
    new_keys = keyval_row[:DKV].astype(jnp.float32).reshape(KVH, HEAD_WIDTH)
    new_values = keyval_row[DKV:].astype(jnp.float32).reshape(KVH, HEAD_WIDTH)
    keys_f = cached_keys.astype(jnp.float32).reshape(CACHE, KVH, HEAD_WIDTH)
    values_f = cached_values.astype(jnp.float32).reshape(CACHE, KVH, HEAD_WIDTH)
    factor = HEAD_WIDTH ** (-0.5)
    scores = jnp.einsum('kgd,ckd->kgc', heads_q, keys_f) * factor
    own_score = jnp.einsum('kgd,kd->kg', heads_q, new_keys) * factor
    in_cache = (jnp.arange(CACHE, dtype=jnp.int32) < length)[None, None, :]
    scores = jnp.where(in_cache, scores, -1e+30)
    highest = jnp.maximum(lax.optimization_barrier(jnp.max(scores, axis=-1)), own_score)
    cached_exp = jnp.where(in_cache, jnp.exp(scores - highest[..., None]), 0.0)
    own_exp = jnp.exp(own_score - highest)
    softmax_sum = lax.optimization_barrier(jnp.sum(cached_exp, axis=-1)) + own_exp
    cached_weight = (cached_exp / softmax_sum[..., None]).astype(jnp.bfloat16)
    own_weight = (own_exp / softmax_sum).astype(jnp.bfloat16)
    mixture = jnp.einsum('kgc,ckd->kgd', cached_weight.astype(jnp.float32), values_f)
    mixture = mixture + own_weight.astype(jnp.float32)[..., None] * new_values[:, None, :]
    return mixture.reshape(KVH * group_size * HEAD_WIDTH).astype(jnp.bfloat16)

def reference(hidden, gain, query_weight, key_value_weight, output_weight, query_down_factor, query_up_factor, output_down_factor, output_up_factor, key_cache, value_cache, lengths, request_adapter, adapter_slot):
    normalized_input = norm_rows(hidden, gain)
    slot_ids = adapter_slot[request_adapter].astype(jnp.int32)

    def shrink_query(operands):
        value_row, pool_slot_index = operands
        return jnp.dot(value_row[None, :], query_down_factor[pool_slot_index], preferred_element_type=jnp.float32)[0]
    shrunk_q = lax.map(shrink_query, (normalized_input, slot_ids)).astype(jnp.bfloat16)

    def expand_query(operands):
        low_rank_rows, pool_slot_index = operands
        return jnp.dot(low_rank_rows[None, :], query_up_factor[pool_slot_index], preferred_element_type=jnp.float32)[0]
    query_delta = lax.map(expand_query, (shrunk_q, slot_ids))
    query_vectors = (jnp.dot(normalized_input, query_weight, preferred_element_type=jnp.float32) + adapter_scale * query_delta).astype(jnp.bfloat16)
    keyval = jnp.dot(normalized_input, key_value_weight, preferred_element_type=jnp.float32).astype(jnp.bfloat16)
    attention_output = lax.map(attend_one, (query_vectors, keyval, key_cache, value_cache, lengths))

    def shrink_output(operands):
        value_row, pool_slot_index = operands
        return jnp.dot(value_row[None, :], output_down_factor[pool_slot_index], preferred_element_type=jnp.float32)[0]
    output_shrunk = lax.map(shrink_output, (attention_output, slot_ids)).astype(jnp.bfloat16)

    def expand_output(operands):
        low_rank_rows, pool_slot_index = operands
        return jnp.dot(low_rank_rows[None, :], output_up_factor[pool_slot_index], preferred_element_type=jnp.float32)[0]
    output_delta = lax.map(expand_output, (output_shrunk, slot_ids))
    summed_rows = jnp.dot(attention_output, output_weight, preferred_element_type=jnp.float32) + adapter_scale * output_delta
    return summed_rows.astype(jnp.bfloat16)
```

```python
import jax
import jax.numpy as jnp
from jax import lax
from jax.sharding import PartitionSpec as P

MODEL_WIDTH = 8192
H = 64
KVH = 8
HEAD_WIDTH = 128
ADAPTER_RANK = 16
CACHE = 512
DKV = 1024


adapter_scale = 0.5
norm_eps = 1e-05


def norm_rows(hidden, gain):
    values = hidden.astype(jnp.float32)
    factor = lax.rsqrt(jnp.mean(values * values, axis=-1, keepdims=True) + norm_eps)
    return (values * factor * gain).astype(jnp.bfloat16)


def lookup_slots(all_ids, adapter_slot):
    table_size = adapter_slot.shape[0]
    matches = all_ids[:, None] == jnp.arange(table_size, dtype=jnp.int32)[None, :]
    return jnp.sum(jnp.where(matches, adapter_slot[None, :], 0), axis=1)


def attend(query_rows, keyval_rows, key_cache, value_cache, lengths):
    group_size = H // KVH
    local_rows = query_rows.shape[0]
    heads_q = query_rows.reshape(local_rows, KVH, group_size, HEAD_WIDTH)
    new_keys = keyval_rows[:, :DKV].reshape(local_rows, KVH, HEAD_WIDTH)
    new_values = keyval_rows[:, DKV:].reshape(local_rows, KVH, HEAD_WIDTH)
    cached_keys = key_cache.reshape(local_rows, CACHE, KVH, HEAD_WIDTH)
    cached_values = value_cache.reshape(local_rows, CACHE, KVH, HEAD_WIDTH)
    factor = HEAD_WIDTH ** (-0.5)
    scores = (
        jnp.einsum("rkgd,rckd->rkgc", heads_q, cached_keys, preferred_element_type=jnp.float32)
        * factor
    )
    own_score = (
        jnp.einsum("rkgd,rkd->rkg", heads_q, new_keys, preferred_element_type=jnp.float32) * factor
    )
    in_cache = (jnp.arange(CACHE, dtype=jnp.int32)[None, :] < lengths[:, None])[:, None, None, :]
    scores = jnp.where(in_cache, scores, -1e30)
    highest = jnp.maximum(jnp.max(scores, axis=-1), own_score)
    cached_exp = jnp.where(in_cache, jnp.exp(scores - highest[..., None]), 0.0)
    own_exp = jnp.exp(own_score - highest)
    softmax_sum = jnp.sum(cached_exp, axis=-1) + own_exp
    cached_weight = (cached_exp / softmax_sum[..., None]).astype(jnp.bfloat16)
    own_weight = (own_exp / softmax_sum).astype(jnp.bfloat16)
    mixture = jnp.einsum(
        "rkgc,rckd->rkgd", cached_weight, cached_values, preferred_element_type=jnp.float32
    )
    mixture = (
        mixture
        + own_weight.astype(jnp.float32)[..., None] * new_values.astype(jnp.float32)[:, :, None, :]
    )
    return mixture.reshape(local_rows, KVH * group_size * HEAD_WIDTH).astype(jnp.bfloat16)


def owner_shrunk(rows, down_factor, owner_mask):
    partial = jnp.einsum("we,bey->wby", rows, down_factor, preferred_element_type=jnp.float32)
    return jnp.sum(jnp.where(owner_mask[:, :, None], partial, 0.0), axis=1).astype(jnp.bfloat16)


def pool_size():
    return lax.axis_size("pool")


def gather_rows(rows):
    count = pool_size()
    me = lax.axis_index("pool")
    step = 4
    while step < count:
        other = lax.ppermute(rows, "pool", [(i, i ^ step) for i in range(count)])
        upper = (me & step) != 0
        first = jnp.where(upper, other, rows)
        second = jnp.where(upper, rows, other)
        rows = jnp.concatenate([first, second], axis=0)
        step *= 2
    fours = [[4 * k + j for j in range(4)] for k in range(count // 4)]
    width = rows.shape[-1]
    rows = lax.all_gather(rows, "pool", axis=0, axis_index_groups=fours)
    rows = rows.reshape(4, count // 4, -1, width).transpose(1, 0, 2, 3)
    return rows.reshape(-1, width)


def scatter_sums(partial):
    count = pool_size()
    me = lax.axis_index("pool")
    width = partial.shape[-1]
    blocks = partial.reshape(count // 2, 2, -1, width)
    odd = (me & 1) != 0
    keep = jnp.where(odd, blocks[:, 1], blocks[:, 0])
    give = jnp.where(odd, blocks[:, 0], blocks[:, 1])
    keep = keep + lax.ppermute(give, "pool", [(i, i ^ 1) for i in range(count)])
    same_core = [[2 * k + c for k in range(count // 2)] for c in range(2)]
    parts = lax.all_to_all(keep, "pool", 0, 0, tiled=True, axis_index_groups=same_core)
    return jnp.sum(parts, axis=0)


def body(
    hidden,
    gain,
    query_weight,
    key_value_weight,
    output_weight,
    query_down_factor,
    query_up_factor,
    output_down_factor,
    output_up_factor,
    key_cache,
    value_cache,
    lengths,
    request_adapter,
    adapter_slot,
):
    count = pool_size()
    own_slots = query_down_factor.shape[0]
    local_rows = hidden.shape[0]
    slot_total = adapter_slot.shape[0]
    col_width = query_weight.shape[1]

    up_blocks = query_up_factor.reshape(own_slots, ADAPTER_RANK, count, col_width)
    up_blocks = up_blocks.transpose(2, 0, 1, 3)
    column_up_factor = lax.all_to_all(up_blocks, "pool", 0, 0, tiled=True)
    column_up_factor = column_up_factor.reshape(slot_total * ADAPTER_RANK, col_width)

    normalized_input = norm_rows(hidden, gain)
    slot_ids = lookup_slots(request_adapter, adapter_slot)
    digits = jnp.stack([slot_ids // 32, slot_ids % 32], axis=1).astype(jnp.bfloat16)
    sent = jnp.concatenate([normalized_input, jnp.pad(digits, ((0, 0), (0, 126)))], axis=1)
    gathered = gather_rows(sent)
    gathered_rows = gathered[:, :MODEL_WIDTH]
    all_digits = gathered[:, MODEL_WIDTH : MODEL_WIDTH + 2].astype(jnp.int32)
    slot_ids = all_digits[:, 0] * 32 + all_digits[:, 1]
    request_total = gathered_rows.shape[0]

    slot_table = slot_ids[:, None] == jnp.arange(slot_total, dtype=jnp.int32)[None, :]
    first_slot = lax.axis_index("pool") * own_slots
    owner_mask = (
        slot_ids[:, None] == first_slot + jnp.arange(own_slots, dtype=jnp.int32)[None, :]
    )
    bf_zero = jnp.zeros((), jnp.bfloat16)

    own_shrunk = owner_shrunk(gathered_rows, query_down_factor, owner_mask)
    spread = jnp.broadcast_to(own_shrunk[None], (count,) + own_shrunk.shape)
    shrunk_q = jnp.sum(
        lax.all_to_all(spread, "pool", 0, 0, tiled=True).astype(jnp.float32), axis=0
    ).astype(jnp.bfloat16)
    picked = jnp.where(slot_table[:, :, None], shrunk_q[:, None, :], bf_zero)
    picked = picked.reshape(request_total, slot_total * ADAPTER_RANK)
    query_delta = jnp.dot(picked, column_up_factor, preferred_element_type=jnp.float32)
    query_cols = (
        jnp.dot(gathered_rows, query_weight, preferred_element_type=jnp.float32)
        + adapter_scale * query_delta
    ).astype(jnp.bfloat16)
    keyval_cols = jnp.dot(
        gathered_rows, key_value_weight, preferred_element_type=jnp.float32
    ).astype(jnp.bfloat16)
    both = jnp.concatenate([query_cols, keyval_cols], axis=1)
    both = lax.all_to_all(both.reshape(count, local_rows, -1), "pool", 0, 0, tiled=True)
    query_rows = both[:, :, :col_width].transpose(1, 0, 2).reshape(local_rows, -1)
    keyval_rows = both[:, :, col_width:].transpose(1, 0, 2).reshape(local_rows, -1)

    attention_output = attend(query_rows, keyval_rows, key_cache, value_cache, lengths)
    every_row = gather_rows(attention_output)
    out_width = output_weight.shape[0]
    columns = lax.dynamic_slice_in_dim(every_row, lax.axis_index("pool") * out_width, out_width, 1)
    output_shrunk = owner_shrunk(every_row, output_down_factor, owner_mask)
    lifted_rows = jnp.where(owner_mask[:, :, None], output_shrunk[:, None, :], bf_zero).reshape(
        request_total, own_slots * ADAPTER_RANK
    )
    up_rows = output_up_factor.reshape(own_slots * ADAPTER_RANK, MODEL_WIDTH)
    partial = jnp.dot(
        columns, output_weight, preferred_element_type=jnp.float32
    ) + adapter_scale * jnp.dot(lifted_rows, up_rows, preferred_element_type=jnp.float32)
    return scatter_sums(partial).astype(jnp.bfloat16)


def solution(mesh):
    placed = (
        P(("groups", "pool"), None),
        P(),
        P(None, "pool"),
        P(None, "pool"),
        P("pool", None),
        P(("groups", "pool"), None, None),
        P(("groups", "pool"), None, None),
        P(("groups", "pool"), None, None),
        P(("groups", "pool"), None, None),
        P(("groups", "pool"), None, None),
        P(("groups", "pool"), None, None),
        P(("groups", "pool")),
        P(("groups", "pool")),
        P("groups"),
    )
    return jax.shard_map(
        body, mesh=mesh, in_specs=placed, out_specs=P(("groups", "pool"), None), check_vma=False
    )
```

```python
import jax
import jax.numpy as jnp
from jax import lax
from jax.sharding import PartitionSpec as P

MODEL_WIDTH = 8192
H = 64
KVH = 8
HEAD_WIDTH = 128
ADAPTER_RANK = 16
CACHE = 512
DKV = 1024


adapter_scale = 0.5
norm_eps = 1e-05


def norm_rows(hidden, gain):
    values = hidden.astype(jnp.float32)
    factor = lax.rsqrt(jnp.mean(values * values, axis=-1, keepdims=True) + norm_eps)
    return (values * factor * gain).astype(jnp.bfloat16)


def lookup_slots(all_ids, adapter_slot):
    table_size = adapter_slot.shape[0]
    matches = all_ids[:, None] == jnp.arange(table_size, dtype=jnp.int32)[None, :]
    return jnp.sum(jnp.where(matches, adapter_slot[None, :], 0), axis=1)


def attend(query_rows, keyval_rows, key_cache, value_cache, lengths):
    group_size = H // KVH
    local_rows = query_rows.shape[0]
    heads_q = query_rows.reshape(local_rows, KVH, group_size, HEAD_WIDTH)
    new_keys = keyval_rows[:, :DKV].reshape(local_rows, KVH, HEAD_WIDTH)
    new_values = keyval_rows[:, DKV:].reshape(local_rows, KVH, HEAD_WIDTH)
    cached_keys = key_cache.reshape(local_rows, CACHE, KVH, HEAD_WIDTH)
    cached_values = value_cache.reshape(local_rows, CACHE, KVH, HEAD_WIDTH)
    factor = HEAD_WIDTH ** (-0.5)
    scores = (
        jnp.einsum("rkgd,rckd->rkgc", heads_q, cached_keys, preferred_element_type=jnp.float32)
        * factor
    )
    own_score = (
        jnp.einsum("rkgd,rkd->rkg", heads_q, new_keys, preferred_element_type=jnp.float32) * factor
    )
    in_cache = (jnp.arange(CACHE, dtype=jnp.int32)[None, :] < lengths[:, None])[:, None, None, :]
    scores = jnp.where(in_cache, scores, -1e30)
    highest = jnp.maximum(jnp.max(scores, axis=-1), own_score)
    cached_exp = jnp.where(in_cache, jnp.exp(scores - highest[..., None]), 0.0)
    own_exp = jnp.exp(own_score - highest)
    softmax_sum = jnp.sum(cached_exp, axis=-1) + own_exp
    cached_weight = (cached_exp / softmax_sum[..., None]).astype(jnp.bfloat16)
    own_weight = (own_exp / softmax_sum).astype(jnp.bfloat16)
    mixture = jnp.einsum(
        "rkgc,rckd->rkgd", cached_weight, cached_values, preferred_element_type=jnp.float32
    )
    mixture = (
        mixture
        + own_weight.astype(jnp.float32)[..., None] * new_values.astype(jnp.float32)[:, :, None, :]
    )
    return mixture.reshape(local_rows, KVH * group_size * HEAD_WIDTH).astype(jnp.bfloat16)


def owner_shrunk(rows, down_factor, owner_mask):
    partial = jnp.einsum("we,bey->wby", rows, down_factor, preferred_element_type=jnp.float32)
    return jnp.sum(jnp.where(owner_mask[:, :, None], partial, 0.0), axis=1).astype(jnp.bfloat16)


def pool_size():
    return lax.axis_size("pool")


def exchange_quads(rows, step):
    count = pool_size()
    me = lax.axis_index("pool")
    parts = [rows] + [
        lax.ppermute(rows, "pool", [(i, i ^ (k * step)) for i in range(count)]) for k in (1, 2, 3)
    ]
    low = (me & step) != 0
    high = (me & (2 * step)) != 0
    swapped = [
        jnp.where(low, parts[1], parts[0]),
        jnp.where(low, parts[0], parts[1]),
        jnp.where(low, parts[3], parts[2]),
        jnp.where(low, parts[2], parts[3]),
    ]
    return jnp.concatenate(
        [
            jnp.where(high, swapped[2], swapped[0]),
            jnp.where(high, swapped[3], swapped[1]),
            jnp.where(high, swapped[0], swapped[2]),
            jnp.where(high, swapped[1], swapped[3]),
        ],
        axis=0,
    )


def exchange_pair(rows, step):
    count = pool_size()
    upper = (lax.axis_index("pool") & step) != 0
    other = lax.ppermute(rows, "pool", [(i, i ^ step) for i in range(count)])
    return jnp.concatenate([jnp.where(upper, other, rows), jnp.where(upper, rows, other)], axis=0)


def gather_rows(rows):
    count = pool_size()
    step = 4
    while step < count:
        if step * 4 <= count:
            rows = exchange_quads(rows, step)
            step *= 4
        else:
            rows = exchange_pair(rows, step)
            step *= 2
    fours = [[4 * k + j for j in range(4)] for k in range(count // 4)]
    return lax.all_gather(rows, "pool", axis=0, axis_index_groups=fours, tiled=True)


def pool_blocks(rows):
    count = pool_size()
    blocks = rows.reshape(4, count // 4, rows.shape[0] // count, rows.shape[1])
    return blocks.transpose(1, 0, 2, 3).reshape(count, -1, rows.shape[1])


def scatter_sums(partial):
    count = pool_size()
    me = lax.axis_index("pool")
    width = partial.shape[-1]
    blocks = partial.reshape(2, 2, count // 4, -1, width)
    odd = (me & 1) != 0
    keep = jnp.where(odd, blocks[:, 1], blocks[:, 0])
    give = jnp.where(odd, blocks[:, 0], blocks[:, 1])
    keep = keep + lax.ppermute(give, "pool", [(i, i ^ 1) for i in range(count)])
    keep = keep.transpose(1, 0, 2, 3).reshape(count // 2, -1, width)
    same_core = [[2 * k + c for k in range(count // 2)] for c in range(2)]
    parts = lax.all_to_all(keep, "pool", 0, 0, tiled=True, axis_index_groups=same_core)
    return jnp.sum(parts, axis=0)


def body(
    hidden,
    gain,
    query_weight,
    key_value_weight,
    output_weight,
    query_down_factor,
    query_up_factor,
    output_down_factor,
    output_up_factor,
    key_cache,
    value_cache,
    lengths,
    request_adapter,
    adapter_slot,
):
    count = pool_size()
    own_slots = query_down_factor.shape[0]
    local_rows = hidden.shape[0]
    slot_total = adapter_slot.shape[0]
    col_width = query_weight.shape[1]

    up_blocks = query_up_factor.reshape(own_slots, ADAPTER_RANK, count, col_width)
    up_blocks = up_blocks.transpose(2, 0, 1, 3)
    column_up_factor = lax.all_to_all(up_blocks, "pool", 0, 0, tiled=True)
    column_up_factor = column_up_factor.reshape(slot_total * ADAPTER_RANK, col_width)

    normalized_input = norm_rows(hidden, gain)
    slot_ids = lookup_slots(request_adapter, adapter_slot)
    digits = jnp.stack([slot_ids // 32, slot_ids % 32], axis=1).astype(jnp.bfloat16)
    sent = jnp.concatenate([normalized_input, jnp.pad(digits, ((0, 0), (0, 126)))], axis=1)
    gathered = gather_rows(sent)
    gathered_rows = gathered[:, :MODEL_WIDTH]
    all_digits = gathered[:, MODEL_WIDTH : MODEL_WIDTH + 2].astype(jnp.int32)
    slot_ids = all_digits[:, 0] * 32 + all_digits[:, 1]
    request_total = gathered_rows.shape[0]

    slot_table = slot_ids[:, None] == jnp.arange(slot_total, dtype=jnp.int32)[None, :]
    first_slot = lax.axis_index("pool") * own_slots
    owner_mask = (
        slot_ids[:, None] == first_slot + jnp.arange(own_slots, dtype=jnp.int32)[None, :]
    )
    bf_zero = jnp.zeros((), jnp.bfloat16)

    own_shrunk = owner_shrunk(gathered_rows, query_down_factor, owner_mask)
    own_shrunk, column_up_factor = lax.optimization_barrier((own_shrunk, column_up_factor))
    spread = jnp.broadcast_to(own_shrunk[None], (count,) + own_shrunk.shape)
    shrunk_q = jnp.sum(
        lax.all_to_all(spread, "pool", 0, 0, tiled=True).astype(jnp.float32), axis=0
    ).astype(jnp.bfloat16)
    query_base = jnp.dot(gathered_rows, query_weight, preferred_element_type=jnp.float32)
    keyval_cols = jnp.dot(
        gathered_rows, key_value_weight, preferred_element_type=jnp.float32
    ).astype(jnp.bfloat16)
    query_base, keyval_cols, shrunk_q = lax.optimization_barrier(
        (query_base, keyval_cols, shrunk_q)
    )
    picked = jnp.where(slot_table[:, :, None], shrunk_q[:, None, :], bf_zero)
    picked = picked.reshape(request_total, slot_total * ADAPTER_RANK)
    query_delta = jnp.dot(picked, column_up_factor, preferred_element_type=jnp.float32)
    query_cols = (query_base + adapter_scale * query_delta).astype(jnp.bfloat16)
    both = pool_blocks(jnp.concatenate([query_cols, keyval_cols], axis=1))
    both = lax.all_to_all(both, "pool", 0, 0, tiled=True)
    query_rows = both[:, :, :col_width].transpose(1, 0, 2).reshape(local_rows, -1)
    keyval_rows = both[:, :, col_width:].transpose(1, 0, 2).reshape(local_rows, -1)

    attention_output = attend(query_rows, keyval_rows, key_cache, value_cache, lengths)
    every_row = gather_rows(attention_output)
    out_width = output_weight.shape[0]
    columns = lax.dynamic_slice_in_dim(every_row, lax.axis_index("pool") * out_width, out_width, 1)
    output_shrunk = owner_shrunk(every_row, output_down_factor, owner_mask)
    lifted_rows = jnp.where(owner_mask[:, :, None], output_shrunk[:, None, :], bf_zero).reshape(
        request_total, own_slots * ADAPTER_RANK
    )
    up_rows = output_up_factor.reshape(own_slots * ADAPTER_RANK, MODEL_WIDTH)
    partial = jnp.dot(
        columns, output_weight, preferred_element_type=jnp.float32
    ) + adapter_scale * jnp.dot(lifted_rows, up_rows, preferred_element_type=jnp.float32)
    return scatter_sums(partial).astype(jnp.bfloat16)


def solution(mesh):
    placed = (
        P(("groups", "pool"), None),
        P(),
        P(None, "pool"),
        P(None, "pool"),
        P("pool", None),
        P(("groups", "pool"), None, None),
        P(("groups", "pool"), None, None),
        P(("groups", "pool"), None, None),
        P(("groups", "pool"), None, None),
        P(("groups", "pool"), None, None),
        P(("groups", "pool"), None, None),
        P(("groups", "pool")),
        P(("groups", "pool")),
        P("groups"),
    )
    return jax.shard_map(
        body, mesh=mesh, in_specs=placed, out_specs=P(("groups", "pool"), None), check_vma=False
    )
```

```python
import jax
import jax.numpy as jnp
from jax import lax
from jax.sharding import PartitionSpec as P

MODEL_WIDTH = 8192
H = 64
KVH = 8
HEAD_WIDTH = 128
ADAPTER_RANK = 16
CACHE = 512
DKV = 1024


adapter_scale = 0.5
norm_eps = 1e-05


def norm_rows(hidden, gain):
    values = hidden.astype(jnp.float32)
    factor = lax.rsqrt(jnp.mean(values * values, axis=-1, keepdims=True) + norm_eps)
    return (values * factor * gain).astype(jnp.bfloat16)


def lookup_slots(all_ids, adapter_slot):
    table_size = adapter_slot.shape[0]
    matches = all_ids[:, None] == jnp.arange(table_size, dtype=jnp.int32)[None, :]
    return jnp.sum(jnp.where(matches, adapter_slot[None, :], 0), axis=1)


def attend(query_rows, keyval_rows, key_cache, value_cache, lengths):
    group_size = H // KVH
    local_rows = query_rows.shape[0]
    heads_q = query_rows.reshape(local_rows, KVH, group_size, HEAD_WIDTH)
    new_keys = keyval_rows[:, :DKV].reshape(local_rows, KVH, HEAD_WIDTH)
    new_values = keyval_rows[:, DKV:].reshape(local_rows, KVH, HEAD_WIDTH)
    cached_keys = key_cache.reshape(local_rows, CACHE, KVH, HEAD_WIDTH)
    cached_values = value_cache.reshape(local_rows, CACHE, KVH, HEAD_WIDTH)
    factor = HEAD_WIDTH ** (-0.5)
    scores = (
        jnp.einsum("rkgd,rckd->rkgc", heads_q, cached_keys, preferred_element_type=jnp.float32)
        * factor
    )
    own_score = (
        jnp.einsum("rkgd,rkd->rkg", heads_q, new_keys, preferred_element_type=jnp.float32) * factor
    )
    in_cache = (jnp.arange(CACHE, dtype=jnp.int32)[None, :] < lengths[:, None])[:, None, None, :]
    scores = jnp.where(in_cache, scores, -1e30)
    highest = jnp.maximum(jnp.max(scores, axis=-1), own_score)
    cached_exp = jnp.where(in_cache, jnp.exp(scores - highest[..., None]), 0.0)
    own_exp = jnp.exp(own_score - highest)
    softmax_sum = jnp.sum(cached_exp, axis=-1) + own_exp
    cached_weight = (cached_exp / softmax_sum[..., None]).astype(jnp.bfloat16)
    own_weight = (own_exp / softmax_sum).astype(jnp.bfloat16)
    mixture = jnp.einsum(
        "rkgc,rckd->rkgd", cached_weight, cached_values, preferred_element_type=jnp.float32
    )
    mixture = (
        mixture
        + own_weight.astype(jnp.float32)[..., None] * new_values.astype(jnp.float32)[:, :, None, :]
    )
    return mixture.reshape(local_rows, KVH * group_size * HEAD_WIDTH).astype(jnp.bfloat16)


def owner_shrunk(rows, down_factor, owner_mask):
    partial = jnp.einsum("we,bey->wby", rows, down_factor, preferred_element_type=jnp.float32)
    return jnp.sum(jnp.where(owner_mask[:, :, None], partial, 0.0), axis=1).astype(jnp.bfloat16)


def pool_size():
    return lax.axis_size("pool")


def exchange_quads(rows, step):
    count = pool_size()
    me = lax.axis_index("pool")
    parts = [rows] + [
        lax.ppermute(rows, "pool", [(i, i ^ (k * step)) for i in range(count)]) for k in (1, 2, 3)
    ]
    low = (me & step) != 0
    high = (me & (2 * step)) != 0
    swapped = [
        jnp.where(low, parts[1], parts[0]),
        jnp.where(low, parts[0], parts[1]),
        jnp.where(low, parts[3], parts[2]),
        jnp.where(low, parts[2], parts[3]),
    ]
    return jnp.concatenate(
        [
            jnp.where(high, swapped[2], swapped[0]),
            jnp.where(high, swapped[3], swapped[1]),
            jnp.where(high, swapped[0], swapped[2]),
            jnp.where(high, swapped[1], swapped[3]),
        ],
        axis=0,
    )


def exchange_pair(rows, step):
    count = pool_size()
    upper = (lax.axis_index("pool") & step) != 0
    other = lax.ppermute(rows, "pool", [(i, i ^ step) for i in range(count)])
    return jnp.concatenate([jnp.where(upper, other, rows), jnp.where(upper, rows, other)], axis=0)


def gather_rows(rows):
    count = pool_size()
    step = 4
    while step < count:
        if step * 4 <= count:
            rows = exchange_quads(rows, step)
            step *= 4
        else:
            rows = exchange_pair(rows, step)
            step *= 2
    fours = [[4 * k + j for j in range(4)] for k in range(count // 4)]
    return lax.all_gather(rows, "pool", axis=0, axis_index_groups=fours, tiled=True)


def core_halves(partial):
    count = pool_size()
    width = partial.shape[-1]
    blocks = partial.reshape(2, 2, count // 4, -1, width)
    odd = (lax.axis_index("pool") & 1) != 0
    keep = jnp.where(odd, blocks[:, 1], blocks[:, 0])
    give = jnp.where(odd, blocks[:, 0], blocks[:, 1])
    return (
        keep.transpose(1, 0, 2, 3).reshape(count // 2, -1, width),
        give.transpose(1, 0, 2, 3).reshape(count // 2, -1, width),
    )


def swap_cores(block):
    count = pool_size()
    return lax.ppermute(block, "pool", [(i, i ^ 1) for i in range(count)])


def exchange_chips(blocks):
    count = pool_size()
    same_core = [[2 * k + c for k in range(count // 2)] for c in range(2)]
    return lax.all_to_all(blocks, "pool", 0, 0, tiled=True, axis_index_groups=same_core)


def pair_columns(kept, received):
    odd = (lax.axis_index("pool") & 1) != 0
    return jnp.concatenate(
        [jnp.where(odd, received, kept), jnp.where(odd, kept, received)], axis=-1
    )


def body(
    hidden,
    gain,
    query_weight,
    key_value_weight,
    output_weight,
    query_down_factor,
    query_up_factor,
    output_down_factor,
    output_up_factor,
    key_cache,
    value_cache,
    lengths,
    request_adapter,
    adapter_slot,
):
    count = pool_size()
    own_slots = query_down_factor.shape[0]
    local_rows = hidden.shape[0]
    col_width = query_weight.shape[1]

    normalized_input = norm_rows(hidden, gain)
    slot_ids = lookup_slots(request_adapter, adapter_slot)
    digits = jnp.stack([slot_ids // 32, slot_ids % 32], axis=1).astype(jnp.bfloat16)
    sent = jnp.concatenate([normalized_input, jnp.pad(digits, ((0, 0), (0, 126)))], axis=1)
    gathered = gather_rows(sent)
    gathered_rows = gathered[:, :MODEL_WIDTH]
    all_digits = gathered[:, MODEL_WIDTH : MODEL_WIDTH + 2].astype(jnp.int32)
    slot_ids = all_digits[:, 0] * 32 + all_digits[:, 1]
    request_total = gathered_rows.shape[0]

    first_slot = lax.axis_index("pool") * own_slots
    owner_mask = (
        slot_ids[:, None] == first_slot + jnp.arange(own_slots, dtype=jnp.int32)[None, :]
    )
    bf_zero = jnp.zeros((), jnp.bfloat16)

    query_shrunk = owner_shrunk(gathered_rows, query_down_factor, owner_mask)
    lifted_rows = jnp.where(owner_mask[:, :, None], query_shrunk[:, None, :], bf_zero).reshape(
        request_total, own_slots * ADAPTER_RANK
    )
    query_delta = adapter_scale * jnp.dot(
        lifted_rows,
        query_up_factor.reshape(own_slots * ADAPTER_RANK, -1),
        preferred_element_type=jnp.float32,
    )
    kept_delta, given_delta = core_halves(query_delta)
    received_delta = swap_cores(given_delta)
    base = jnp.concatenate(
        [
            jnp.dot(gathered_rows, query_weight, preferred_element_type=jnp.float32),
            jnp.dot(gathered_rows, key_value_weight, preferred_element_type=jnp.float32),
        ],
        axis=1,
    )
    kept_base, given_base = core_halves(base)
    received_base = swap_cores(given_base)
    pair_query = pair_columns(kept_base[:, :, :col_width], received_base[:, :, :col_width])
    pair_keyval = pair_columns(kept_base[:, :, col_width:], received_base[:, :, col_width:])
    pair_delta = kept_delta + received_delta
    first_column = (lax.axis_index("pool") // 2) * (2 * col_width)
    there = lax.dynamic_slice_in_dim(pair_delta, first_column, 2 * col_width, 2)
    pair_delta = lax.dynamic_update_slice_in_dim(pair_delta, there + pair_query, first_column, 2)
    arrived = exchange_chips(jnp.concatenate([pair_delta, pair_keyval], axis=2))
    query_width = pair_delta.shape[2]
    query_rows = jnp.sum(arrived[:, :, :query_width], axis=0).astype(jnp.bfloat16)
    keyval_rows = arrived[:, :, query_width:].astype(jnp.bfloat16)
    keyval_rows = keyval_rows.reshape(count // 2, local_rows, 2, -1)
    keyval_rows = keyval_rows.transpose(1, 0, 2, 3).reshape(local_rows, -1)

    attention_output = attend(query_rows, keyval_rows, key_cache, value_cache, lengths)
    every_row = gather_rows(attention_output)
    out_width = output_weight.shape[0]
    columns = lax.dynamic_slice_in_dim(every_row, lax.axis_index("pool") * out_width, out_width, 1)
    output_shrunk = owner_shrunk(every_row, output_down_factor, owner_mask)
    lifted_rows = jnp.where(owner_mask[:, :, None], output_shrunk[:, None, :], bf_zero).reshape(
        request_total, own_slots * ADAPTER_RANK
    )
    up_rows = output_up_factor.reshape(own_slots * ADAPTER_RANK, MODEL_WIDTH)
    partial = jnp.dot(
        columns, output_weight, preferred_element_type=jnp.float32
    ) + adapter_scale * jnp.dot(lifted_rows, up_rows, preferred_element_type=jnp.float32)
    kept, given = core_halves(partial)
    arrived = exchange_chips(kept + swap_cores(given))
    return jnp.sum(arrived, axis=0).astype(jnp.bfloat16)


def solution(mesh):
    placed = (
        P(("groups", "pool"), None),
        P(),
        P(None, "pool"),
        P(None, "pool"),
        P("pool", None),
        P(("groups", "pool"), None, None),
        P(("groups", "pool"), None, None),
        P(("groups", "pool"), None, None),
        P(("groups", "pool"), None, None),
        P(("groups", "pool"), None, None),
        P(("groups", "pool"), None, None),
        P(("groups", "pool")),
        P(("groups", "pool")),
        P("groups"),
    )
    return jax.shard_map(
        body, mesh=mesh, in_specs=placed, out_specs=P(("groups", "pool"), None), check_vma=False
    )
```

```python
import jax
import jax.numpy as jnp
from jax import lax
from jax.experimental import pallas as pl
from jax.experimental.pallas import tpu as pltpu
from jax.sharding import PartitionSpec as P

MODEL_WIDTH = 8192
H = 64
KVH = 8
HEAD_WIDTH = 128
ADAPTER_RANK = 16
CACHE = 512
DKV = 1024


adapter_scale = 0.5
norm_eps = 1e-05


def norm_rows(hidden, gain):
    values = hidden.astype(jnp.float32)
    factor = lax.rsqrt(jnp.mean(values * values, axis=-1, keepdims=True) + norm_eps)
    return (values * factor * gain).astype(jnp.bfloat16)


def lookup_slots(all_ids, adapter_slot):
    table_size = adapter_slot.shape[0]
    matches = all_ids[:, None] == jnp.arange(table_size, dtype=jnp.int32)[None, :]
    return jnp.sum(jnp.where(matches, adapter_slot[None, :], 0), axis=1)


def attend(query_rows, keyval_rows, key_cache, value_cache, lengths):
    group_size = H // KVH
    local_rows = query_rows.shape[0]
    heads_q = query_rows.reshape(local_rows, KVH, group_size, HEAD_WIDTH)
    new_keys = keyval_rows[:, :DKV].reshape(local_rows, KVH, HEAD_WIDTH)
    new_values = keyval_rows[:, DKV:].reshape(local_rows, KVH, HEAD_WIDTH)
    cached_keys = key_cache.reshape(local_rows, CACHE, KVH, HEAD_WIDTH)
    cached_values = value_cache.reshape(local_rows, CACHE, KVH, HEAD_WIDTH)
    factor = HEAD_WIDTH ** (-0.5)
    scores = (
        jnp.einsum("rkgd,rckd->rkgc", heads_q, cached_keys, preferred_element_type=jnp.float32)
        * factor
    )
    own_score = (
        jnp.einsum("rkgd,rkd->rkg", heads_q, new_keys, preferred_element_type=jnp.float32) * factor
    )
    in_cache = (jnp.arange(CACHE, dtype=jnp.int32)[None, :] < lengths[:, None])[:, None, None, :]
    scores = jnp.where(in_cache, scores, -1e30)
    highest = jnp.maximum(jnp.max(scores, axis=-1), own_score)
    cached_exp = jnp.where(in_cache, jnp.exp(scores - highest[..., None]), 0.0)
    own_exp = jnp.exp(own_score - highest)
    softmax_sum = jnp.sum(cached_exp, axis=-1) + own_exp
    cached_weight = (cached_exp / softmax_sum[..., None]).astype(jnp.bfloat16)
    own_weight = (own_exp / softmax_sum).astype(jnp.bfloat16)
    mixture = jnp.einsum(
        "rkgc,rckd->rkgd", cached_weight, cached_values, preferred_element_type=jnp.float32
    )
    mixture = (
        mixture
        + own_weight.astype(jnp.float32)[..., None] * new_values.astype(jnp.float32)[:, :, None, :]
    )
    return mixture.reshape(local_rows, KVH * group_size * HEAD_WIDTH).astype(jnp.bfloat16)


def owner_shrunk(rows, down_factor, owner_mask):
    partial = jnp.einsum("we,bey->wby", rows, down_factor, preferred_element_type=jnp.float32)
    return jnp.sum(jnp.where(owner_mask[:, :, None], partial, 0.0), axis=1).astype(jnp.bfloat16)


def pool_size():
    return lax.axis_size("pool")


def exchange_quads(rows, step):
    count = pool_size()
    me = lax.axis_index("pool")
    parts = [rows] + [
        lax.ppermute(rows, "pool", [(i, i ^ (k * step)) for i in range(count)]) for k in (1, 2, 3)
    ]
    low = (me & step) != 0
    high = (me & (2 * step)) != 0
    swapped = [
        jnp.where(low, parts[1], parts[0]),
        jnp.where(low, parts[0], parts[1]),
        jnp.where(low, parts[3], parts[2]),
        jnp.where(low, parts[2], parts[3]),
    ]
    return jnp.concatenate(
        [
            jnp.where(high, swapped[2], swapped[0]),
            jnp.where(high, swapped[3], swapped[1]),
            jnp.where(high, swapped[0], swapped[2]),
            jnp.where(high, swapped[1], swapped[3]),
        ],
        axis=0,
    )


def exchange_pair(rows, step):
    count = pool_size()
    upper = (lax.axis_index("pool") & step) != 0
    other = lax.ppermute(rows, "pool", [(i, i ^ step) for i in range(count)])
    return jnp.concatenate([jnp.where(upper, other, rows), jnp.where(upper, rows, other)], axis=0)


def gather_rows(rows):
    count = pool_size()
    step = 4
    while step < count:
        if step * 4 <= count:
            rows = exchange_quads(rows, step)
            step *= 4
        else:
            rows = exchange_pair(rows, step)
            step *= 2
    fours = [[4 * k + j for j in range(4)] for k in range(count // 4)]
    return lax.all_gather(rows, "pool", axis=0, axis_index_groups=fours, tiled=True)


def core_halves(partial):
    count = pool_size()
    width = partial.shape[-1]
    blocks = partial.reshape(2, 2, count // 4, -1, width)
    odd = (lax.axis_index("pool") & 1) != 0
    keep = jnp.where(odd, blocks[:, 1], blocks[:, 0])
    give = jnp.where(odd, blocks[:, 0], blocks[:, 1])
    return (
        keep.transpose(1, 0, 2, 3).reshape(count // 2, -1, width),
        give.transpose(1, 0, 2, 3).reshape(count // 2, -1, width),
    )


def swap_cores(block):
    count = pool_size()
    return lax.ppermute(block, "pool", [(i, i ^ 1) for i in range(count)])


def exchange_chips(blocks):
    count = pool_size()
    same_core = [[2 * k + c for k in range(count // 2)] for c in range(2)]
    return lax.all_to_all(blocks, "pool", 0, 0, tiled=True, axis_index_groups=same_core)


def pair_columns(kept, received):
    odd = (lax.axis_index("pool") & 1) != 0
    return jnp.concatenate(
        [jnp.where(odd, received, kept), jnp.where(odd, kept, received)], axis=-1
    )


CHUNKS = 8
LANES = 128
KERNEL_VMEM = 52 * 1024 * 1024


def whole_block(shape):
    return pl.BlockSpec(shape, lambda: (0,) * len(shape))


def own_lift(rows_ref, down_ref, marks_ref, first_slot):
    ranks = down_ref.shape[0]
    width = down_ref.shape[1]
    step = width // CHUNKS
    total = None
    for k in range(CHUNKS):
        part = lax.dot_general(
            rows_ref[:, k * step : (k + 1) * step],
            down_ref[:, k * step : (k + 1) * step],
            (((1,), (1,)), ((), ())),
            preferred_element_type=jnp.float32,
        )
        total = part if total is None else total + part
    marks = marks_ref[...].astype(jnp.float32)
    slots = (marks[:, 0:1] * 32.0 + marks[:, 1:2]).astype(jnp.int32)
    place = lax.broadcasted_iota(jnp.int32, total.shape, 1) // ADAPTER_RANK + first_slot
    return jnp.where(slots == place, total, 0.0).astype(jnp.bfloat16)


def split_store(values, odd, kept_ref, given_ref, first, add):
    width = values.shape[1]
    size = values.shape[0] // 4
    local = kept_ref.shape[1]
    spot = pl.ds(first, width)
    for y in range(2):
        even_rows = values[2 * y * size : (2 * y + 1) * size]
        odd_rows = values[(2 * y + 1) * size : (2 * y + 2) * size]
        kept = jnp.where(odd, odd_rows, even_rows)
        given = jnp.where(odd, even_rows, odd_rows)
        for z in range(size // local):
            k = 2 * z + y
            kept_piece = kept[z * local : (z + 1) * local]
            given_piece = given[z * local : (z + 1) * local]
            if add:
                kept_piece = kept_piece + kept_ref[k, :, spot]
                given_piece = given_piece + given_ref[k, :, spot]
            kept_ref[k, :, spot] = kept_piece
            given_ref[k, :, spot] = given_piece


def query_kernel(
    where_ref, rows_ref, marks_ref, query_hbm, keyval_hbm, down_hbm, up_hbm,
    kept_ref, given_ref, query_vmem, keyval_vmem, down_vmem, up_vmem, sems,
):
    me = where_ref[0]
    odd = (me % 2) == 1
    width = down_vmem.shape[1]
    step = width // CHUNKS
    down_copy = pltpu.make_async_copy(down_hbm, down_vmem, sems.at[CHUNKS])
    up_copy = pltpu.make_async_copy(up_hbm, up_vmem, sems.at[CHUNKS + 1])
    keyval_copy = pltpu.make_async_copy(keyval_hbm, keyval_vmem, sems.at[CHUNKS + 2])
    query_copies = [
        pltpu.make_async_copy(
            query_hbm.at[pl.ds(k * step, step)], query_vmem.at[pl.ds(k * step, step)], sems.at[k]
        )
        for k in range(CHUNKS)
    ]
    down_copy.start()
    up_copy.start()
    for copy in query_copies:
        copy.start()
    keyval_copy.start()
    down_copy.wait()
    lifted = own_lift(rows_ref, down_vmem, marks_ref, where_ref[1])
    up_copy.wait()
    for k in range(CHUNKS):
        spot = slice(k * step, (k + 1) * step)
        delta = adapter_scale * jnp.dot(
            lifted, up_vmem[:, spot], preferred_element_type=jnp.float32
        )
        split_store(delta, odd, kept_ref, given_ref, k * step, False)
    query = None
    for k in range(CHUNKS):
        spot = slice(k * step, (k + 1) * step)
        query_copies[k].wait()
        part = jnp.dot(rows_ref[:, spot], query_vmem[spot], preferred_element_type=jnp.float32)
        query = part if query is None else query + part
    columns = query.shape[1]
    split_store(
        query, odd, kept_ref, given_ref, pl.multiple_of(me * columns, LANES), True
    )
    keyval_copy.wait()
    keyval = None
    for k in range(CHUNKS):
        spot = slice(k * step, (k + 1) * step)
        part = jnp.dot(rows_ref[:, spot], keyval_vmem[spot], preferred_element_type=jnp.float32)
        keyval = part if keyval is None else keyval + part
    none = jnp.zeros_like(keyval)
    both = jnp.concatenate([jnp.where(odd, none, keyval), jnp.where(odd, keyval, none)], axis=1)
    split_store(both, odd, kept_ref, given_ref, width, False)


def query_halves(where, gathered, query_weight, key_value_weight, down, up, count, local_rows):
    rows = gathered.shape[0]
    width, columns = query_weight.shape
    keyval_columns = key_value_weight.shape[1]
    ranks = down.shape[0]
    sent = jax.ShapeDtypeStruct(
        (count // 2, local_rows, width + 2 * keyval_columns), jnp.float32
    )
    return pl.pallas_call(
        query_kernel,
        in_specs=[
            pl.BlockSpec(memory_space=pltpu.SMEM),
            whole_block((rows, width)),
            whole_block((rows, LANES)),
        ]
        + [pl.BlockSpec(memory_space=pl.ANY)] * 4,
        out_specs=[whole_block(sent.shape)] * 2,
        out_shape=[sent, sent],
        scratch_shapes=[
            pltpu.VMEM((width, columns), jnp.bfloat16),
            pltpu.VMEM((width, keyval_columns), jnp.bfloat16),
            pltpu.VMEM((ranks, width), jnp.bfloat16),
            pltpu.VMEM((ranks, width), jnp.bfloat16),
            pltpu.SemaphoreType.DMA((CHUNKS + 3,)),
        ],
        compiler_params=pltpu.CompilerParams(vmem_limit_bytes=KERNEL_VMEM),
        name="query_halves",
    )(where, gathered[:, :width], gathered[:, width:], query_weight, key_value_weight, down, up)


def output_kernel(
    where_ref, rows_ref, marks_ref, output_hbm, down_hbm, up_hbm,
    kept_ref, given_ref, output_vmem, down_vmem, up_vmem, sems,
):
    me = where_ref[0]
    odd = (me % 2) == 1
    depth, width = output_vmem.shape
    step = width // CHUNKS
    down_copy = pltpu.make_async_copy(down_hbm, down_vmem, sems.at[CHUNKS])
    up_copy = pltpu.make_async_copy(up_hbm, up_vmem, sems.at[CHUNKS + 1])
    output_copies = [
        pltpu.make_async_copy(
            output_hbm.at[:, pl.ds(k * step, step)],
            output_vmem.at[:, pl.ds(k * step, step)],
            sems.at[k],
        )
        for k in range(CHUNKS)
    ]
    down_copy.start()
    up_copy.start()
    for copy in output_copies:
        copy.start()
    down_copy.wait()
    lifted = own_lift(rows_ref, down_vmem, marks_ref, where_ref[1])
    columns = rows_ref[:, pl.ds(pl.multiple_of(me * depth, LANES), depth)]
    up_copy.wait()
    for k in range(CHUNKS):
        spot = slice(k * step, (k + 1) * step)
        output_copies[k].wait()
        part = jnp.dot(columns, output_vmem[:, spot], preferred_element_type=jnp.float32)
        part = part + adapter_scale * jnp.dot(
            lifted, up_vmem[:, spot], preferred_element_type=jnp.float32
        )
        split_store(part, odd, kept_ref, given_ref, k * step, False)


def output_halves(where, every_row, gathered, output_weight, down, up, count, local_rows):
    rows = every_row.shape[0]
    depth, width = output_weight.shape
    ranks = down.shape[0]
    sent = jax.ShapeDtypeStruct((count // 2, local_rows, width), jnp.float32)
    return pl.pallas_call(
        output_kernel,
        in_specs=[
            pl.BlockSpec(memory_space=pltpu.SMEM),
            whole_block((rows, width)),
            whole_block((rows, LANES)),
        ]
        + [pl.BlockSpec(memory_space=pl.ANY)] * 3,
        out_specs=[whole_block(sent.shape)] * 2,
        out_shape=[sent, sent],
        scratch_shapes=[
            pltpu.VMEM((depth, width), jnp.bfloat16),
            pltpu.VMEM((ranks, width), jnp.bfloat16),
            pltpu.VMEM((ranks, width), jnp.bfloat16),
            pltpu.SemaphoreType.DMA((CHUNKS + 2,)),
        ],
        compiler_params=pltpu.CompilerParams(vmem_limit_bytes=KERNEL_VMEM),
        name="output_halves",
    )(where, every_row, gathered[:, width:], output_weight, down, up)


def by_rank(factor):
    return factor.transpose(0, 2, 1).reshape(-1, factor.shape[1])


def body(
    hidden,
    gain,
    query_weight,
    key_value_weight,
    output_weight,
    query_down_factor,
    query_up_factor,
    output_down_factor,
    output_up_factor,
    key_cache,
    value_cache,
    lengths,
    request_adapter,
    adapter_slot,
):
    count = pool_size()
    own_slots = query_down_factor.shape[0]
    local_rows = hidden.shape[0]
    col_width = query_weight.shape[1]

    normalized_input = norm_rows(hidden, gain)
    slot_ids = lookup_slots(request_adapter, adapter_slot)
    digits = jnp.stack([slot_ids // 32, slot_ids % 32], axis=1).astype(jnp.bfloat16)
    sent = jnp.concatenate([normalized_input, jnp.pad(digits, ((0, 0), (0, 126)))], axis=1)
    gathered = gather_rows(sent)
    gathered_rows = gathered[:, :MODEL_WIDTH]
    all_digits = gathered[:, MODEL_WIDTH : MODEL_WIDTH + 2].astype(jnp.int32)
    slot_ids = all_digits[:, 0] * 32 + all_digits[:, 1]
    request_total = gathered_rows.shape[0]

    first_slot = lax.axis_index("pool") * own_slots
    owner_mask = (
        slot_ids[:, None] == first_slot + jnp.arange(own_slots, dtype=jnp.int32)[None, :]
    )
    bf_zero = jnp.zeros((), jnp.bfloat16)

    aligned = col_width % LANES == 0 and key_value_weight.shape[1] % LANES == 0
    query_width = MODEL_WIDTH
    if aligned:
        where = jnp.stack([lax.axis_index("pool"), first_slot]).astype(jnp.int32)
        kept, given = query_halves(
            where,
            gathered,
            query_weight,
            key_value_weight,
            by_rank(query_down_factor),
            query_up_factor.reshape(own_slots * ADAPTER_RANK, -1),
            count,
            local_rows,
        )
        leaving = kept + swap_cores(given)
    else:
        query_shrunk = owner_shrunk(gathered_rows, query_down_factor, owner_mask)
        lifted_rows = jnp.where(owner_mask[:, :, None], query_shrunk[:, None, :], bf_zero).reshape(
            request_total, own_slots * ADAPTER_RANK
        )
        query_delta = adapter_scale * jnp.dot(
            lifted_rows,
            query_up_factor.reshape(own_slots * ADAPTER_RANK, -1),
            preferred_element_type=jnp.float32,
        )
        kept_delta, given_delta = core_halves(query_delta)
        received_delta = swap_cores(given_delta)
        base = jnp.concatenate(
            [
                jnp.dot(gathered_rows, query_weight, preferred_element_type=jnp.float32),
                jnp.dot(gathered_rows, key_value_weight, preferred_element_type=jnp.float32),
            ],
            axis=1,
        )
        kept_base, given_base = core_halves(base)
        received_base = swap_cores(given_base)
        pair_query = pair_columns(kept_base[:, :, :col_width], received_base[:, :, :col_width])
        pair_keyval = pair_columns(kept_base[:, :, col_width:], received_base[:, :, col_width:])
        pair_delta = kept_delta + received_delta
        first_column = (lax.axis_index("pool") // 2) * (2 * col_width)
        there = lax.dynamic_slice_in_dim(pair_delta, first_column, 2 * col_width, 2)
        pair_delta = lax.dynamic_update_slice_in_dim(pair_delta, there + pair_query, first_column, 2)
        leaving = jnp.concatenate([pair_delta, pair_keyval], axis=2)
    arrived = exchange_chips(leaving)
    query_rows = jnp.sum(arrived[:, :, :query_width], axis=0).astype(jnp.bfloat16)
    keyval_rows = arrived[:, :, query_width:].astype(jnp.bfloat16)
    keyval_rows = keyval_rows.reshape(count // 2, local_rows, 2, -1)
    keyval_rows = keyval_rows.transpose(1, 0, 2, 3).reshape(local_rows, -1)

    attention_output = attend(query_rows, keyval_rows, key_cache, value_cache, lengths)
    every_row = gather_rows(attention_output)
    if aligned:
        kept, given = output_halves(
            where,
            every_row,
            gathered,
            output_weight,
            by_rank(output_down_factor),
            output_up_factor.reshape(own_slots * ADAPTER_RANK, -1),
            count,
            local_rows,
        )
    else:
        out_width = output_weight.shape[0]
        columns = lax.dynamic_slice_in_dim(every_row, lax.axis_index("pool") * out_width, out_width, 1)
        output_shrunk = owner_shrunk(every_row, output_down_factor, owner_mask)
        lifted_rows = jnp.where(owner_mask[:, :, None], output_shrunk[:, None, :], bf_zero).reshape(
            request_total, own_slots * ADAPTER_RANK
        )
        up_rows = output_up_factor.reshape(own_slots * ADAPTER_RANK, MODEL_WIDTH)
        partial = jnp.dot(
            columns, output_weight, preferred_element_type=jnp.float32
        ) + adapter_scale * jnp.dot(lifted_rows, up_rows, preferred_element_type=jnp.float32)
        kept, given = core_halves(partial)
    arrived = exchange_chips(kept + swap_cores(given))
    return jnp.sum(arrived, axis=0).astype(jnp.bfloat16)


def solution(mesh):
    placed = (
        P(("groups", "pool"), None),
        P(),
        P(None, "pool"),
        P(None, "pool"),
        P("pool", None),
        P(("groups", "pool"), None, None),
        P(("groups", "pool"), None, None),
        P(("groups", "pool"), None, None),
        P(("groups", "pool"), None, None),
        P(("groups", "pool"), None, None),
        P(("groups", "pool"), None, None),
        P(("groups", "pool")),
        P(("groups", "pool")),
        P("groups"),
    )
    return jax.shard_map(
        body, mesh=mesh, in_specs=placed, out_specs=P(("groups", "pool"), None), check_vma=False
    )
```

```python
import jax
import jax.numpy as jnp
from jax import lax
from jax.experimental import pallas as pl
from jax.experimental.pallas import tpu as pltpu
from jax.sharding import PartitionSpec as P

MODEL_WIDTH = 8192
H = 64
KVH = 8
HEAD_WIDTH = 128
ADAPTER_RANK = 16
CACHE = 512
DKV = 1024


adapter_scale = 0.5
norm_eps = 1e-05


def norm_rows(hidden, gain):
    values = hidden.astype(jnp.float32)
    factor = lax.rsqrt(jnp.mean(values * values, axis=-1, keepdims=True) + norm_eps)
    return (values * factor * gain).astype(jnp.bfloat16)


def lookup_slots(all_ids, adapter_slot):
    table_size = adapter_slot.shape[0]
    matches = all_ids[:, None] == jnp.arange(table_size, dtype=jnp.int32)[None, :]
    return jnp.sum(jnp.where(matches, adapter_slot[None, :], 0), axis=1)


def attend(query_rows, keyval_rows, key_cache, value_cache, lengths):
    group_size = H // KVH
    local_rows = query_rows.shape[0]
    heads_q = query_rows.reshape(local_rows, KVH, group_size, HEAD_WIDTH)
    new_keys = keyval_rows[:, :DKV].reshape(local_rows, KVH, HEAD_WIDTH)
    new_values = keyval_rows[:, DKV:].reshape(local_rows, KVH, HEAD_WIDTH)
    cached_keys = key_cache.reshape(local_rows, CACHE, KVH, HEAD_WIDTH)
    cached_values = value_cache.reshape(local_rows, CACHE, KVH, HEAD_WIDTH)
    factor = HEAD_WIDTH ** (-0.5)
    scores = (
        jnp.einsum("rkgd,rckd->rkgc", heads_q, cached_keys, preferred_element_type=jnp.float32)
        * factor
    )
    own_score = (
        jnp.einsum("rkgd,rkd->rkg", heads_q, new_keys, preferred_element_type=jnp.float32) * factor
    )
    in_cache = (jnp.arange(CACHE, dtype=jnp.int32)[None, :] < lengths[:, None])[:, None, None, :]
    scores = jnp.where(in_cache, scores, -1e30)
    highest = jnp.maximum(jnp.max(scores, axis=-1), own_score)
    cached_exp = jnp.where(in_cache, jnp.exp(scores - highest[..., None]), 0.0)
    own_exp = jnp.exp(own_score - highest)
    softmax_sum = jnp.sum(cached_exp, axis=-1) + own_exp
    cached_weight = (cached_exp / softmax_sum[..., None]).astype(jnp.bfloat16)
    own_weight = (own_exp / softmax_sum).astype(jnp.bfloat16)
    mixture = jnp.einsum(
        "rkgc,rckd->rkgd", cached_weight, cached_values, preferred_element_type=jnp.float32
    )
    mixture = (
        mixture
        + own_weight.astype(jnp.float32)[..., None] * new_values.astype(jnp.float32)[:, :, None, :]
    )
    return mixture.reshape(local_rows, KVH * group_size * HEAD_WIDTH).astype(jnp.bfloat16)


def owner_shrunk(rows, down_factor, owner_mask):
    partial = jnp.einsum("we,bey->wby", rows, down_factor, preferred_element_type=jnp.float32)
    return jnp.sum(jnp.where(owner_mask[:, :, None], partial, 0.0), axis=1).astype(jnp.bfloat16)


def pool_size():
    return lax.axis_size("pool")


def exchange_quads(rows, step):
    count = pool_size()
    me = lax.axis_index("pool")
    parts = [rows] + [
        lax.ppermute(rows, "pool", [(i, i ^ (k * step)) for i in range(count)]) for k in (1, 2, 3)
    ]
    low = (me & step) != 0
    high = (me & (2 * step)) != 0
    swapped = [
        jnp.where(low, parts[1], parts[0]),
        jnp.where(low, parts[0], parts[1]),
        jnp.where(low, parts[3], parts[2]),
        jnp.where(low, parts[2], parts[3]),
    ]
    return jnp.concatenate(
        [
            jnp.where(high, swapped[2], swapped[0]),
            jnp.where(high, swapped[3], swapped[1]),
            jnp.where(high, swapped[0], swapped[2]),
            jnp.where(high, swapped[1], swapped[3]),
        ],
        axis=0,
    )


def exchange_pair(rows, step):
    count = pool_size()
    upper = (lax.axis_index("pool") & step) != 0
    other = lax.ppermute(rows, "pool", [(i, i ^ step) for i in range(count)])
    return jnp.concatenate([jnp.where(upper, other, rows), jnp.where(upper, rows, other)], axis=0)


def gather_rows(rows, beside=None):
    count = pool_size()
    step = 4
    held = None if beside is None else beside(rows)
    while step < count:
        if step * 4 <= count:
            rows = exchange_quads(rows, step)
            step *= 4
        else:
            rows = exchange_pair(rows, step)
            step *= 2
    if held is not None:
        rows, held = lax.optimization_barrier((rows, held))
    fours = [[4 * k + j for j in range(4)] for k in range(count // 4)]
    rows = lax.all_gather(rows, "pool", axis=0, axis_index_groups=fours, tiled=True)
    return rows if beside is None else (rows, held)


def core_halves(partial):
    count = pool_size()
    width = partial.shape[-1]
    blocks = partial.reshape(2, 2, count // 4, -1, width)
    odd = (lax.axis_index("pool") & 1) != 0
    keep = jnp.where(odd, blocks[:, 1], blocks[:, 0])
    give = jnp.where(odd, blocks[:, 0], blocks[:, 1])
    return (
        keep.transpose(1, 0, 2, 3).reshape(count // 2, -1, width),
        give.transpose(1, 0, 2, 3).reshape(count // 2, -1, width),
    )


def swap_cores(block):
    count = pool_size()
    return lax.ppermute(block, "pool", [(i, i ^ 1) for i in range(count)])


def exchange_chips(blocks):
    count = pool_size()
    same_core = [[2 * k + c for k in range(count // 2)] for c in range(2)]
    return lax.all_to_all(blocks, "pool", 0, 0, tiled=True, axis_index_groups=same_core)


def pair_columns(kept, received):
    odd = (lax.axis_index("pool") & 1) != 0
    return jnp.concatenate(
        [jnp.where(odd, received, kept), jnp.where(odd, kept, received)], axis=-1
    )


CHUNKS = 8
LANES = 128
KERNEL_VMEM = 24 * 1024 * 1024
QUERY_BRING_VMEM = 40 * 1024 * 1024
OUTPUT_VMEM = 44 * 1024 * 1024
NORM_VMEM = 8 * 1024 * 1024


def whole_block(shape):
    return pl.BlockSpec(shape, lambda: (0,) * len(shape))


def own_lift(rows_ref, down_ref, marks_ref, first_slot):
    ranks = down_ref.shape[0]
    width = down_ref.shape[1]
    step = width // CHUNKS
    total = None
    for k in range(CHUNKS):
        part = lax.dot_general(
            rows_ref[:, k * step : (k + 1) * step],
            down_ref[:, k * step : (k + 1) * step],
            (((1,), (1,)), ((), ())),
            preferred_element_type=jnp.float32,
        )
        total = part if total is None else total + part
    marks = marks_ref[...].astype(jnp.float32)
    slots = (marks[:, 0:1] * 32.0 + marks[:, 1:2]).astype(jnp.int32)
    place = lax.broadcasted_iota(jnp.int32, total.shape, 1) // ADAPTER_RANK + first_slot
    return jnp.where(slots == place, total, 0.0).astype(jnp.bfloat16)


def split_store(values, odd, kept_ref, given_ref, first, add):
    width = values.shape[1]
    size = values.shape[0] // 4
    local = kept_ref.shape[1]
    spot = pl.ds(first, width)
    for y in range(2):
        even_rows = values[2 * y * size : (2 * y + 1) * size]
        odd_rows = values[(2 * y + 1) * size : (2 * y + 2) * size]
        kept = jnp.where(odd, odd_rows, even_rows)
        given = jnp.where(odd, even_rows, odd_rows)
        for z in range(size // local):
            k = 2 * z + y
            kept_piece = kept[z * local : (z + 1) * local]
            given_piece = given[z * local : (z + 1) * local]
            if add:
                kept_piece = kept_piece + kept_ref[k, :, spot]
                given_piece = given_piece + given_ref[k, :, spot]
            kept_ref[k, :, spot] = kept_piece
            given_ref[k, :, spot] = given_piece


def query_kernel(
    where_ref, rows_ref, marks_ref, query_vmem, keyval_vmem, down_vmem, up_vmem,
    kept_ref, given_ref,
):
    me = where_ref[0]
    odd = (me % 2) == 1
    width = down_vmem.shape[1]
    step = width // CHUNKS
    lifted = own_lift(rows_ref, down_vmem, marks_ref, where_ref[1])
    for k in range(CHUNKS):
        spot = slice(k * step, (k + 1) * step)
        delta = adapter_scale * jnp.dot(
            lifted, up_vmem[:, spot], preferred_element_type=jnp.float32
        )
        split_store(delta, odd, kept_ref, given_ref, k * step, False)
    query = None
    for k in range(CHUNKS):
        spot = slice(k * step, (k + 1) * step)
        part = jnp.dot(rows_ref[:, spot], query_vmem[spot], preferred_element_type=jnp.float32)
        query = part if query is None else query + part
    columns = query.shape[1]
    split_store(
        query, odd, kept_ref, given_ref, pl.multiple_of(me * columns, LANES), True
    )
    keyval = None
    for k in range(CHUNKS):
        spot = slice(k * step, (k + 1) * step)
        part = jnp.dot(rows_ref[:, spot], keyval_vmem[spot], preferred_element_type=jnp.float32)
        keyval = part if keyval is None else keyval + part
    none = jnp.zeros_like(keyval)
    both = jnp.concatenate([jnp.where(odd, none, keyval), jnp.where(odd, keyval, none)], axis=1)
    split_store(both, odd, kept_ref, given_ref, width, False)


def query_halves(where, gathered, query_weight, key_value_weight, down, up, count, local_rows):
    rows = gathered.shape[0]
    width, columns = query_weight.shape
    keyval_columns = key_value_weight.shape[1]
    ranks = down.shape[0]
    sent = jax.ShapeDtypeStruct(
        (count // 2, local_rows, width + 2 * keyval_columns), jnp.float32
    )
    return pl.pallas_call(
        query_kernel,
        in_specs=[
            pl.BlockSpec(memory_space=pltpu.SMEM),
            whole_block((rows, width)),
            whole_block((rows, LANES)),
        ]
        + [pl.BlockSpec(memory_space=pltpu.VMEM)] * 4,
        out_specs=[whole_block(sent.shape)] * 2,
        out_shape=[sent, sent],
        compiler_params=pltpu.CompilerParams(vmem_limit_bytes=KERNEL_VMEM),
        name="query_halves",
    )(where, gathered[:, :width], gathered[:, width:], query_weight, key_value_weight, down, up)


def output_kernel(
    where_ref, rows_ref, marks_ref, near_vmem, output_hbm, down_vmem, up_vmem,
    kept_ref, given_ref, late_vmem, sems,
):
    me = where_ref[0]
    odd = (me % 2) == 1
    depth, width = output_hbm.shape
    near = near_vmem.shape[1]
    step = width // CHUNKS
    late = [
        pltpu.make_async_copy(
            output_hbm.at[:, pl.ds(k * step, step)],
            late_vmem.at[:, pl.ds(k * step - near, step)],
            sems.at[k - near // step],
        )
        for k in range(near // step, CHUNKS)
    ]
    for copy in late:
        copy.start()
    lifted = own_lift(rows_ref, down_vmem, marks_ref, where_ref[1])
    columns = rows_ref[:, pl.ds(pl.multiple_of(me * depth, LANES), depth)]
    for k in range(CHUNKS):
        spot = slice(k * step, (k + 1) * step)
        if k * step < near:
            weight = near_vmem[:, spot]
        else:
            late[k - near // step].wait()
            weight = late_vmem[:, k * step - near : (k + 1) * step - near]
        part = jnp.dot(columns, weight, preferred_element_type=jnp.float32)
        part = part + adapter_scale * jnp.dot(
            lifted, up_vmem[:, spot], preferred_element_type=jnp.float32
        )
        split_store(part, odd, kept_ref, given_ref, k * step, False)


def output_halves(
    where, every_row, gathered, output_near, output_weight, down, up, count, local_rows
):
    rows = every_row.shape[0]
    depth, width = output_weight.shape
    ranks = down.shape[0]
    sent = jax.ShapeDtypeStruct((count // 2, local_rows, width), jnp.float32)
    return pl.pallas_call(
        output_kernel,
        in_specs=[
            pl.BlockSpec(memory_space=pltpu.SMEM),
            whole_block((rows, width)),
            whole_block((rows, LANES)),
        ]
        + [
            pl.BlockSpec(memory_space=pltpu.VMEM),
            pl.BlockSpec(memory_space=pl.ANY),
            pl.BlockSpec(memory_space=pltpu.VMEM),
            pl.BlockSpec(memory_space=pltpu.VMEM),
        ],
        out_specs=[whole_block(sent.shape)] * 2,
        out_shape=[sent, sent],
        scratch_shapes=[
            pltpu.VMEM((depth, width - output_near.shape[1]), jnp.bfloat16),
            pltpu.SemaphoreType.DMA((CHUNKS,)),
        ],
        compiler_params=pltpu.CompilerParams(vmem_limit_bytes=OUTPUT_VMEM),
        name="output_halves",
    )(where, every_row, gathered[:, width:], output_near, output_weight, down, up)


def bring_kernel(where_ref, source, target, sems):
    step = source.shape[0] // 4
    copies = []
    for k in range(4):
        spot = pl.ds(k * step, step)
        copies.append(
            pltpu.make_async_copy(
                source.at[spot, pl.ds(0, target.shape[1])], target.at[spot], sems.at[k]
            )
        )
    for copy in copies:
        copy.start()
    for copy in copies:
        copy.wait()


def bring(where, weight, columns, vmem):
    rows = weight.shape[0]
    return pl.pallas_call(
        bring_kernel,
        in_specs=[
            pl.BlockSpec(memory_space=pltpu.SMEM),
            pl.BlockSpec(memory_space=pl.ANY),
        ],
        out_specs=pl.BlockSpec(memory_space=pltpu.VMEM),
        out_shape=jax.ShapeDtypeStruct((rows, columns), weight.dtype),
        scratch_shapes=[pltpu.SemaphoreType.DMA((4,))],
        compiler_params=pltpu.CompilerParams(vmem_limit_bytes=vmem),
        cost_estimate=pl.CostEstimate(
            flops=0, bytes_accessed=4 * rows * columns, transcendentals=0
        ),
        name="bring",
    )(where, weight)


def norm_kernel(hidden_ref, gain_ref, adapter_ref, slot_ref, sent_ref):
    rows, width = hidden_ref.shape
    values = hidden_ref[...].astype(jnp.float32)
    factor = lax.rsqrt(jnp.mean(values * values, axis=-1, keepdims=True) + norm_eps)
    sent_ref[:, :width] = (values * factor * gain_ref[...]).astype(jnp.bfloat16)
    row = lax.broadcasted_iota(jnp.int32, (rows, LANES), 0)
    lane = lax.broadcasted_iota(jnp.int32, (rows, LANES), 1)
    marks = jnp.zeros((rows, LANES), jnp.int32)
    for r in range(rows):
        slot = slot_ref[adapter_ref[r]]
        digit = jnp.where(lane == 0, slot // 32, jnp.where(lane == 1, slot % 32, 0))
        marks = jnp.where(row == r, digit, marks)
    sent_ref[:, width:] = marks.astype(jnp.float32).astype(jnp.bfloat16)


def norm_and_marks(hidden, gain, request_adapter, adapter_slot):
    rows, width = hidden.shape
    return pl.pallas_call(
        norm_kernel,
        in_specs=[
            whole_block(hidden.shape),
            whole_block((1, width)),
            pl.BlockSpec(memory_space=pltpu.SMEM),
            pl.BlockSpec(memory_space=pltpu.SMEM),
        ],
        out_specs=whole_block((rows, width + LANES)),
        out_shape=jax.ShapeDtypeStruct((rows, width + LANES), jnp.bfloat16),
        compiler_params=pltpu.CompilerParams(vmem_limit_bytes=NORM_VMEM),
        name="norm_and_marks",
    )(hidden, gain.reshape(1, width), request_adapter, adapter_slot)


def by_rank(factor):
    return factor.transpose(0, 2, 1).reshape(-1, factor.shape[1])


def body(
    hidden,
    gain,
    query_weight,
    key_value_weight,
    output_weight,
    query_down_factor,
    query_up_factor,
    output_down_factor,
    output_up_factor,
    key_cache,
    value_cache,
    lengths,
    request_adapter,
    adapter_slot,
):
    count = pool_size()
    own_slots = query_down_factor.shape[0]
    local_rows = hidden.shape[0]
    col_width = query_weight.shape[1]

    aligned = col_width % LANES == 0 and key_value_weight.shape[1] % LANES == 0
    if aligned:
        sent = norm_and_marks(hidden, gain, request_adapter, adapter_slot)
    else:
        normalized_input = norm_rows(hidden, gain)
        slot_ids = lookup_slots(request_adapter, adapter_slot)
        digits = jnp.stack([slot_ids // 32, slot_ids % 32], axis=1).astype(jnp.bfloat16)
        sent = jnp.concatenate([normalized_input, jnp.pad(digits, ((0, 0), (0, 126)))], axis=1)
    first_slot = lax.axis_index("pool") * own_slots
    where = jnp.stack([lax.axis_index("pool"), first_slot]).astype(jnp.int32)
    if aligned:

        def bring_query(rows):
            now, _ = lax.optimization_barrier((where, rows))
            return bring(now, query_weight, col_width, QUERY_BRING_VMEM)

        gathered, query_near = gather_rows(sent, bring_query)
    else:
        gathered = gather_rows(sent)
    gathered_rows = gathered[:, :MODEL_WIDTH]
    all_digits = gathered[:, MODEL_WIDTH : MODEL_WIDTH + 2].astype(jnp.int32)
    slot_ids = all_digits[:, 0] * 32 + all_digits[:, 1]
    request_total = gathered_rows.shape[0]

    owner_mask = (
        slot_ids[:, None] == first_slot + jnp.arange(own_slots, dtype=jnp.int32)[None, :]
    )
    bf_zero = jnp.zeros((), jnp.bfloat16)

    query_width = MODEL_WIDTH
    if aligned:
        kept, given = query_halves(
            where,
            gathered,
            query_near,
            key_value_weight,
            by_rank(query_down_factor),
            query_up_factor.reshape(own_slots * ADAPTER_RANK, -1),
            count,
            local_rows,
        )
        leaving = kept + swap_cores(given)
    else:
        query_shrunk = owner_shrunk(gathered_rows, query_down_factor, owner_mask)
        lifted_rows = jnp.where(owner_mask[:, :, None], query_shrunk[:, None, :], bf_zero).reshape(
            request_total, own_slots * ADAPTER_RANK
        )
        query_delta = adapter_scale * jnp.dot(
            lifted_rows,
            query_up_factor.reshape(own_slots * ADAPTER_RANK, -1),
            preferred_element_type=jnp.float32,
        )
        kept_delta, given_delta = core_halves(query_delta)
        received_delta = swap_cores(given_delta)
        base = jnp.concatenate(
            [
                jnp.dot(gathered_rows, query_weight, preferred_element_type=jnp.float32),
                jnp.dot(gathered_rows, key_value_weight, preferred_element_type=jnp.float32),
            ],
            axis=1,
        )
        kept_base, given_base = core_halves(base)
        received_base = swap_cores(given_base)
        pair_query = pair_columns(kept_base[:, :, :col_width], received_base[:, :, :col_width])
        pair_keyval = pair_columns(kept_base[:, :, col_width:], received_base[:, :, col_width:])
        pair_delta = kept_delta + received_delta
        first_column = (lax.axis_index("pool") // 2) * (2 * col_width)
        there = lax.dynamic_slice_in_dim(pair_delta, first_column, 2 * col_width, 2)
        pair_delta = lax.dynamic_update_slice_in_dim(pair_delta, there + pair_query, first_column, 2)
        leaving = jnp.concatenate([pair_delta, pair_keyval], axis=2)
    arrived = exchange_chips(leaving)
    arrived, lengths = lax.optimization_barrier((arrived, lengths))
    query_rows = jnp.sum(arrived[:, :, :query_width], axis=0).astype(jnp.bfloat16)
    keyval_rows = arrived[:, :, query_width:].astype(jnp.bfloat16)
    keyval_rows = keyval_rows.reshape(count // 2, local_rows, 2, -1)
    keyval_rows = keyval_rows.transpose(1, 0, 2, 3).reshape(local_rows, -1)

    attention_output = attend(query_rows, keyval_rows, key_cache, value_cache, lengths)
    if aligned:

        def bring_output(rows):
            now, _ = lax.optimization_barrier((where, rows))
            return bring(now, output_weight, output_weight.shape[1] // 2, OUTPUT_VMEM)

        every_row, output_near = gather_rows(attention_output, bring_output)
    else:
        every_row = gather_rows(attention_output)
    if aligned:
        kept, given = output_halves(
            where,
            every_row,
            gathered,
            output_near,
            output_weight,
            by_rank(output_down_factor),
            output_up_factor.reshape(own_slots * ADAPTER_RANK, -1),
            count,
            local_rows,
        )
    else:
        out_width = output_weight.shape[0]
        columns = lax.dynamic_slice_in_dim(every_row, lax.axis_index("pool") * out_width, out_width, 1)
        output_shrunk = owner_shrunk(every_row, output_down_factor, owner_mask)
        lifted_rows = jnp.where(owner_mask[:, :, None], output_shrunk[:, None, :], bf_zero).reshape(
            request_total, own_slots * ADAPTER_RANK
        )
        up_rows = output_up_factor.reshape(own_slots * ADAPTER_RANK, MODEL_WIDTH)
        partial = jnp.dot(
            columns, output_weight, preferred_element_type=jnp.float32
        ) + adapter_scale * jnp.dot(lifted_rows, up_rows, preferred_element_type=jnp.float32)
        kept, given = core_halves(partial)
    arrived = exchange_chips(kept + swap_cores(given))
    return jnp.sum(arrived, axis=0).astype(jnp.bfloat16)


def solution(mesh):
    placed = (
        P(("groups", "pool"), None),
        P(),
        P(None, "pool"),
        P(None, "pool"),
        P("pool", None),
        P(("groups", "pool"), None, None),
        P(("groups", "pool"), None, None),
        P(("groups", "pool"), None, None),
        P(("groups", "pool"), None, None),
        P(("groups", "pool"), None, None),
        P(("groups", "pool"), None, None),
        P(("groups", "pool")),
        P(("groups", "pool")),
        P("groups"),
    )
    return jax.shard_map(
        body, mesh=mesh, in_specs=placed, out_specs=P(("groups", "pool"), None), check_vma=False
    )
```

```python
import jax
import jax.numpy as jnp
from jax import lax
from jax.experimental import pallas as pl
from jax.experimental.pallas import tpu as pltpu
from jax.sharding import PartitionSpec as P

MODEL_WIDTH = 8192
H = 64
KVH = 8
HEAD_WIDTH = 128
ADAPTER_RANK = 16
CACHE = 512
DKV = 1024


adapter_scale = 0.5
norm_eps = 1e-05


def norm_rows(hidden, gain):
    values = hidden.astype(jnp.float32)
    factor = lax.rsqrt(jnp.mean(values * values, axis=-1, keepdims=True) + norm_eps)
    return (values * factor * gain).astype(jnp.bfloat16)


def lookup_slots(all_ids, adapter_slot):
    table_size = adapter_slot.shape[0]
    matches = all_ids[:, None] == jnp.arange(table_size, dtype=jnp.int32)[None, :]
    return jnp.sum(jnp.where(matches, adapter_slot[None, :], 0), axis=1)


def attend(query_rows, keyval_rows, key_cache, value_cache, lengths):
    group_size = H // KVH
    local_rows = query_rows.shape[0]
    heads_q = query_rows.reshape(local_rows, KVH, group_size, HEAD_WIDTH)
    new_keys = keyval_rows[:, :DKV].reshape(local_rows, KVH, HEAD_WIDTH)
    new_values = keyval_rows[:, DKV:].reshape(local_rows, KVH, HEAD_WIDTH)
    cached_keys = key_cache.reshape(local_rows, CACHE, KVH, HEAD_WIDTH)
    cached_values = value_cache.reshape(local_rows, CACHE, KVH, HEAD_WIDTH)
    factor = HEAD_WIDTH ** (-0.5)
    scores = (
        jnp.einsum("rkgd,rckd->rkgc", heads_q, cached_keys, preferred_element_type=jnp.float32)
        * factor
    )
    own_score = (
        jnp.einsum("rkgd,rkd->rkg", heads_q, new_keys, preferred_element_type=jnp.float32) * factor
    )
    in_cache = (jnp.arange(CACHE, dtype=jnp.int32)[None, :] < lengths[:, None])[:, None, None, :]
    scores = jnp.where(in_cache, scores, -1e30)
    highest = jnp.maximum(jnp.max(scores, axis=-1), own_score)
    cached_exp = jnp.where(in_cache, jnp.exp(scores - highest[..., None]), 0.0)
    own_exp = jnp.exp(own_score - highest)
    softmax_sum = jnp.sum(cached_exp, axis=-1) + own_exp
    cached_weight = (cached_exp / softmax_sum[..., None]).astype(jnp.bfloat16)
    own_weight = (own_exp / softmax_sum).astype(jnp.bfloat16)
    mixture = jnp.einsum(
        "rkgc,rckd->rkgd", cached_weight, cached_values, preferred_element_type=jnp.float32
    )
    mixture = (
        mixture
        + own_weight.astype(jnp.float32)[..., None] * new_values.astype(jnp.float32)[:, :, None, :]
    )
    return mixture.reshape(local_rows, KVH * group_size * HEAD_WIDTH).astype(jnp.bfloat16)


def owner_shrunk(rows, down_factor, owner_mask):
    partial = jnp.einsum("we,bey->wby", rows, down_factor, preferred_element_type=jnp.float32)
    return jnp.sum(jnp.where(owner_mask[:, :, None], partial, 0.0), axis=1).astype(jnp.bfloat16)


def pool_size():
    return lax.axis_size("pool")


def exchange_quads(rows, step):
    count = pool_size()
    me = lax.axis_index("pool")
    parts = [rows] + [
        lax.ppermute(rows, "pool", [(i, i ^ (k * step)) for i in range(count)]) for k in (1, 2, 3)
    ]
    low = (me & step) != 0
    high = (me & (2 * step)) != 0
    swapped = [
        jnp.where(low, parts[1], parts[0]),
        jnp.where(low, parts[0], parts[1]),
        jnp.where(low, parts[3], parts[2]),
        jnp.where(low, parts[2], parts[3]),
    ]
    return jnp.concatenate(
        [
            jnp.where(high, swapped[2], swapped[0]),
            jnp.where(high, swapped[3], swapped[1]),
            jnp.where(high, swapped[0], swapped[2]),
            jnp.where(high, swapped[1], swapped[3]),
        ],
        axis=0,
    )


def exchange_pair(rows, step):
    count = pool_size()
    upper = (lax.axis_index("pool") & step) != 0
    other = lax.ppermute(rows, "pool", [(i, i ^ step) for i in range(count)])
    return jnp.concatenate([jnp.where(upper, other, rows), jnp.where(upper, rows, other)], axis=0)


def gather_rows(rows, beside=None):
    count = pool_size()
    step = 4
    held = None if beside is None else beside(rows)
    while step < count:
        if step * 4 <= count:
            rows = exchange_quads(rows, step)
            step *= 4
        else:
            rows = exchange_pair(rows, step)
            step *= 2
    if held is not None:
        rows, held = lax.optimization_barrier((rows, held))
    fours = [[4 * k + j for j in range(4)] for k in range(count // 4)]
    rows = lax.all_gather(rows, "pool", axis=0, axis_index_groups=fours, tiled=True)
    return rows if beside is None else (rows, held)


def core_halves(partial):
    count = pool_size()
    width = partial.shape[-1]
    blocks = partial.reshape(2, 2, count // 4, -1, width)
    odd = (lax.axis_index("pool") & 1) != 0
    keep = jnp.where(odd, blocks[:, 1], blocks[:, 0])
    give = jnp.where(odd, blocks[:, 0], blocks[:, 1])
    return (
        keep.transpose(1, 0, 2, 3).reshape(count // 2, -1, width),
        give.transpose(1, 0, 2, 3).reshape(count // 2, -1, width),
    )


def swap_cores(block):
    count = pool_size()
    return lax.ppermute(block, "pool", [(i, i ^ 1) for i in range(count)])


def exchange_chips(blocks):
    count = pool_size()
    same_core = [[2 * k + c for k in range(count // 2)] for c in range(2)]
    return lax.all_to_all(blocks, "pool", 0, 0, tiled=True, axis_index_groups=same_core)


def pair_columns(kept, received):
    odd = (lax.axis_index("pool") & 1) != 0
    return jnp.concatenate(
        [jnp.where(odd, received, kept), jnp.where(odd, kept, received)], axis=-1
    )


CHUNKS = 8
LANES = 128
KERNEL_VMEM = 24 * 1024 * 1024
BRING_VMEM = 40 * 1024 * 1024


def whole_block(shape):
    return pl.BlockSpec(shape, lambda: (0,) * len(shape))


def own_lift(rows_ref, down_ref, marks_ref, first_slot):
    ranks = down_ref.shape[0]
    width = down_ref.shape[1]
    step = width // CHUNKS
    total = None
    for k in range(CHUNKS):
        part = lax.dot_general(
            rows_ref[:, k * step : (k + 1) * step],
            down_ref[:, k * step : (k + 1) * step],
            (((1,), (1,)), ((), ())),
            preferred_element_type=jnp.float32,
        )
        total = part if total is None else total + part
    marks = marks_ref[...].astype(jnp.float32)
    slots = (marks[:, 0:1] * 32.0 + marks[:, 1:2]).astype(jnp.int32)
    place = lax.broadcasted_iota(jnp.int32, total.shape, 1) // ADAPTER_RANK + first_slot
    return jnp.where(slots == place, total, 0.0).astype(jnp.bfloat16)


def split_store(values, odd, kept_ref, given_ref, first, add):
    width = values.shape[1]
    size = values.shape[0] // 4
    local = kept_ref.shape[1]
    spot = pl.ds(first, width)
    for y in range(2):
        even_rows = values[2 * y * size : (2 * y + 1) * size]
        odd_rows = values[(2 * y + 1) * size : (2 * y + 2) * size]
        kept = jnp.where(odd, odd_rows, even_rows)
        given = jnp.where(odd, even_rows, odd_rows)
        for z in range(size // local):
            k = 2 * z + y
            kept_piece = kept[z * local : (z + 1) * local]
            given_piece = given[z * local : (z + 1) * local]
            if add:
                kept_piece = kept_piece + kept_ref[k, :, spot]
                given_piece = given_piece + given_ref[k, :, spot]
            kept_ref[k, :, spot] = kept_piece
            given_ref[k, :, spot] = given_piece


def query_kernel(
    where_ref, rows_ref, marks_ref, query_vmem, keyval_vmem, down_vmem, up_vmem,
    kept_ref, given_ref,
):
    me = where_ref[0]
    odd = (me % 2) == 1
    width = down_vmem.shape[1]
    step = width // CHUNKS
    lifted = own_lift(rows_ref, down_vmem, marks_ref, where_ref[1])
    for k in range(CHUNKS):
        spot = slice(k * step, (k + 1) * step)
        delta = adapter_scale * jnp.dot(
            lifted, up_vmem[:, spot], preferred_element_type=jnp.float32
        )
        split_store(delta, odd, kept_ref, given_ref, k * step, False)
    query = None
    for k in range(CHUNKS):
        spot = slice(k * step, (k + 1) * step)
        part = jnp.dot(rows_ref[:, spot], query_vmem[spot], preferred_element_type=jnp.float32)
        query = part if query is None else query + part
    columns = query.shape[1]
    split_store(
        query, odd, kept_ref, given_ref, pl.multiple_of(me * columns, LANES), True
    )
    keyval = None
    for k in range(CHUNKS):
        spot = slice(k * step, (k + 1) * step)
        part = jnp.dot(rows_ref[:, spot], keyval_vmem[spot], preferred_element_type=jnp.float32)
        keyval = part if keyval is None else keyval + part
    none = jnp.zeros_like(keyval)
    both = jnp.concatenate([jnp.where(odd, none, keyval), jnp.where(odd, keyval, none)], axis=1)
    split_store(both, odd, kept_ref, given_ref, width, False)


def query_halves(where, gathered, query_weight, key_value_weight, down, up, count, local_rows):
    rows = gathered.shape[0]
    width, columns = query_weight.shape
    keyval_columns = key_value_weight.shape[1]
    ranks = down.shape[0]
    sent = jax.ShapeDtypeStruct(
        (count // 2, local_rows, width + 2 * keyval_columns), jnp.float32
    )
    return pl.pallas_call(
        query_kernel,
        in_specs=[
            pl.BlockSpec(memory_space=pltpu.SMEM),
            whole_block((rows, width)),
            whole_block((rows, LANES)),
        ]
        + [pl.BlockSpec(memory_space=pltpu.VMEM)] * 4,
        out_specs=[whole_block(sent.shape)] * 2,
        out_shape=[sent, sent],
        compiler_params=pltpu.CompilerParams(vmem_limit_bytes=KERNEL_VMEM),
        name="query_halves",
    )(where, gathered[:, :width], gathered[:, width:], query_weight, key_value_weight, down, up)


def output_kernel(
    where_ref, rows_ref, marks_ref, output_vmem, down_vmem, up_vmem, kept_ref, given_ref
):
    me = where_ref[0]
    odd = (me % 2) == 1
    depth, width = output_vmem.shape
    step = width // CHUNKS
    lifted = own_lift(rows_ref, down_vmem, marks_ref, where_ref[1])
    columns = rows_ref[:, pl.ds(pl.multiple_of(me * depth, LANES), depth)]
    for k in range(CHUNKS):
        spot = slice(k * step, (k + 1) * step)
        part = jnp.dot(columns, output_vmem[:, spot], preferred_element_type=jnp.float32)
        part = part + adapter_scale * jnp.dot(
            lifted, up_vmem[:, spot], preferred_element_type=jnp.float32
        )
        split_store(part, odd, kept_ref, given_ref, k * step, False)


def output_halves(where, every_row, gathered, output_weight, down, up, count, local_rows):
    rows = every_row.shape[0]
    depth, width = output_weight.shape
    ranks = down.shape[0]
    sent = jax.ShapeDtypeStruct((count // 2, local_rows, width), jnp.float32)
    return pl.pallas_call(
        output_kernel,
        in_specs=[
            pl.BlockSpec(memory_space=pltpu.SMEM),
            whole_block((rows, width)),
            whole_block((rows, LANES)),
        ]
        + [pl.BlockSpec(memory_space=pltpu.VMEM)] * 3,
        out_specs=[whole_block(sent.shape)] * 2,
        out_shape=[sent, sent],
        compiler_params=pltpu.CompilerParams(vmem_limit_bytes=KERNEL_VMEM),
        name="output_halves",
    )(where, every_row, gathered[:, width:], output_weight, down, up)


def bring_kernel(*refs):
    count = (len(refs) - 2) // 2
    sources, targets, sems = refs[1 : count + 1], refs[count + 1 : -1], refs[-1]
    copies = []
    for source, target in zip(sources, targets):
        step = source.shape[0] // 4
        for k in range(4):
            spot = pl.ds(k * step, step)
            copies.append(
                pltpu.make_async_copy(source.at[spot], target.at[spot], sems.at[len(copies)])
            )
    for copy in copies:
        copy.start()
    for copy in copies:
        copy.wait()


def bring(where, arrays):
    size = sum(2 * array.size for array in arrays)
    return pl.pallas_call(
        bring_kernel,
        in_specs=[pl.BlockSpec(memory_space=pltpu.SMEM)]
        + [pl.BlockSpec(memory_space=pl.ANY)] * len(arrays),
        out_specs=[pl.BlockSpec(memory_space=pltpu.VMEM)] * len(arrays),
        out_shape=[jax.ShapeDtypeStruct(array.shape, array.dtype) for array in arrays],
        scratch_shapes=[pltpu.SemaphoreType.DMA((4 * len(arrays),))],
        compiler_params=pltpu.CompilerParams(vmem_limit_bytes=BRING_VMEM),
        cost_estimate=pl.CostEstimate(flops=0, bytes_accessed=2 * size, transcendentals=0),
        name="bring",
    )(where, *arrays)


def by_rank(factor):
    return factor.transpose(0, 2, 1).reshape(-1, factor.shape[1])


def body(
    hidden,
    gain,
    query_weight,
    key_value_weight,
    output_weight,
    query_down_factor,
    query_up_factor,
    output_down_factor,
    output_up_factor,
    key_cache,
    value_cache,
    lengths,
    request_adapter,
    adapter_slot,
):
    count = pool_size()
    own_slots = query_down_factor.shape[0]
    local_rows = hidden.shape[0]
    col_width = query_weight.shape[1]

    normalized_input = norm_rows(hidden, gain)
    slot_ids = lookup_slots(request_adapter, adapter_slot)
    digits = jnp.stack([slot_ids // 32, slot_ids % 32], axis=1).astype(jnp.bfloat16)
    sent = jnp.concatenate([normalized_input, jnp.pad(digits, ((0, 0), (0, 126)))], axis=1)
    first_slot = lax.axis_index("pool") * own_slots
    where = jnp.stack([lax.axis_index("pool"), first_slot]).astype(jnp.int32)
    aligned = col_width % LANES == 0 and key_value_weight.shape[1] % LANES == 0
    if aligned:

        def bring_query(rows):
            now, _ = lax.optimization_barrier((where, rows))
            return bring(
                now,
                [query_weight],
            )

        gathered, (query_near,) = gather_rows(sent, bring_query)
    else:
        gathered = gather_rows(sent)
    gathered_rows = gathered[:, :MODEL_WIDTH]
    all_digits = gathered[:, MODEL_WIDTH : MODEL_WIDTH + 2].astype(jnp.int32)
    slot_ids = all_digits[:, 0] * 32 + all_digits[:, 1]
    request_total = gathered_rows.shape[0]

    owner_mask = (
        slot_ids[:, None] == first_slot + jnp.arange(own_slots, dtype=jnp.int32)[None, :]
    )
    bf_zero = jnp.zeros((), jnp.bfloat16)

    query_width = MODEL_WIDTH
    if aligned:
        kept, given = query_halves(
            where,
            gathered,
            query_near,
            key_value_weight,
            by_rank(query_down_factor),
            query_up_factor.reshape(own_slots * ADAPTER_RANK, -1),
            count,
            local_rows,
        )
        leaving = kept + swap_cores(given)
    else:
        query_shrunk = owner_shrunk(gathered_rows, query_down_factor, owner_mask)
        lifted_rows = jnp.where(owner_mask[:, :, None], query_shrunk[:, None, :], bf_zero).reshape(
            request_total, own_slots * ADAPTER_RANK
        )
        query_delta = adapter_scale * jnp.dot(
            lifted_rows,
            query_up_factor.reshape(own_slots * ADAPTER_RANK, -1),
            preferred_element_type=jnp.float32,
        )
        kept_delta, given_delta = core_halves(query_delta)
        received_delta = swap_cores(given_delta)
        base = jnp.concatenate(
            [
                jnp.dot(gathered_rows, query_weight, preferred_element_type=jnp.float32),
                jnp.dot(gathered_rows, key_value_weight, preferred_element_type=jnp.float32),
            ],
            axis=1,
        )
        kept_base, given_base = core_halves(base)
        received_base = swap_cores(given_base)
        pair_query = pair_columns(kept_base[:, :, :col_width], received_base[:, :, :col_width])
        pair_keyval = pair_columns(kept_base[:, :, col_width:], received_base[:, :, col_width:])
        pair_delta = kept_delta + received_delta
        first_column = (lax.axis_index("pool") // 2) * (2 * col_width)
        there = lax.dynamic_slice_in_dim(pair_delta, first_column, 2 * col_width, 2)
        pair_delta = lax.dynamic_update_slice_in_dim(pair_delta, there + pair_query, first_column, 2)
        leaving = jnp.concatenate([pair_delta, pair_keyval], axis=2)
    arrived = exchange_chips(leaving)
    arrived, lengths = lax.optimization_barrier((arrived, lengths))
    query_rows = jnp.sum(arrived[:, :, :query_width], axis=0).astype(jnp.bfloat16)
    keyval_rows = arrived[:, :, query_width:].astype(jnp.bfloat16)
    keyval_rows = keyval_rows.reshape(count // 2, local_rows, 2, -1)
    keyval_rows = keyval_rows.transpose(1, 0, 2, 3).reshape(local_rows, -1)

    attention_output = attend(query_rows, keyval_rows, key_cache, value_cache, lengths)
    if aligned:

        def bring_output(rows):
            now, _ = lax.optimization_barrier((where, rows))
            return bring(now, [output_weight])

        every_row, (output_near,) = gather_rows(attention_output, bring_output)
    else:
        every_row = gather_rows(attention_output)
    if aligned:
        kept, given = output_halves(
            where,
            every_row,
            gathered,
            output_near,
            by_rank(output_down_factor),
            output_up_factor.reshape(own_slots * ADAPTER_RANK, -1),
            count,
            local_rows,
        )
    else:
        out_width = output_weight.shape[0]
        columns = lax.dynamic_slice_in_dim(every_row, lax.axis_index("pool") * out_width, out_width, 1)
        output_shrunk = owner_shrunk(every_row, output_down_factor, owner_mask)
        lifted_rows = jnp.where(owner_mask[:, :, None], output_shrunk[:, None, :], bf_zero).reshape(
            request_total, own_slots * ADAPTER_RANK
        )
        up_rows = output_up_factor.reshape(own_slots * ADAPTER_RANK, MODEL_WIDTH)
        partial = jnp.dot(
            columns, output_weight, preferred_element_type=jnp.float32
        ) + adapter_scale * jnp.dot(lifted_rows, up_rows, preferred_element_type=jnp.float32)
        kept, given = core_halves(partial)
    arrived = exchange_chips(kept + swap_cores(given))
    return jnp.sum(arrived, axis=0).astype(jnp.bfloat16)


def solution(mesh):
    placed = (
        P(("groups", "pool"), None),
        P(),
        P(None, "pool"),
        P(None, "pool"),
        P("pool", None),
        P(("groups", "pool"), None, None),
        P(("groups", "pool"), None, None),
        P(("groups", "pool"), None, None),
        P(("groups", "pool"), None, None),
        P(("groups", "pool"), None, None),
        P(("groups", "pool"), None, None),
        P(("groups", "pool")),
        P(("groups", "pool")),
        P("groups"),
    )
    return jax.shard_map(
        body, mesh=mesh, in_specs=placed, out_specs=P(("groups", "pool"), None), check_vma=False
    )
```

```python
import jax
import jax.numpy as jnp
from jax import lax
from jax.experimental import pallas as pl
from jax.experimental.pallas import tpu as pltpu
from jax.sharding import PartitionSpec as P

MODEL_WIDTH = 8192
H = 64
KVH = 8
HEAD_WIDTH = 128
ADAPTER_RANK = 16
CACHE = 512
DKV = 1024


adapter_scale = 0.5
norm_eps = 1e-05


def norm_rows(hidden, gain):
    values = hidden.astype(jnp.float32)
    factor = lax.rsqrt(jnp.mean(values * values, axis=-1, keepdims=True) + norm_eps)
    return (values * factor * gain).astype(jnp.bfloat16)


def lookup_slots(all_ids, adapter_slot):
    table_size = adapter_slot.shape[0]
    matches = all_ids[:, None] == jnp.arange(table_size, dtype=jnp.int32)[None, :]
    return jnp.sum(jnp.where(matches, adapter_slot[None, :], 0), axis=1)


def attend(query_rows, keyval_rows, key_cache, value_cache, lengths):
    group_size = H // KVH
    local_rows = query_rows.shape[0]
    heads_q = query_rows.reshape(local_rows, KVH, group_size, HEAD_WIDTH)
    new_keys = keyval_rows[:, :DKV].reshape(local_rows, KVH, HEAD_WIDTH)
    new_values = keyval_rows[:, DKV:].reshape(local_rows, KVH, HEAD_WIDTH)
    cached_keys = key_cache.reshape(local_rows, CACHE, KVH, HEAD_WIDTH)
    cached_values = value_cache.reshape(local_rows, CACHE, KVH, HEAD_WIDTH)
    factor = HEAD_WIDTH ** (-0.5)
    scores = (
        jnp.einsum("rkgd,rckd->rkgc", heads_q, cached_keys, preferred_element_type=jnp.float32)
        * factor
    )
    own_score = (
        jnp.einsum("rkgd,rkd->rkg", heads_q, new_keys, preferred_element_type=jnp.float32) * factor
    )
    in_cache = (jnp.arange(CACHE, dtype=jnp.int32)[None, :] < lengths[:, None])[:, None, None, :]
    scores = jnp.where(in_cache, scores, -1e30)
    highest = jnp.maximum(jnp.max(scores, axis=-1), own_score)
    cached_exp = jnp.where(in_cache, jnp.exp(scores - highest[..., None]), 0.0)
    own_exp = jnp.exp(own_score - highest)
    softmax_sum = jnp.sum(cached_exp, axis=-1) + own_exp
    cached_weight = (cached_exp / softmax_sum[..., None]).astype(jnp.bfloat16)
    own_weight = (own_exp / softmax_sum).astype(jnp.bfloat16)
    mixture = jnp.einsum(
        "rkgc,rckd->rkgd", cached_weight, cached_values, preferred_element_type=jnp.float32
    )
    mixture = (
        mixture
        + own_weight.astype(jnp.float32)[..., None] * new_values.astype(jnp.float32)[:, :, None, :]
    )
    return mixture.reshape(local_rows, KVH * group_size * HEAD_WIDTH).astype(jnp.bfloat16)


def owner_shrunk(rows, down_factor, owner_mask):
    partial = jnp.einsum("we,bey->wby", rows, down_factor, preferred_element_type=jnp.float32)
    return jnp.sum(jnp.where(owner_mask[:, :, None], partial, 0.0), axis=1).astype(jnp.bfloat16)


def pool_size():
    return lax.axis_size("pool")


def exchange_quads(rows, step):
    count = pool_size()
    me = lax.axis_index("pool")
    parts = [rows] + [
        lax.ppermute(rows, "pool", [(i, i ^ (k * step)) for i in range(count)]) for k in (1, 2, 3)
    ]
    low = (me & step) != 0
    high = (me & (2 * step)) != 0
    swapped = [
        jnp.where(low, parts[1], parts[0]),
        jnp.where(low, parts[0], parts[1]),
        jnp.where(low, parts[3], parts[2]),
        jnp.where(low, parts[2], parts[3]),
    ]
    return jnp.concatenate(
        [
            jnp.where(high, swapped[2], swapped[0]),
            jnp.where(high, swapped[3], swapped[1]),
            jnp.where(high, swapped[0], swapped[2]),
            jnp.where(high, swapped[1], swapped[3]),
        ],
        axis=0,
    )


def exchange_pair(rows, step):
    count = pool_size()
    upper = (lax.axis_index("pool") & step) != 0
    other = lax.ppermute(rows, "pool", [(i, i ^ step) for i in range(count)])
    return jnp.concatenate([jnp.where(upper, other, rows), jnp.where(upper, rows, other)], axis=0)


def gather_rows(rows, beside=None):
    count = pool_size()
    step = 4
    held = None if beside is None else beside(rows)
    while step < count:
        if step * 4 <= count:
            rows = exchange_quads(rows, step)
            step *= 4
        else:
            rows = exchange_pair(rows, step)
            step *= 2
    if held is not None:
        rows, held = lax.optimization_barrier((rows, held))
    fours = [[4 * k + j for j in range(4)] for k in range(count // 4)]
    rows = lax.all_gather(rows, "pool", axis=0, axis_index_groups=fours, tiled=True)
    return rows if beside is None else (rows, held)


def core_halves(partial):
    count = pool_size()
    width = partial.shape[-1]
    blocks = partial.reshape(2, 2, count // 4, -1, width)
    odd = (lax.axis_index("pool") & 1) != 0
    keep = jnp.where(odd, blocks[:, 1], blocks[:, 0])
    give = jnp.where(odd, blocks[:, 0], blocks[:, 1])
    return (
        keep.transpose(1, 0, 2, 3).reshape(count // 2, -1, width),
        give.transpose(1, 0, 2, 3).reshape(count // 2, -1, width),
    )


def swap_cores(block):
    count = pool_size()
    return lax.ppermute(block, "pool", [(i, i ^ 1) for i in range(count)])


def exchange_chips(blocks):
    count = pool_size()
    same_core = [[2 * k + c for k in range(count // 2)] for c in range(2)]
    return lax.all_to_all(blocks, "pool", 0, 0, tiled=True, axis_index_groups=same_core)


def pair_columns(kept, received):
    odd = (lax.axis_index("pool") & 1) != 0
    return jnp.concatenate(
        [jnp.where(odd, received, kept), jnp.where(odd, kept, received)], axis=-1
    )


CHUNKS = 8
LANES = 128
KERNEL_VMEM = 24 * 1024 * 1024
BRING_VMEM = 40 * 1024 * 1024


def whole_block(shape):
    return pl.BlockSpec(shape, lambda: (0,) * len(shape))


def own_lift(rows_ref, down_ref, marks_ref, first_slot):
    ranks = down_ref.shape[0]
    width = down_ref.shape[1]
    step = width // CHUNKS
    total = None
    for k in range(CHUNKS):
        part = lax.dot_general(
            rows_ref[:, k * step : (k + 1) * step],
            down_ref[:, k * step : (k + 1) * step],
            (((1,), (1,)), ((), ())),
            preferred_element_type=jnp.float32,
        )
        total = part if total is None else total + part
    marks = marks_ref[...].astype(jnp.float32)
    slots = (marks[:, 0:1] * 32.0 + marks[:, 1:2]).astype(jnp.int32)
    place = lax.broadcasted_iota(jnp.int32, total.shape, 1) // ADAPTER_RANK + first_slot
    return jnp.where(slots == place, total, 0.0).astype(jnp.bfloat16)


def split_store(values, odd, kept_ref, given_ref, first, add):
    width = values.shape[1]
    size = values.shape[0] // 4
    local = kept_ref.shape[1]
    spot = pl.ds(first, width)
    for y in range(2):
        even_rows = values[2 * y * size : (2 * y + 1) * size]
        odd_rows = values[(2 * y + 1) * size : (2 * y + 2) * size]
        kept = jnp.where(odd, odd_rows, even_rows)
        given = jnp.where(odd, even_rows, odd_rows)
        for z in range(size // local):
            k = 2 * z + y
            kept_piece = kept[z * local : (z + 1) * local]
            given_piece = given[z * local : (z + 1) * local]
            if add:
                kept_piece = kept_piece + kept_ref[k, :, spot]
                given_piece = given_piece + given_ref[k, :, spot]
            kept_ref[k, :, spot] = kept_piece
            given_ref[k, :, spot] = given_piece


def query_kernel(
    where_ref, rows_ref, marks_ref, query_vmem, keyval_vmem, down_vmem, up_vmem,
    kept_ref, given_ref,
):
    me = where_ref[0]
    odd = (me % 2) == 1
    width = down_vmem.shape[1]
    step = width // CHUNKS
    lifted = own_lift(rows_ref, down_vmem, marks_ref, where_ref[1])
    for k in range(CHUNKS):
        spot = slice(k * step, (k + 1) * step)
        delta = adapter_scale * jnp.dot(
            lifted, up_vmem[:, spot], preferred_element_type=jnp.float32
        )
        split_store(delta, odd, kept_ref, given_ref, k * step, False)
    query = None
    for k in range(CHUNKS):
        spot = slice(k * step, (k + 1) * step)
        part = jnp.dot(rows_ref[:, spot], query_vmem[spot], preferred_element_type=jnp.float32)
        query = part if query is None else query + part
    columns = query.shape[1]
    split_store(
        query, odd, kept_ref, given_ref, pl.multiple_of(me * columns, LANES), True
    )
    keyval = None
    for k in range(CHUNKS):
        spot = slice(k * step, (k + 1) * step)
        part = jnp.dot(rows_ref[:, spot], keyval_vmem[spot], preferred_element_type=jnp.float32)
        keyval = part if keyval is None else keyval + part
    none = jnp.zeros_like(keyval)
    both = jnp.concatenate([jnp.where(odd, none, keyval), jnp.where(odd, keyval, none)], axis=1)
    split_store(both, odd, kept_ref, given_ref, width, False)


def query_halves(where, gathered, query_weight, key_value_weight, down, up, count, local_rows):
    rows = gathered.shape[0]
    width, columns = query_weight.shape
    keyval_columns = key_value_weight.shape[1]
    ranks = down.shape[0]
    sent = jax.ShapeDtypeStruct(
        (count // 2, local_rows, width + 2 * keyval_columns), jnp.float32
    )
    return pl.pallas_call(
        query_kernel,
        in_specs=[
            pl.BlockSpec(memory_space=pltpu.SMEM),
            whole_block((rows, width)),
            whole_block((rows, LANES)),
        ]
        + [pl.BlockSpec(memory_space=pltpu.VMEM)] * 4,
        out_specs=[whole_block(sent.shape)] * 2,
        out_shape=[sent, sent],
        compiler_params=pltpu.CompilerParams(vmem_limit_bytes=KERNEL_VMEM),
        name="query_halves",
    )(where, gathered[:, :width], gathered[:, width:], query_weight, key_value_weight, down, up)


def output_kernel(
    where_ref, rows_ref, marks_ref, output_vmem, down_vmem, up_vmem, kept_ref, given_ref
):
    me = where_ref[0]
    odd = (me % 2) == 1
    depth, width = output_vmem.shape
    step = width // CHUNKS
    lifted = own_lift(rows_ref, down_vmem, marks_ref, where_ref[1])
    columns = rows_ref[:, pl.ds(pl.multiple_of(me * depth, LANES), depth)]
    for k in range(CHUNKS):
        spot = slice(k * step, (k + 1) * step)
        part = jnp.dot(columns, output_vmem[:, spot], preferred_element_type=jnp.float32)
        part = part + adapter_scale * jnp.dot(
            lifted, up_vmem[:, spot], preferred_element_type=jnp.float32
        )
        split_store(part, odd, kept_ref, given_ref, k * step, False)


def output_halves(where, every_row, gathered, output_weight, down, up, count, local_rows):
    rows = every_row.shape[0]
    depth, width = output_weight.shape
    ranks = down.shape[0]
    sent = jax.ShapeDtypeStruct((count // 2, local_rows, width), jnp.float32)
    return pl.pallas_call(
        output_kernel,
        in_specs=[
            pl.BlockSpec(memory_space=pltpu.SMEM),
            whole_block((rows, width)),
            whole_block((rows, LANES)),
        ]
        + [pl.BlockSpec(memory_space=pltpu.VMEM)] * 3,
        out_specs=[whole_block(sent.shape)] * 2,
        out_shape=[sent, sent],
        compiler_params=pltpu.CompilerParams(vmem_limit_bytes=KERNEL_VMEM),
        name="output_halves",
    )(where, every_row, gathered[:, width:], output_weight, down, up)


def bring_kernel(*refs):
    count = (len(refs) - 2) // 2
    sources, targets, sems = refs[1 : count + 1], refs[count + 1 : -1], refs[-1]
    copies = []
    for source, target in zip(sources, targets):
        step = source.shape[0] // 4
        for k in range(4):
            spot = pl.ds(k * step, step)
            copies.append(
                pltpu.make_async_copy(source.at[spot], target.at[spot], sems.at[len(copies)])
            )
    for copy in copies:
        copy.start()
    for copy in copies:
        copy.wait()


def bring(where, arrays):
    size = sum(2 * array.size for array in arrays)
    return pl.pallas_call(
        bring_kernel,
        in_specs=[pl.BlockSpec(memory_space=pltpu.SMEM)]
        + [pl.BlockSpec(memory_space=pl.ANY)] * len(arrays),
        out_specs=[pl.BlockSpec(memory_space=pltpu.VMEM)] * len(arrays),
        out_shape=[jax.ShapeDtypeStruct(array.shape, array.dtype) for array in arrays],
        scratch_shapes=[pltpu.SemaphoreType.DMA((4 * len(arrays),))],
        compiler_params=pltpu.CompilerParams(vmem_limit_bytes=BRING_VMEM),
        cost_estimate=pl.CostEstimate(flops=0, bytes_accessed=2 * size, transcendentals=0),
        name="bring",
    )(where, *arrays)


def by_rank(factor):
    return factor.transpose(0, 2, 1).reshape(-1, factor.shape[1])


def body(
    hidden,
    gain,
    query_weight,
    key_value_weight,
    output_weight,
    query_down_factor,
    query_up_factor,
    output_down_factor,
    output_up_factor,
    key_cache,
    value_cache,
    lengths,
    request_adapter,
    adapter_slot,
):
    count = pool_size()
    own_slots = query_down_factor.shape[0]
    local_rows = hidden.shape[0]
    col_width = query_weight.shape[1]

    normalized_input = norm_rows(hidden, gain)
    slot_ids = lookup_slots(request_adapter, adapter_slot)
    digits = jnp.stack([slot_ids // 32, slot_ids % 32], axis=1).astype(jnp.bfloat16)
    sent = jnp.concatenate([normalized_input, jnp.pad(digits, ((0, 0), (0, 126)))], axis=1)
    first_slot = lax.axis_index("pool") * own_slots
    where = jnp.stack([lax.axis_index("pool"), first_slot]).astype(jnp.int32)
    aligned = col_width % LANES == 0 and key_value_weight.shape[1] % LANES == 0
    if aligned:

        def bring_query(rows):
            now, _ = lax.optimization_barrier((where, rows))
            return bring(
                now,
                [query_weight],
            )

        gathered, (query_near,) = gather_rows(sent, bring_query)
    else:
        gathered = gather_rows(sent)
    gathered_rows = gathered[:, :MODEL_WIDTH]
    all_digits = gathered[:, MODEL_WIDTH : MODEL_WIDTH + 2].astype(jnp.int32)
    slot_ids = all_digits[:, 0] * 32 + all_digits[:, 1]
    request_total = gathered_rows.shape[0]

    owner_mask = (
        slot_ids[:, None] == first_slot + jnp.arange(own_slots, dtype=jnp.int32)[None, :]
    )
    bf_zero = jnp.zeros((), jnp.bfloat16)

    query_width = MODEL_WIDTH
    if aligned:
        kept, given = query_halves(
            where,
            gathered,
            query_near,
            key_value_weight,
            by_rank(query_down_factor),
            query_up_factor.reshape(own_slots * ADAPTER_RANK, -1),
            count,
            local_rows,
        )
        leaving = kept + swap_cores(given)
    else:
        query_shrunk = owner_shrunk(gathered_rows, query_down_factor, owner_mask)
        lifted_rows = jnp.where(owner_mask[:, :, None], query_shrunk[:, None, :], bf_zero).reshape(
            request_total, own_slots * ADAPTER_RANK
        )
        query_delta = adapter_scale * jnp.dot(
            lifted_rows,
            query_up_factor.reshape(own_slots * ADAPTER_RANK, -1),
            preferred_element_type=jnp.float32,
        )
        kept_delta, given_delta = core_halves(query_delta)
        received_delta = swap_cores(given_delta)
        base = jnp.concatenate(
            [
                jnp.dot(gathered_rows, query_weight, preferred_element_type=jnp.float32),
                jnp.dot(gathered_rows, key_value_weight, preferred_element_type=jnp.float32),
            ],
            axis=1,
        )
        kept_base, given_base = core_halves(base)
        received_base = swap_cores(given_base)
        pair_query = pair_columns(kept_base[:, :, :col_width], received_base[:, :, :col_width])
        pair_keyval = pair_columns(kept_base[:, :, col_width:], received_base[:, :, col_width:])
        pair_delta = kept_delta + received_delta
        first_column = (lax.axis_index("pool") // 2) * (2 * col_width)
        there = lax.dynamic_slice_in_dim(pair_delta, first_column, 2 * col_width, 2)
        pair_delta = lax.dynamic_update_slice_in_dim(pair_delta, there + pair_query, first_column, 2)
        leaving = jnp.concatenate([pair_delta, pair_keyval], axis=2)
    arrived = exchange_chips(leaving)
    arrived, lengths = lax.optimization_barrier((arrived, lengths))
    query_rows = jnp.sum(arrived[:, :, :query_width], axis=0).astype(jnp.bfloat16)
    keyval_rows = arrived[:, :, query_width:].astype(jnp.bfloat16)
    keyval_rows = keyval_rows.reshape(count // 2, local_rows, 2, -1)
    keyval_rows = keyval_rows.transpose(1, 0, 2, 3).reshape(local_rows, -1)

    attention_output = attend(query_rows, keyval_rows, key_cache, value_cache, lengths)
    if aligned:

        def bring_output(rows):
            now, _ = lax.optimization_barrier((where, rows))
            return bring(now, [output_weight])

        every_row, (output_near,) = gather_rows(attention_output, bring_output)
    else:
        every_row = gather_rows(attention_output)
    if aligned:
        kept, given = output_halves(
            where,
            every_row,
            gathered,
            output_near,
            by_rank(output_down_factor),
            output_up_factor.reshape(own_slots * ADAPTER_RANK, -1),
            count,
            local_rows,
        )
    else:
        out_width = output_weight.shape[0]
        columns = lax.dynamic_slice_in_dim(every_row, lax.axis_index("pool") * out_width, out_width, 1)
        output_shrunk = owner_shrunk(every_row, output_down_factor, owner_mask)
        lifted_rows = jnp.where(owner_mask[:, :, None], output_shrunk[:, None, :], bf_zero).reshape(
            request_total, own_slots * ADAPTER_RANK
        )
        up_rows = output_up_factor.reshape(own_slots * ADAPTER_RANK, MODEL_WIDTH)
        partial = jnp.dot(
            columns, output_weight, preferred_element_type=jnp.float32
        ) + adapter_scale * jnp.dot(lifted_rows, up_rows, preferred_element_type=jnp.float32)
        kept, given = core_halves(partial)
    pair_sums = (kept + swap_cores(given)).astype(jnp.bfloat16)
    arrived = exchange_chips(pair_sums).astype(jnp.float32)
    return jnp.sum(arrived, axis=0).astype(jnp.bfloat16)


def solution(mesh):
    placed = (
        P(("groups", "pool"), None),
        P(),
        P(None, "pool"),
        P(None, "pool"),
        P("pool", None),
        P(("groups", "pool"), None, None),
        P(("groups", "pool"), None, None),
        P(("groups", "pool"), None, None),
        P(("groups", "pool"), None, None),
        P(("groups", "pool"), None, None),
        P(("groups", "pool"), None, None),
        P(("groups", "pool")),
        P(("groups", "pool")),
        P("groups"),
    )
    return jax.shard_map(
        body, mesh=mesh, in_specs=placed, out_specs=P(("groups", "pool"), None), check_vma=False
    )
```

```python
import jax
import jax.numpy as jnp
from jax import lax
from jax.experimental import pallas as pl
from jax.experimental.pallas import tpu as pltpu
from jax.sharding import PartitionSpec as P

MODEL_WIDTH = 8192
H = 64
KVH = 8
HEAD_WIDTH = 128
ADAPTER_RANK = 16
CACHE = 512
DKV = 1024


adapter_scale = 0.5
norm_eps = 1e-05


def norm_rows(hidden, gain):
    values = hidden.astype(jnp.float32)
    factor = lax.rsqrt(jnp.mean(values * values, axis=-1, keepdims=True) + norm_eps)
    return (values * factor * gain).astype(jnp.bfloat16)


def lookup_slots(all_ids, adapter_slot):
    table_size = adapter_slot.shape[0]
    matches = all_ids[:, None] == jnp.arange(table_size, dtype=jnp.int32)[None, :]
    return jnp.sum(jnp.where(matches, adapter_slot[None, :], 0), axis=1)


def attend(query_rows, keyval_rows, key_cache, value_cache, lengths):
    group_size = H // KVH
    local_rows = query_rows.shape[0]
    heads_q = query_rows.reshape(local_rows, KVH, group_size, HEAD_WIDTH)
    new_keys = keyval_rows[:, :DKV].reshape(local_rows, KVH, HEAD_WIDTH)
    new_values = keyval_rows[:, DKV:].reshape(local_rows, KVH, HEAD_WIDTH)
    cached_keys = key_cache.reshape(local_rows, CACHE, KVH, HEAD_WIDTH)
    cached_values = value_cache.reshape(local_rows, CACHE, KVH, HEAD_WIDTH)
    factor = HEAD_WIDTH ** (-0.5)
    scores = (
        jnp.einsum("rkgd,rckd->rkgc", heads_q, cached_keys, preferred_element_type=jnp.float32)
        * factor
    )
    own_score = (
        jnp.einsum("rkgd,rkd->rkg", heads_q, new_keys, preferred_element_type=jnp.float32) * factor
    )
    in_cache = (jnp.arange(CACHE, dtype=jnp.int32)[None, :] < lengths[:, None])[:, None, None, :]
    scores = jnp.where(in_cache, scores, -1e30)
    highest = jnp.maximum(jnp.max(scores, axis=-1), own_score)
    cached_exp = jnp.where(in_cache, jnp.exp(scores - highest[..., None]), 0.0)
    own_exp = jnp.exp(own_score - highest)
    softmax_sum = jnp.sum(cached_exp, axis=-1) + own_exp
    cached_weight = (cached_exp / softmax_sum[..., None]).astype(jnp.bfloat16)
    own_weight = (own_exp / softmax_sum).astype(jnp.bfloat16)
    mixture = jnp.einsum(
        "rkgc,rckd->rkgd", cached_weight, cached_values, preferred_element_type=jnp.float32
    )
    mixture = (
        mixture
        + own_weight.astype(jnp.float32)[..., None] * new_values.astype(jnp.float32)[:, :, None, :]
    )
    return mixture.reshape(local_rows, KVH * group_size * HEAD_WIDTH).astype(jnp.bfloat16)


def owner_shrunk(rows, down_factor, owner_mask):
    partial = jnp.einsum("we,bey->wby", rows, down_factor, preferred_element_type=jnp.float32)
    return jnp.sum(jnp.where(owner_mask[:, :, None], partial, 0.0), axis=1).astype(jnp.bfloat16)


def pool_size():
    return lax.axis_size("pool")


def exchange_quads(rows, step):
    count = pool_size()
    me = lax.axis_index("pool")
    parts = [rows] + [
        lax.ppermute(rows, "pool", [(i, i ^ (k * step)) for i in range(count)]) for k in (1, 2, 3)
    ]
    low = (me & step) != 0
    high = (me & (2 * step)) != 0
    swapped = [
        jnp.where(low, parts[1], parts[0]),
        jnp.where(low, parts[0], parts[1]),
        jnp.where(low, parts[3], parts[2]),
        jnp.where(low, parts[2], parts[3]),
    ]
    return jnp.concatenate(
        [
            jnp.where(high, swapped[2], swapped[0]),
            jnp.where(high, swapped[3], swapped[1]),
            jnp.where(high, swapped[0], swapped[2]),
            jnp.where(high, swapped[1], swapped[3]),
        ],
        axis=0,
    )


def exchange_pair(rows, step):
    count = pool_size()
    upper = (lax.axis_index("pool") & step) != 0
    other = lax.ppermute(rows, "pool", [(i, i ^ step) for i in range(count)])
    return jnp.concatenate([jnp.where(upper, other, rows), jnp.where(upper, rows, other)], axis=0)


def gather_rows(rows, beside=None):
    count = pool_size()
    step = 4
    held = None if beside is None else beside(rows)
    while step < count:
        if step * 4 <= count:
            rows = exchange_quads(rows, step)
            step *= 4
        else:
            rows = exchange_pair(rows, step)
            step *= 2
    if held is not None:
        rows, held = lax.optimization_barrier((rows, held))
    fours = [[4 * k + j for j in range(4)] for k in range(count // 4)]
    rows = lax.all_gather(rows, "pool", axis=0, axis_index_groups=fours, tiled=True)
    return rows if beside is None else (rows, held)


def core_halves(partial):
    count = pool_size()
    width = partial.shape[-1]
    blocks = partial.reshape(2, 2, count // 4, -1, width)
    odd = (lax.axis_index("pool") & 1) != 0
    keep = jnp.where(odd, blocks[:, 1], blocks[:, 0])
    give = jnp.where(odd, blocks[:, 0], blocks[:, 1])
    return (
        keep.transpose(1, 0, 2, 3).reshape(count // 2, -1, width),
        give.transpose(1, 0, 2, 3).reshape(count // 2, -1, width),
    )


def swap_cores(block):
    count = pool_size()
    return lax.ppermute(block, "pool", [(i, i ^ 1) for i in range(count)])


def exchange_chips(blocks):
    count = pool_size()
    same_core = [[2 * k + c for k in range(count // 2)] for c in range(2)]
    return lax.all_to_all(blocks, "pool", 0, 0, tiled=True, axis_index_groups=same_core)


def pair_columns(kept, received):
    odd = (lax.axis_index("pool") & 1) != 0
    return jnp.concatenate(
        [jnp.where(odd, received, kept), jnp.where(odd, kept, received)], axis=-1
    )


CHUNKS = 8
NORM_VMEM = 57000 * 1024
LANES = 128
KERNEL_VMEM = 24 * 1024 * 1024
BRING_VMEM = 40 * 1024 * 1024


def whole_block(shape):
    return pl.BlockSpec(shape, lambda: (0,) * len(shape))


def own_lift(rows_ref, down_ref, marks_ref, first_slot):
    ranks = down_ref.shape[0]
    width = down_ref.shape[1]
    step = width // CHUNKS
    total = None
    for k in range(CHUNKS):
        part = lax.dot_general(
            rows_ref[:, k * step : (k + 1) * step],
            down_ref[:, k * step : (k + 1) * step],
            (((1,), (1,)), ((), ())),
            preferred_element_type=jnp.float32,
        )
        total = part if total is None else total + part
    marks = marks_ref[...].astype(jnp.float32)
    slots = (marks[:, 0:1] * 32.0 + marks[:, 1:2]).astype(jnp.int32)
    place = lax.broadcasted_iota(jnp.int32, total.shape, 1) // ADAPTER_RANK + first_slot
    return jnp.where(slots == place, total, 0.0).astype(jnp.bfloat16)


def split_store(values, odd, kept_ref, given_ref, first, add):
    width = values.shape[1]
    size = values.shape[0] // 4
    local = kept_ref.shape[1]
    spot = pl.ds(first, width)
    for y in range(2):
        even_rows = values[2 * y * size : (2 * y + 1) * size]
        odd_rows = values[(2 * y + 1) * size : (2 * y + 2) * size]
        kept = jnp.where(odd, odd_rows, even_rows)
        given = jnp.where(odd, even_rows, odd_rows)
        for z in range(size // local):
            k = 2 * z + y
            kept_piece = kept[z * local : (z + 1) * local]
            given_piece = given[z * local : (z + 1) * local]
            if add:
                kept_piece = kept_piece + kept_ref[k, :, spot]
                given_piece = given_piece + given_ref[k, :, spot]
            kept_ref[k, :, spot] = kept_piece
            given_ref[k, :, spot] = given_piece


def query_kernel(
    where_ref, rows_ref, marks_ref, query_vmem, keyval_vmem, down_vmem, up_vmem,
    kept_ref, given_ref,
):
    me = where_ref[0]
    odd = (me % 2) == 1
    width = down_vmem.shape[1]
    step = width // CHUNKS
    lifted = own_lift(rows_ref, down_vmem, marks_ref, where_ref[1])
    for k in range(CHUNKS):
        spot = slice(k * step, (k + 1) * step)
        delta = adapter_scale * jnp.dot(
            lifted, up_vmem[:, spot], preferred_element_type=jnp.float32
        )
        split_store(delta, odd, kept_ref, given_ref, k * step, False)
    query = None
    for k in range(CHUNKS):
        spot = slice(k * step, (k + 1) * step)
        part = jnp.dot(rows_ref[:, spot], query_vmem[spot], preferred_element_type=jnp.float32)
        query = part if query is None else query + part
    columns = query.shape[1]
    split_store(
        query, odd, kept_ref, given_ref, pl.multiple_of(me * columns, LANES), True
    )
    keyval = None
    for k in range(CHUNKS):
        spot = slice(k * step, (k + 1) * step)
        part = jnp.dot(rows_ref[:, spot], keyval_vmem[spot], preferred_element_type=jnp.float32)
        keyval = part if keyval is None else keyval + part
    none = jnp.zeros_like(keyval)
    both = jnp.concatenate([jnp.where(odd, none, keyval), jnp.where(odd, keyval, none)], axis=1)
    split_store(both, odd, kept_ref, given_ref, width, False)


def query_halves(where, gathered, query_weight, key_value_weight, down, up, count, local_rows):
    rows = gathered.shape[0]
    width, columns = query_weight.shape
    keyval_columns = key_value_weight.shape[1]
    ranks = down.shape[0]
    sent = jax.ShapeDtypeStruct(
        (count // 2, local_rows, width + 2 * keyval_columns), jnp.float32
    )
    return pl.pallas_call(
        query_kernel,
        in_specs=[
            pl.BlockSpec(memory_space=pltpu.SMEM),
            whole_block((rows, width)),
            whole_block((rows, LANES)),
        ]
        + [pl.BlockSpec(memory_space=pltpu.VMEM)] * 4,
        out_specs=[whole_block(sent.shape)] * 2,
        out_shape=[sent, sent],
        compiler_params=pltpu.CompilerParams(vmem_limit_bytes=KERNEL_VMEM),
        name="query_halves",
    )(where, gathered[:, :width], gathered[:, width:], query_weight, key_value_weight, down, up)


def output_kernel(
    where_ref, rows_ref, marks_ref, output_vmem, down_vmem, up_vmem, kept_ref, given_ref
):
    me = where_ref[0]
    odd = (me % 2) == 1
    depth, width = output_vmem.shape
    step = width // CHUNKS
    lifted = own_lift(rows_ref, down_vmem, marks_ref, where_ref[1])
    columns = rows_ref[:, pl.ds(pl.multiple_of(me * depth, LANES), depth)]
    for k in range(CHUNKS):
        spot = slice(k * step, (k + 1) * step)
        part = jnp.dot(columns, output_vmem[:, spot], preferred_element_type=jnp.float32)
        part = part + adapter_scale * jnp.dot(
            lifted, up_vmem[:, spot], preferred_element_type=jnp.float32
        )
        split_store(part, odd, kept_ref, given_ref, k * step, False)


def output_halves(where, every_row, gathered, output_weight, down, up, count, local_rows):
    rows = every_row.shape[0]
    depth, width = output_weight.shape
    ranks = down.shape[0]
    sent = jax.ShapeDtypeStruct((count // 2, local_rows, width), jnp.float32)
    return pl.pallas_call(
        output_kernel,
        in_specs=[
            pl.BlockSpec(memory_space=pltpu.SMEM),
            whole_block((rows, width)),
            whole_block((rows, LANES)),
        ]
        + [pl.BlockSpec(memory_space=pltpu.VMEM)] * 3,
        out_specs=[whole_block(sent.shape)] * 2,
        out_shape=[sent, sent],
        compiler_params=pltpu.CompilerParams(vmem_limit_bytes=KERNEL_VMEM),
        name="output_halves",
    )(where, every_row, gathered[:, width:], output_weight, down, up)


def bring_kernel(*refs):
    count = (len(refs) - 2) // 2
    sources, targets, sems = refs[1 : count + 1], refs[count + 1 : -1], refs[-1]
    copies = []
    for source, target in zip(sources, targets):
        step = source.shape[0] // 4
        for k in range(4):
            spot = pl.ds(k * step, step)
            copies.append(
                pltpu.make_async_copy(source.at[spot], target.at[spot], sems.at[len(copies)])
            )
    for copy in copies:
        copy.start()
    for copy in copies:
        copy.wait()


def bring(where, arrays):
    size = sum(2 * array.size for array in arrays)
    return pl.pallas_call(
        bring_kernel,
        in_specs=[pl.BlockSpec(memory_space=pltpu.SMEM)]
        + [pl.BlockSpec(memory_space=pl.ANY)] * len(arrays),
        out_specs=[pl.BlockSpec(memory_space=pltpu.VMEM)] * len(arrays),
        out_shape=[jax.ShapeDtypeStruct(array.shape, array.dtype) for array in arrays],
        scratch_shapes=[pltpu.SemaphoreType.DMA((4 * len(arrays),))],
        compiler_params=pltpu.CompilerParams(vmem_limit_bytes=BRING_VMEM),
        cost_estimate=pl.CostEstimate(flops=0, bytes_accessed=2 * size, transcendentals=0),
        name="bring",
    )(where, *arrays)


def norm_kernel(
    hidden_hbm, gain_hbm, adapter_hbm, slot_hbm,
    sent_ref, hidden_ref, gain_ref, adapter_ref, slot_ref, sems,
):
    copies = [
        pltpu.make_async_copy(source, target, sems.at[k])
        for k, (source, target) in enumerate(
            (
                (adapter_hbm, adapter_ref),
                (slot_hbm, slot_ref),
                (hidden_hbm, hidden_ref),
                (gain_hbm, gain_ref),
            )
        )
    ]
    for copy in copies:
        copy.start()
    rows, width = hidden_ref.shape
    copies[2].wait()
    values = hidden_ref[...].astype(jnp.float32)
    factor = lax.rsqrt(jnp.mean(values * values, axis=-1, keepdims=True) + norm_eps)
    copies[3].wait()
    sent_ref[:, :width] = (values * factor * gain_ref[...]).astype(jnp.bfloat16)
    copies[0].wait()
    copies[1].wait()
    row = lax.broadcasted_iota(jnp.int32, (rows, LANES), 0)
    lane = lax.broadcasted_iota(jnp.int32, (rows, LANES), 1)
    marks = jnp.zeros((rows, LANES), jnp.int32)
    for r in range(rows):
        slot = slot_ref[adapter_ref[r]]
        digit = jnp.where(lane == 0, slot // 32, jnp.where(lane == 1, slot % 32, 0))
        marks = jnp.where(row == r, digit, marks)
    sent_ref[:, width:] = marks.astype(jnp.float32).astype(jnp.bfloat16)


def norm_and_marks(hidden, gain, request_adapter, adapter_slot):
    rows, width = hidden.shape
    return pl.pallas_call(
        norm_kernel,
        in_specs=[pl.BlockSpec(memory_space=pl.ANY)] * 4,
        out_specs=whole_block((rows, width + LANES)),
        out_shape=jax.ShapeDtypeStruct((rows, width + LANES), jnp.bfloat16),
        scratch_shapes=[
            pltpu.VMEM(hidden.shape, jnp.bfloat16),
            pltpu.VMEM((1, width), jnp.float32),
            pltpu.SMEM(request_adapter.shape, jnp.int32),
            pltpu.SMEM(adapter_slot.shape, jnp.int32),
            pltpu.SemaphoreType.DMA((4,)),
        ],
        compiler_params=pltpu.CompilerParams(vmem_limit_bytes=NORM_VMEM),
        name="norm_and_marks",
    )(hidden, gain.reshape(1, width), request_adapter, adapter_slot)


def by_rank(factor):
    return factor.transpose(0, 2, 1).reshape(-1, factor.shape[1])


def body(
    hidden,
    gain,
    query_weight,
    key_value_weight,
    output_weight,
    query_down_factor,
    query_up_factor,
    output_down_factor,
    output_up_factor,
    key_cache,
    value_cache,
    lengths,
    request_adapter,
    adapter_slot,
):
    count = pool_size()
    own_slots = query_down_factor.shape[0]
    local_rows = hidden.shape[0]
    col_width = query_weight.shape[1]

    aligned = col_width % LANES == 0 and key_value_weight.shape[1] % LANES == 0
    if aligned:
        sent = norm_and_marks(hidden, gain, request_adapter, adapter_slot)
    else:
        normalized_input = norm_rows(hidden, gain)
        slot_ids = lookup_slots(request_adapter, adapter_slot)
        digits = jnp.stack([slot_ids // 32, slot_ids % 32], axis=1).astype(jnp.bfloat16)
        sent = jnp.concatenate([normalized_input, jnp.pad(digits, ((0, 0), (0, 126)))], axis=1)
    first_slot = lax.axis_index("pool") * own_slots
    where = jnp.stack([lax.axis_index("pool"), first_slot]).astype(jnp.int32)
    if aligned:

        def bring_query(rows):
            now, _ = lax.optimization_barrier((where, rows))
            return bring(
                now,
                [query_weight],
            )

        gathered, (query_near,) = gather_rows(sent, bring_query)
    else:
        gathered = gather_rows(sent)
    gathered_rows = gathered[:, :MODEL_WIDTH]
    all_digits = gathered[:, MODEL_WIDTH : MODEL_WIDTH + 2].astype(jnp.int32)
    slot_ids = all_digits[:, 0] * 32 + all_digits[:, 1]
    request_total = gathered_rows.shape[0]

    owner_mask = (
        slot_ids[:, None] == first_slot + jnp.arange(own_slots, dtype=jnp.int32)[None, :]
    )
    bf_zero = jnp.zeros((), jnp.bfloat16)

    query_width = MODEL_WIDTH
    if aligned:
        kept, given = query_halves(
            where,
            gathered,
            query_near,
            key_value_weight,
            by_rank(query_down_factor),
            query_up_factor.reshape(own_slots * ADAPTER_RANK, -1),
            count,
            local_rows,
        )
        leaving = kept + swap_cores(given)
    else:
        query_shrunk = owner_shrunk(gathered_rows, query_down_factor, owner_mask)
        lifted_rows = jnp.where(owner_mask[:, :, None], query_shrunk[:, None, :], bf_zero).reshape(
            request_total, own_slots * ADAPTER_RANK
        )
        query_delta = adapter_scale * jnp.dot(
            lifted_rows,
            query_up_factor.reshape(own_slots * ADAPTER_RANK, -1),
            preferred_element_type=jnp.float32,
        )
        kept_delta, given_delta = core_halves(query_delta)
        received_delta = swap_cores(given_delta)
        base = jnp.concatenate(
            [
                jnp.dot(gathered_rows, query_weight, preferred_element_type=jnp.float32),
                jnp.dot(gathered_rows, key_value_weight, preferred_element_type=jnp.float32),
            ],
            axis=1,
        )
        kept_base, given_base = core_halves(base)
        received_base = swap_cores(given_base)
        pair_query = pair_columns(kept_base[:, :, :col_width], received_base[:, :, :col_width])
        pair_keyval = pair_columns(kept_base[:, :, col_width:], received_base[:, :, col_width:])
        pair_delta = kept_delta + received_delta
        first_column = (lax.axis_index("pool") // 2) * (2 * col_width)
        there = lax.dynamic_slice_in_dim(pair_delta, first_column, 2 * col_width, 2)
        pair_delta = lax.dynamic_update_slice_in_dim(pair_delta, there + pair_query, first_column, 2)
        leaving = jnp.concatenate([pair_delta, pair_keyval], axis=2)
    arrived = exchange_chips(leaving)
    arrived, lengths = lax.optimization_barrier((arrived, lengths))
    query_rows = jnp.sum(arrived[:, :, :query_width], axis=0).astype(jnp.bfloat16)
    keyval_rows = arrived[:, :, query_width:].astype(jnp.bfloat16)
    keyval_rows = keyval_rows.reshape(count // 2, local_rows, 2, -1)
    keyval_rows = keyval_rows.transpose(1, 0, 2, 3).reshape(local_rows, -1)

    attention_output = attend(query_rows, keyval_rows, key_cache, value_cache, lengths)
    if aligned:

        def bring_output(rows):
            now, _ = lax.optimization_barrier((where, rows))
            return bring(now, [output_weight])

        every_row, (output_near,) = gather_rows(attention_output, bring_output)
    else:
        every_row = gather_rows(attention_output)
    if aligned:
        kept, given = output_halves(
            where,
            every_row,
            gathered,
            output_near,
            by_rank(output_down_factor),
            output_up_factor.reshape(own_slots * ADAPTER_RANK, -1),
            count,
            local_rows,
        )
    else:
        out_width = output_weight.shape[0]
        columns = lax.dynamic_slice_in_dim(every_row, lax.axis_index("pool") * out_width, out_width, 1)
        output_shrunk = owner_shrunk(every_row, output_down_factor, owner_mask)
        lifted_rows = jnp.where(owner_mask[:, :, None], output_shrunk[:, None, :], bf_zero).reshape(
            request_total, own_slots * ADAPTER_RANK
        )
        up_rows = output_up_factor.reshape(own_slots * ADAPTER_RANK, MODEL_WIDTH)
        partial = jnp.dot(
            columns, output_weight, preferred_element_type=jnp.float32
        ) + adapter_scale * jnp.dot(lifted_rows, up_rows, preferred_element_type=jnp.float32)
        kept, given = core_halves(partial)
    pair_sums = (kept + swap_cores(given)).astype(jnp.bfloat16)
    arrived = exchange_chips(pair_sums).astype(jnp.float32)
    return jnp.sum(arrived, axis=0).astype(jnp.bfloat16)


def solution(mesh):
    placed = (
        P(("groups", "pool"), None),
        P(),
        P(None, "pool"),
        P(None, "pool"),
        P("pool", None),
        P(("groups", "pool"), None, None),
        P(("groups", "pool"), None, None),
        P(("groups", "pool"), None, None),
        P(("groups", "pool"), None, None),
        P(("groups", "pool"), None, None),
        P(("groups", "pool"), None, None),
        P(("groups", "pool")),
        P(("groups", "pool")),
        P("groups"),
    )
    return jax.shard_map(
        body, mesh=mesh, in_specs=placed, out_specs=P(("groups", "pool"), None), check_vma=False
    )
```

```python
import jax
import jax.numpy as jnp
from jax import lax
from jax.experimental import pallas as pl
from jax.experimental.pallas import tpu as pltpu
from jax.sharding import PartitionSpec as P

MODEL_WIDTH = 8192
H = 64
KVH = 8
HEAD_WIDTH = 128
ADAPTER_RANK = 16
CACHE = 512
DKV = 1024


adapter_scale = 0.5
norm_eps = 1e-05


def norm_rows(hidden, gain):
    values = hidden.astype(jnp.float32)
    factor = lax.rsqrt(jnp.mean(values * values, axis=-1, keepdims=True) + norm_eps)
    return (values * factor * gain).astype(jnp.bfloat16)


def lookup_slots(all_ids, adapter_slot):
    table_size = adapter_slot.shape[0]
    matches = all_ids[:, None] == jnp.arange(table_size, dtype=jnp.int32)[None, :]
    return jnp.sum(jnp.where(matches, adapter_slot[None, :], 0), axis=1)


def attend(query_rows, keyval_rows, key_cache, value_cache, lengths):
    group_size = H // KVH
    local_rows = query_rows.shape[0]
    heads_q = query_rows.reshape(local_rows, KVH, group_size, HEAD_WIDTH)
    new_keys = keyval_rows[:, :DKV].reshape(local_rows, KVH, HEAD_WIDTH)
    new_values = keyval_rows[:, DKV:].reshape(local_rows, KVH, HEAD_WIDTH)
    cached_keys = key_cache.reshape(local_rows, CACHE, KVH, HEAD_WIDTH)
    cached_values = value_cache.reshape(local_rows, CACHE, KVH, HEAD_WIDTH)
    factor = HEAD_WIDTH ** (-0.5)
    scores = (
        jnp.einsum("rkgd,rckd->rkgc", heads_q, cached_keys, preferred_element_type=jnp.float32)
        * factor
    )
    own_score = (
        jnp.einsum("rkgd,rkd->rkg", heads_q, new_keys, preferred_element_type=jnp.float32) * factor
    )
    in_cache = (jnp.arange(CACHE, dtype=jnp.int32)[None, :] < lengths[:, None])[:, None, None, :]
    scores = jnp.where(in_cache, scores, -1e30)
    highest = jnp.maximum(jnp.max(scores, axis=-1), own_score)
    cached_exp = jnp.where(in_cache, jnp.exp(scores - highest[..., None]), 0.0)
    own_exp = jnp.exp(own_score - highest)
    softmax_sum = jnp.sum(cached_exp, axis=-1) + own_exp
    cached_weight = (cached_exp / softmax_sum[..., None]).astype(jnp.bfloat16)
    own_weight = (own_exp / softmax_sum).astype(jnp.bfloat16)
    mixture = jnp.einsum(
        "rkgc,rckd->rkgd", cached_weight, cached_values, preferred_element_type=jnp.float32
    )
    mixture = (
        mixture
        + own_weight.astype(jnp.float32)[..., None] * new_values.astype(jnp.float32)[:, :, None, :]
    )
    return mixture.reshape(local_rows, KVH * group_size * HEAD_WIDTH).astype(jnp.bfloat16)


def owner_shrunk(rows, down_factor, owner_mask):
    partial = jnp.einsum("we,bey->wby", rows, down_factor, preferred_element_type=jnp.float32)
    return jnp.sum(jnp.where(owner_mask[:, :, None], partial, 0.0), axis=1).astype(jnp.bfloat16)


def pool_size():
    return lax.axis_size("pool")


def exchange_quads(rows, step):
    count = pool_size()
    me = lax.axis_index("pool")
    parts = [rows] + [
        lax.ppermute(rows, "pool", [(i, i ^ (k * step)) for i in range(count)]) for k in (1, 2, 3)
    ]
    low = (me & step) != 0
    high = (me & (2 * step)) != 0
    swapped = [
        jnp.where(low, parts[1], parts[0]),
        jnp.where(low, parts[0], parts[1]),
        jnp.where(low, parts[3], parts[2]),
        jnp.where(low, parts[2], parts[3]),
    ]
    return jnp.concatenate(
        [
            jnp.where(high, swapped[2], swapped[0]),
            jnp.where(high, swapped[3], swapped[1]),
            jnp.where(high, swapped[0], swapped[2]),
            jnp.where(high, swapped[1], swapped[3]),
        ],
        axis=0,
    )


def exchange_pair(rows, step):
    count = pool_size()
    upper = (lax.axis_index("pool") & step) != 0
    other = lax.ppermute(rows, "pool", [(i, i ^ step) for i in range(count)])
    return jnp.concatenate([jnp.where(upper, other, rows), jnp.where(upper, rows, other)], axis=0)


def gather_rows(rows, beside=None):
    count = pool_size()
    step = 4
    held = None if beside is None else beside(rows)
    while step < count:
        if step * 4 <= count:
            rows = exchange_quads(rows, step)
            step *= 4
        else:
            rows = exchange_pair(rows, step)
            step *= 2
    if held is not None:
        rows, held = lax.optimization_barrier((rows, held))
    fours = [[4 * k + j for j in range(4)] for k in range(count // 4)]
    rows = lax.all_gather(rows, "pool", axis=0, axis_index_groups=fours, tiled=True)
    return rows if beside is None else (rows, held)


def core_halves(partial):
    count = pool_size()
    width = partial.shape[-1]
    blocks = partial.reshape(2, 2, count // 4, -1, width)
    odd = (lax.axis_index("pool") & 1) != 0
    keep = jnp.where(odd, blocks[:, 1], blocks[:, 0])
    give = jnp.where(odd, blocks[:, 0], blocks[:, 1])
    return (
        keep.transpose(1, 0, 2, 3).reshape(count // 2, -1, width),
        give.transpose(1, 0, 2, 3).reshape(count // 2, -1, width),
    )


def swap_cores(block):
    count = pool_size()
    return lax.ppermute(block, "pool", [(i, i ^ 1) for i in range(count)])


def exchange_chips(blocks):
    count = pool_size()
    same_core = [[2 * k + c for k in range(count // 2)] for c in range(2)]
    return lax.all_to_all(blocks, "pool", 0, 0, tiled=True, axis_index_groups=same_core)


def pair_columns(kept, received):
    odd = (lax.axis_index("pool") & 1) != 0
    return jnp.concatenate(
        [jnp.where(odd, received, kept), jnp.where(odd, kept, received)], axis=-1
    )


CHUNKS = 8
NORM_VMEM = 57000 * 1024
LANES = 128
KERNEL_VMEM = 24 * 1024 * 1024
BRING_VMEM = 40 * 1024 * 1024


def whole_block(shape):
    return pl.BlockSpec(shape, lambda: (0,) * len(shape))


def own_lift(rows_ref, down_ref, marks_ref, first_slot):
    ranks = down_ref.shape[0]
    width = down_ref.shape[1]
    step = width // CHUNKS
    total = None
    for k in range(CHUNKS):
        part = lax.dot_general(
            rows_ref[:, k * step : (k + 1) * step],
            down_ref[:, k * step : (k + 1) * step],
            (((1,), (1,)), ((), ())),
            preferred_element_type=jnp.float32,
        )
        total = part if total is None else total + part
    marks = marks_ref[...].astype(jnp.float32)
    slots = (marks[:, 0:1] * 32.0 + marks[:, 1:2]).astype(jnp.int32)
    place = lax.broadcasted_iota(jnp.int32, total.shape, 1) // ADAPTER_RANK + first_slot
    return jnp.where(slots == place, total, 0.0).astype(jnp.bfloat16)


def split_store(values, odd, place, kept_ref, given_ref, first, add):
    width = values.shape[1]
    size = values.shape[0] // 4
    local = kept_ref.shape[1]
    spot = pl.ds(first, width)
    for y in range(2):
        even_rows = values[2 * y * size : (2 * y + 1) * size]
        odd_rows = values[(2 * y + 1) * size : (2 * y + 2) * size]
        kept = jnp.where(odd, odd_rows, even_rows)
        given = jnp.where(odd, even_rows, odd_rows)
        for z in range(size // local):
            k = place(z, y)
            kept_piece = kept[z * local : (z + 1) * local]
            given_piece = given[z * local : (z + 1) * local]
            if add:
                kept_piece = kept_piece + kept_ref[k, :, spot]
                given_piece = given_piece + given_ref[k, :, spot]
            kept_ref[k, :, spot] = kept_piece
            given_ref[k, :, spot] = given_piece


def query_kernel(
    where_ref, rows_ref, marks_ref, query_vmem, keyval_vmem, down_vmem, up_vmem,
    kept_ref, given_ref,
):
    me = where_ref[0]
    odd = (me % 2) == 1
    far = kept_ref.shape[0] // 2

    def place(z, y):
        return jnp.bitwise_xor((me // 2) % 2, y) * far + jnp.bitwise_xor(me // 4, z)

    width = down_vmem.shape[1]
    step = width // CHUNKS
    lifted = own_lift(rows_ref, down_vmem, marks_ref, where_ref[1])
    for k in range(CHUNKS):
        spot = slice(k * step, (k + 1) * step)
        delta = adapter_scale * jnp.dot(
            lifted, up_vmem[:, spot], preferred_element_type=jnp.float32
        )
        split_store(delta, odd, place, kept_ref, given_ref, k * step, False)
    query = None
    for k in range(CHUNKS):
        spot = slice(k * step, (k + 1) * step)
        part = jnp.dot(rows_ref[:, spot], query_vmem[spot], preferred_element_type=jnp.float32)
        query = part if query is None else query + part
    columns = query.shape[1]
    split_store(
        query, odd, place, kept_ref, given_ref, pl.multiple_of(me * columns, LANES), True
    )
    keyval = None
    for k in range(CHUNKS):
        spot = slice(k * step, (k + 1) * step)
        part = jnp.dot(rows_ref[:, spot], keyval_vmem[spot], preferred_element_type=jnp.float32)
        keyval = part if keyval is None else keyval + part
    none = jnp.zeros_like(keyval)
    both = jnp.concatenate([jnp.where(odd, none, keyval), jnp.where(odd, keyval, none)], axis=1)
    split_store(both, odd, place, kept_ref, given_ref, width, False)


def query_halves(where, gathered, query_weight, key_value_weight, down, up, count, local_rows):
    rows = gathered.shape[0]
    width, columns = query_weight.shape
    keyval_columns = key_value_weight.shape[1]
    ranks = down.shape[0]
    sent = jax.ShapeDtypeStruct(
        (count // 2, local_rows, width + 2 * keyval_columns), jnp.float32
    )
    return pl.pallas_call(
        query_kernel,
        in_specs=[
            pl.BlockSpec(memory_space=pltpu.SMEM),
            whole_block((rows, width)),
            whole_block((rows, LANES)),
        ]
        + [pl.BlockSpec(memory_space=pltpu.VMEM)] * 4,
        out_specs=[whole_block(sent.shape)] * 2,
        out_shape=[sent, sent],
        compiler_params=pltpu.CompilerParams(vmem_limit_bytes=KERNEL_VMEM),
        name="query_halves",
    )(where, gathered[:, :width], gathered[:, width:], query_weight, key_value_weight, down, up)


def output_kernel(
    where_ref, rows_ref, marks_ref, output_vmem, down_vmem, up_vmem, kept_ref, given_ref
):
    me = where_ref[0]
    odd = (me % 2) == 1
    depth, width = output_vmem.shape
    step = width // CHUNKS
    lifted = own_lift(rows_ref, down_vmem, marks_ref, where_ref[1])
    columns = rows_ref[:, pl.ds(pl.multiple_of(me * depth, LANES), depth)]
    for k in range(CHUNKS):
        spot = slice(k * step, (k + 1) * step)
        part = jnp.dot(columns, output_vmem[:, spot], preferred_element_type=jnp.float32)
        part = part + adapter_scale * jnp.dot(
            lifted, up_vmem[:, spot], preferred_element_type=jnp.float32
        )
        split_store(part, odd, lambda z, y: 2 * z + y, kept_ref, given_ref, k * step, False)


def output_halves(where, every_row, gathered, output_weight, down, up, count, local_rows):
    rows = every_row.shape[0]
    depth, width = output_weight.shape
    ranks = down.shape[0]
    sent = jax.ShapeDtypeStruct((count // 2, local_rows, width), jnp.float32)
    return pl.pallas_call(
        output_kernel,
        in_specs=[
            pl.BlockSpec(memory_space=pltpu.SMEM),
            whole_block((rows, width)),
            whole_block((rows, LANES)),
        ]
        + [pl.BlockSpec(memory_space=pltpu.VMEM)] * 3,
        out_specs=[whole_block(sent.shape)] * 2,
        out_shape=[sent, sent],
        compiler_params=pltpu.CompilerParams(vmem_limit_bytes=KERNEL_VMEM),
        name="output_halves",
    )(where, every_row, gathered[:, width:], output_weight, down, up)


def bring_kernel(*refs):
    count = (len(refs) - 2) // 2
    sources, targets, sems = refs[1 : count + 1], refs[count + 1 : -1], refs[-1]
    copies = []
    for source, target in zip(sources, targets):
        step = source.shape[0] // 4
        for k in range(4):
            spot = pl.ds(k * step, step)
            copies.append(
                pltpu.make_async_copy(source.at[spot], target.at[spot], sems.at[len(copies)])
            )
    for copy in copies:
        copy.start()
    for copy in copies:
        copy.wait()


def bring(where, arrays):
    size = sum(2 * array.size for array in arrays)
    return pl.pallas_call(
        bring_kernel,
        in_specs=[pl.BlockSpec(memory_space=pltpu.SMEM)]
        + [pl.BlockSpec(memory_space=pl.ANY)] * len(arrays),
        out_specs=[pl.BlockSpec(memory_space=pltpu.VMEM)] * len(arrays),
        out_shape=[jax.ShapeDtypeStruct(array.shape, array.dtype) for array in arrays],
        scratch_shapes=[pltpu.SemaphoreType.DMA((4 * len(arrays),))],
        compiler_params=pltpu.CompilerParams(vmem_limit_bytes=BRING_VMEM),
        cost_estimate=pl.CostEstimate(flops=0, bytes_accessed=2 * size, transcendentals=0),
        name="bring",
    )(where, *arrays)


def norm_kernel(
    hidden_hbm, gain_hbm, adapter_hbm, slot_hbm,
    sent_ref, hidden_ref, gain_ref, adapter_ref, slot_ref, sems,
):
    copies = [
        pltpu.make_async_copy(source, target, sems.at[k])
        for k, (source, target) in enumerate(
            (
                (adapter_hbm, adapter_ref),
                (slot_hbm, slot_ref),
                (hidden_hbm, hidden_ref),
                (gain_hbm, gain_ref),
            )
        )
    ]
    for copy in copies:
        copy.start()
    rows, width = hidden_ref.shape
    copies[2].wait()
    values = hidden_ref[...].astype(jnp.float32)
    factor = lax.rsqrt(jnp.mean(values * values, axis=-1, keepdims=True) + norm_eps)
    copies[3].wait()
    sent_ref[:, :width] = (values * factor * gain_ref[...]).astype(jnp.bfloat16)
    copies[0].wait()
    copies[1].wait()
    row = lax.broadcasted_iota(jnp.int32, (rows, LANES), 0)
    lane = lax.broadcasted_iota(jnp.int32, (rows, LANES), 1)
    marks = jnp.zeros((rows, LANES), jnp.int32)
    for r in range(rows):
        slot = slot_ref[adapter_ref[r]]
        digit = jnp.where(lane == 0, slot // 32, jnp.where(lane == 1, slot % 32, 0))
        marks = jnp.where(row == r, digit, marks)
    sent_ref[:, width:] = marks.astype(jnp.float32).astype(jnp.bfloat16)


def norm_and_marks(hidden, gain, request_adapter, adapter_slot):
    rows, width = hidden.shape
    return pl.pallas_call(
        norm_kernel,
        in_specs=[pl.BlockSpec(memory_space=pl.ANY)] * 4,
        out_specs=whole_block((rows, width + LANES)),
        out_shape=jax.ShapeDtypeStruct((rows, width + LANES), jnp.bfloat16),
        scratch_shapes=[
            pltpu.VMEM(hidden.shape, jnp.bfloat16),
            pltpu.VMEM((1, width), jnp.float32),
            pltpu.SMEM(request_adapter.shape, jnp.int32),
            pltpu.SMEM(adapter_slot.shape, jnp.int32),
            pltpu.SemaphoreType.DMA((4,)),
        ],
        compiler_params=pltpu.CompilerParams(vmem_limit_bytes=NORM_VMEM),
        name="norm_and_marks",
    )(hidden, gain.reshape(1, width), request_adapter, adapter_slot)


def by_rank(factor):
    return factor.transpose(0, 2, 1).reshape(-1, factor.shape[1])


def permuted(block, offset):
    count = pool_size()
    return lax.ppermute(block, "pool", [(i, i ^ offset) for i in range(count)])


def in_order(upper, own, other, axis):
    return jnp.concatenate(
        [jnp.where(upper, other, own), jnp.where(upper, own, other)], axis=axis
    )


def scatter_chips(pair_sums, query_width):
    me = lax.axis_index("pool")
    chips, local, width = pair_sums.shape
    blocks = pair_sums.reshape(2, chips // 2, local, width)
    other = permuted(blocks[1], 2)
    own = blocks[0]
    query = own[..., :query_width] + other[..., :query_width]
    keyval = in_order((me & 2) != 0, own[..., query_width:], other[..., query_width:], -1)
    line = jnp.concatenate([query, keyval], axis=-1)
    parts = [line[0]] + [permuted(line[k], 4 * k) for k in (1, 2, 3)]
    query = sum(part[:, :query_width] for part in parts).astype(jnp.bfloat16)
    pieces = [part[:, query_width:].astype(jnp.bfloat16) for part in parts]
    low, high = (me & 4) != 0, (me & 8) != 0
    near = in_order(low, pieces[0], pieces[1], -1)
    far = in_order(low, pieces[2], pieces[3], -1)
    return query, in_order(high, near, far, -1)


def body(
    hidden,
    gain,
    query_weight,
    key_value_weight,
    output_weight,
    query_down_factor,
    query_up_factor,
    output_down_factor,
    output_up_factor,
    key_cache,
    value_cache,
    lengths,
    request_adapter,
    adapter_slot,
):
    count = pool_size()
    own_slots = query_down_factor.shape[0]
    local_rows = hidden.shape[0]
    col_width = query_weight.shape[1]

    aligned = (
        count == 16 and col_width % LANES == 0 and key_value_weight.shape[1] % LANES == 0
    )
    if aligned:
        sent = norm_and_marks(hidden, gain, request_adapter, adapter_slot)
    else:
        normalized_input = norm_rows(hidden, gain)
        slot_ids = lookup_slots(request_adapter, adapter_slot)
        digits = jnp.stack([slot_ids // 32, slot_ids % 32], axis=1).astype(jnp.bfloat16)
        sent = jnp.concatenate([normalized_input, jnp.pad(digits, ((0, 0), (0, 126)))], axis=1)
    first_slot = lax.axis_index("pool") * own_slots
    where = jnp.stack([lax.axis_index("pool"), first_slot]).astype(jnp.int32)
    if aligned:

        def bring_query(rows):
            now, _ = lax.optimization_barrier((where, rows))
            return bring(
                now,
                [query_weight],
            )

        gathered, (query_near,) = gather_rows(sent, bring_query)
    else:
        gathered = gather_rows(sent)
    gathered_rows = gathered[:, :MODEL_WIDTH]
    all_digits = gathered[:, MODEL_WIDTH : MODEL_WIDTH + 2].astype(jnp.int32)
    slot_ids = all_digits[:, 0] * 32 + all_digits[:, 1]
    request_total = gathered_rows.shape[0]

    owner_mask = (
        slot_ids[:, None] == first_slot + jnp.arange(own_slots, dtype=jnp.int32)[None, :]
    )
    bf_zero = jnp.zeros((), jnp.bfloat16)

    query_width = MODEL_WIDTH
    if aligned:
        kept, given = query_halves(
            where,
            gathered,
            query_near,
            key_value_weight,
            by_rank(query_down_factor),
            query_up_factor.reshape(own_slots * ADAPTER_RANK, -1),
            count,
            local_rows,
        )
        query_rows, keyval_rows = scatter_chips(kept + swap_cores(given), query_width)
    else:
        query_shrunk = owner_shrunk(gathered_rows, query_down_factor, owner_mask)
        lifted_rows = jnp.where(owner_mask[:, :, None], query_shrunk[:, None, :], bf_zero).reshape(
            request_total, own_slots * ADAPTER_RANK
        )
        query_delta = adapter_scale * jnp.dot(
            lifted_rows,
            query_up_factor.reshape(own_slots * ADAPTER_RANK, -1),
            preferred_element_type=jnp.float32,
        )
        kept_delta, given_delta = core_halves(query_delta)
        received_delta = swap_cores(given_delta)
        base = jnp.concatenate(
            [
                jnp.dot(gathered_rows, query_weight, preferred_element_type=jnp.float32),
                jnp.dot(gathered_rows, key_value_weight, preferred_element_type=jnp.float32),
            ],
            axis=1,
        )
        kept_base, given_base = core_halves(base)
        received_base = swap_cores(given_base)
        pair_query = pair_columns(kept_base[:, :, :col_width], received_base[:, :, :col_width])
        pair_keyval = pair_columns(kept_base[:, :, col_width:], received_base[:, :, col_width:])
        pair_delta = kept_delta + received_delta
        first_column = (lax.axis_index("pool") // 2) * (2 * col_width)
        there = lax.dynamic_slice_in_dim(pair_delta, first_column, 2 * col_width, 2)
        pair_delta = lax.dynamic_update_slice_in_dim(pair_delta, there + pair_query, first_column, 2)
        leaving = jnp.concatenate([pair_delta, pair_keyval], axis=2)
        arrived = exchange_chips(leaving)
        query_rows = jnp.sum(arrived[:, :, :query_width], axis=0).astype(jnp.bfloat16)
        keyval_rows = arrived[:, :, query_width:].astype(jnp.bfloat16)
        keyval_rows = keyval_rows.reshape(count // 2, local_rows, 2, -1)
        keyval_rows = keyval_rows.transpose(1, 0, 2, 3).reshape(local_rows, -1)

    attention_output = attend(query_rows, keyval_rows, key_cache, value_cache, lengths)
    if aligned:

        def bring_output(rows):
            now, _ = lax.optimization_barrier((where, rows))
            return bring(now, [output_weight])

        every_row, (output_near,) = gather_rows(attention_output, bring_output)
    else:
        every_row = gather_rows(attention_output)
    if aligned:
        kept, given = output_halves(
            where,
            every_row,
            gathered,
            output_near,
            by_rank(output_down_factor),
            output_up_factor.reshape(own_slots * ADAPTER_RANK, -1),
            count,
            local_rows,
        )
    else:
        out_width = output_weight.shape[0]
        columns = lax.dynamic_slice_in_dim(every_row, lax.axis_index("pool") * out_width, out_width, 1)
        output_shrunk = owner_shrunk(every_row, output_down_factor, owner_mask)
        lifted_rows = jnp.where(owner_mask[:, :, None], output_shrunk[:, None, :], bf_zero).reshape(
            request_total, own_slots * ADAPTER_RANK
        )
        up_rows = output_up_factor.reshape(own_slots * ADAPTER_RANK, MODEL_WIDTH)
        partial = jnp.dot(
            columns, output_weight, preferred_element_type=jnp.float32
        ) + adapter_scale * jnp.dot(lifted_rows, up_rows, preferred_element_type=jnp.float32)
        kept, given = core_halves(partial)
    pair_sums = (kept + swap_cores(given)).astype(jnp.bfloat16)
    arrived = exchange_chips(pair_sums).astype(jnp.float32)
    return jnp.sum(arrived, axis=0).astype(jnp.bfloat16)


def solution(mesh):
    placed = (
        P(("groups", "pool"), None),
        P(),
        P(None, "pool"),
        P(None, "pool"),
        P("pool", None),
        P(("groups", "pool"), None, None),
        P(("groups", "pool"), None, None),
        P(("groups", "pool"), None, None),
        P(("groups", "pool"), None, None),
        P(("groups", "pool"), None, None),
        P(("groups", "pool"), None, None),
        P(("groups", "pool")),
        P(("groups", "pool")),
        P("groups"),
    )
    return jax.shard_map(
        body, mesh=mesh, in_specs=placed, out_specs=P(("groups", "pool"), None), check_vma=False
    )
```

```python
import jax
import jax.numpy as jnp
from jax import lax
from jax.experimental import pallas as pl
from jax.experimental.pallas import tpu as pltpu
from jax.sharding import PartitionSpec as P

MODEL_WIDTH = 8192
H = 64
KVH = 8
HEAD_WIDTH = 128
ADAPTER_RANK = 16
CACHE = 512
DKV = 1024


adapter_scale = 0.5
norm_eps = 1e-05


def norm_rows(hidden, gain):
    values = hidden.astype(jnp.float32)
    factor = lax.rsqrt(jnp.mean(values * values, axis=-1, keepdims=True) + norm_eps)
    return (values * factor * gain).astype(jnp.bfloat16)


def lookup_slots(all_ids, adapter_slot):
    table_size = adapter_slot.shape[0]
    matches = all_ids[:, None] == jnp.arange(table_size, dtype=jnp.int32)[None, :]
    return jnp.sum(jnp.where(matches, adapter_slot[None, :], 0), axis=1)


def attend(query_rows, keyval_rows, key_cache, value_cache, lengths):
    group_size = H // KVH
    local_rows = query_rows.shape[0]
    heads_q = query_rows.reshape(local_rows, KVH, group_size, HEAD_WIDTH)
    new_keys = keyval_rows[:, :DKV].reshape(local_rows, KVH, HEAD_WIDTH)
    new_values = keyval_rows[:, DKV:].reshape(local_rows, KVH, HEAD_WIDTH)
    cached_keys = key_cache.reshape(local_rows, CACHE, KVH, HEAD_WIDTH)
    cached_values = value_cache.reshape(local_rows, CACHE, KVH, HEAD_WIDTH)
    factor = HEAD_WIDTH ** (-0.5)
    scores = (
        jnp.einsum("rkgd,rckd->rkgc", heads_q, cached_keys, preferred_element_type=jnp.float32)
        * factor
    )
    own_score = (
        jnp.einsum("rkgd,rkd->rkg", heads_q, new_keys, preferred_element_type=jnp.float32) * factor
    )
    in_cache = (jnp.arange(CACHE, dtype=jnp.int32)[None, :] < lengths[:, None])[:, None, None, :]
    scores = jnp.where(in_cache, scores, -1e30)
    highest = jnp.maximum(jnp.max(scores, axis=-1), own_score)
    cached_exp = jnp.where(in_cache, jnp.exp(scores - highest[..., None]), 0.0)
    own_exp = jnp.exp(own_score - highest)
    softmax_sum = jnp.sum(cached_exp, axis=-1) + own_exp
    cached_weight = (cached_exp / softmax_sum[..., None]).astype(jnp.bfloat16)
    own_weight = (own_exp / softmax_sum).astype(jnp.bfloat16)
    mixture = jnp.einsum(
        "rkgc,rckd->rkgd", cached_weight, cached_values, preferred_element_type=jnp.float32
    )
    mixture = (
        mixture
        + own_weight.astype(jnp.float32)[..., None] * new_values.astype(jnp.float32)[:, :, None, :]
    )
    return mixture.reshape(local_rows, KVH * group_size * HEAD_WIDTH).astype(jnp.bfloat16)


def owner_shrunk(rows, down_factor, owner_mask):
    partial = jnp.einsum("we,bey->wby", rows, down_factor, preferred_element_type=jnp.float32)
    return jnp.sum(jnp.where(owner_mask[:, :, None], partial, 0.0), axis=1).astype(jnp.bfloat16)


def pool_size():
    return lax.axis_size("pool")


def exchange_quads(rows, step):
    count = pool_size()
    me = lax.axis_index("pool")
    parts = [rows] + [
        lax.ppermute(rows, "pool", [(i, i ^ (k * step)) for i in range(count)]) for k in (1, 2, 3)
    ]
    low = (me & step) != 0
    high = (me & (2 * step)) != 0
    swapped = [
        jnp.where(low, parts[1], parts[0]),
        jnp.where(low, parts[0], parts[1]),
        jnp.where(low, parts[3], parts[2]),
        jnp.where(low, parts[2], parts[3]),
    ]
    return jnp.concatenate(
        [
            jnp.where(high, swapped[2], swapped[0]),
            jnp.where(high, swapped[3], swapped[1]),
            jnp.where(high, swapped[0], swapped[2]),
            jnp.where(high, swapped[1], swapped[3]),
        ],
        axis=0,
    )


def exchange_pair(rows, step):
    count = pool_size()
    upper = (lax.axis_index("pool") & step) != 0
    other = lax.ppermute(rows, "pool", [(i, i ^ step) for i in range(count)])
    return jnp.concatenate([jnp.where(upper, other, rows), jnp.where(upper, rows, other)], axis=0)


def gather_rows(rows, beside=None):
    count = pool_size()
    step = 4
    held = None if beside is None else beside(rows)
    while step < count:
        if step * 4 <= count:
            rows = exchange_quads(rows, step)
            step *= 4
        else:
            rows = exchange_pair(rows, step)
            step *= 2
    if held is not None:
        rows, held = lax.optimization_barrier((rows, held))
    fours = [[4 * k + j for j in range(4)] for k in range(count // 4)]
    rows = lax.all_gather(rows, "pool", axis=0, axis_index_groups=fours, tiled=True)
    return rows if beside is None else (rows, held)


def core_halves(partial):
    count = pool_size()
    width = partial.shape[-1]
    blocks = partial.reshape(2, 2, count // 4, -1, width)
    odd = (lax.axis_index("pool") & 1) != 0
    keep = jnp.where(odd, blocks[:, 1], blocks[:, 0])
    give = jnp.where(odd, blocks[:, 0], blocks[:, 1])
    return (
        keep.transpose(1, 0, 2, 3).reshape(count // 2, -1, width),
        give.transpose(1, 0, 2, 3).reshape(count // 2, -1, width),
    )


def swap_cores(block):
    count = pool_size()
    return lax.ppermute(block, "pool", [(i, i ^ 1) for i in range(count)])


def exchange_chips(blocks):
    count = pool_size()
    same_core = [[2 * k + c for k in range(count // 2)] for c in range(2)]
    return lax.all_to_all(blocks, "pool", 0, 0, tiled=True, axis_index_groups=same_core)


def pair_columns(kept, received):
    odd = (lax.axis_index("pool") & 1) != 0
    return jnp.concatenate(
        [jnp.where(odd, received, kept), jnp.where(odd, kept, received)], axis=-1
    )


CHUNKS = 8
NORM_VMEM = 57000 * 1024
LANES = 128
KERNEL_VMEM = 24 * 1024 * 1024
BRING_VMEM = 40 * 1024 * 1024


def whole_block(shape):
    return pl.BlockSpec(shape, lambda: (0,) * len(shape))


def own_lift(rows_ref, down_ref, marks_ref, first_slot):
    ranks = down_ref.shape[0]
    width = down_ref.shape[1]
    step = width // CHUNKS
    total = None
    for k in range(CHUNKS):
        part = lax.dot_general(
            rows_ref[:, k * step : (k + 1) * step],
            down_ref[:, k * step : (k + 1) * step],
            (((1,), (1,)), ((), ())),
            preferred_element_type=jnp.float32,
        )
        total = part if total is None else total + part
    marks = marks_ref[...].astype(jnp.float32)
    slots = (marks[:, 0:1] * 32.0 + marks[:, 1:2]).astype(jnp.int32)
    place = lax.broadcasted_iota(jnp.int32, total.shape, 1) // ADAPTER_RANK + first_slot
    return jnp.where(slots == place, total, 0.0).astype(jnp.bfloat16)


def split_store(values, odd, place, kept_ref, given_ref, first, add):
    width = values.shape[1]
    size = values.shape[0] // 4
    local = kept_ref.shape[1]
    spot = pl.ds(first, width)
    for y in range(2):
        even_rows = values[2 * y * size : (2 * y + 1) * size]
        odd_rows = values[(2 * y + 1) * size : (2 * y + 2) * size]
        kept = jnp.where(odd, odd_rows, even_rows)
        given = jnp.where(odd, even_rows, odd_rows)
        for z in range(size // local):
            k = place(z, y)
            kept_piece = kept[z * local : (z + 1) * local]
            given_piece = given[z * local : (z + 1) * local]
            if add:
                kept_piece = kept_piece + kept_ref[k, :, spot]
                given_piece = given_piece + given_ref[k, :, spot]
            kept_ref[k, :, spot] = kept_piece
            given_ref[k, :, spot] = given_piece


def relative_place(me, chips):
    def place(z, y):
        return jnp.bitwise_xor((me // 2) % 2, y) * (chips // 2) + jnp.bitwise_xor(me // 4, z)

    return place


def query_kernel(
    where_ref, rows_ref, marks_ref, query_vmem, keyval_vmem, down_vmem, up_vmem,
    kept_ref, given_ref,
):
    me = where_ref[0]
    odd = (me % 2) == 1
    place = relative_place(me, kept_ref.shape[0])
    width = down_vmem.shape[1]
    step = width // CHUNKS
    lifted = own_lift(rows_ref, down_vmem, marks_ref, where_ref[1])
    for k in range(CHUNKS):
        spot = slice(k * step, (k + 1) * step)
        delta = adapter_scale * jnp.dot(
            lifted, up_vmem[:, spot], preferred_element_type=jnp.float32
        )
        split_store(delta, odd, place, kept_ref, given_ref, k * step, False)
    query = None
    for k in range(CHUNKS):
        spot = slice(k * step, (k + 1) * step)
        part = jnp.dot(rows_ref[:, spot], query_vmem[spot], preferred_element_type=jnp.float32)
        query = part if query is None else query + part
    columns = query.shape[1]
    split_store(
        query, odd, place, kept_ref, given_ref, pl.multiple_of(me * columns, LANES), True
    )
    keyval = None
    for k in range(CHUNKS):
        spot = slice(k * step, (k + 1) * step)
        part = jnp.dot(rows_ref[:, spot], keyval_vmem[spot], preferred_element_type=jnp.float32)
        keyval = part if keyval is None else keyval + part
    none = jnp.zeros_like(keyval)
    both = jnp.concatenate([jnp.where(odd, none, keyval), jnp.where(odd, keyval, none)], axis=1)
    split_store(both, odd, place, kept_ref, given_ref, width, False)


def query_halves(where, gathered, query_weight, key_value_weight, down, up, count, local_rows):
    rows = gathered.shape[0]
    width, columns = query_weight.shape
    keyval_columns = key_value_weight.shape[1]
    ranks = down.shape[0]
    sent = jax.ShapeDtypeStruct(
        (count // 2, local_rows, width + 2 * keyval_columns), jnp.float32
    )
    return pl.pallas_call(
        query_kernel,
        in_specs=[
            pl.BlockSpec(memory_space=pltpu.SMEM),
            whole_block((rows, width)),
            whole_block((rows, LANES)),
        ]
        + [pl.BlockSpec(memory_space=pltpu.VMEM)] * 4,
        out_specs=[whole_block(sent.shape)] * 2,
        out_shape=[sent, sent],
        compiler_params=pltpu.CompilerParams(vmem_limit_bytes=KERNEL_VMEM),
        name="query_halves",
    )(where, gathered[:, :width], gathered[:, width:], query_weight, key_value_weight, down, up)


def output_kernel(
    where_ref, rows_ref, marks_ref, output_vmem, down_vmem, up_vmem, kept_ref, given_ref
):
    me = where_ref[0]
    odd = (me % 2) == 1
    place = relative_place(me, kept_ref.shape[0])
    depth, width = output_vmem.shape
    step = width // CHUNKS
    lifted = own_lift(rows_ref, down_vmem, marks_ref, where_ref[1])
    columns = rows_ref[:, pl.ds(pl.multiple_of(me * depth, LANES), depth)]
    for k in range(CHUNKS):
        spot = slice(k * step, (k + 1) * step)
        part = jnp.dot(columns, output_vmem[:, spot], preferred_element_type=jnp.float32)
        part = part + adapter_scale * jnp.dot(
            lifted, up_vmem[:, spot], preferred_element_type=jnp.float32
        )
        split_store(part, odd, place, kept_ref, given_ref, k * step, False)


def output_halves(where, every_row, gathered, output_weight, down, up, count, local_rows):
    rows = every_row.shape[0]
    depth, width = output_weight.shape
    ranks = down.shape[0]
    sent = jax.ShapeDtypeStruct((count // 2, local_rows, width), jnp.float32)
    return pl.pallas_call(
        output_kernel,
        in_specs=[
            pl.BlockSpec(memory_space=pltpu.SMEM),
            whole_block((rows, width)),
            whole_block((rows, LANES)),
        ]
        + [pl.BlockSpec(memory_space=pltpu.VMEM)] * 3,
        out_specs=[whole_block(sent.shape)] * 2,
        out_shape=[sent, sent],
        compiler_params=pltpu.CompilerParams(vmem_limit_bytes=KERNEL_VMEM),
        name="output_halves",
    )(where, every_row, gathered[:, width:], output_weight, down, up)


def bring_kernel(*refs):
    count = (len(refs) - 2) // 2
    sources, targets, sems = refs[1 : count + 1], refs[count + 1 : -1], refs[-1]
    copies = []
    for source, target in zip(sources, targets):
        step = source.shape[0] // 4
        for k in range(4):
            spot = pl.ds(k * step, step)
            copies.append(
                pltpu.make_async_copy(source.at[spot], target.at[spot], sems.at[len(copies)])
            )
    for copy in copies:
        copy.start()
    for copy in copies:
        copy.wait()


def bring(where, arrays):
    size = sum(2 * array.size for array in arrays)
    return pl.pallas_call(
        bring_kernel,
        in_specs=[pl.BlockSpec(memory_space=pltpu.SMEM)]
        + [pl.BlockSpec(memory_space=pl.ANY)] * len(arrays),
        out_specs=[pl.BlockSpec(memory_space=pltpu.VMEM)] * len(arrays),
        out_shape=[jax.ShapeDtypeStruct(array.shape, array.dtype) for array in arrays],
        scratch_shapes=[pltpu.SemaphoreType.DMA((4 * len(arrays),))],
        compiler_params=pltpu.CompilerParams(vmem_limit_bytes=BRING_VMEM),
        cost_estimate=pl.CostEstimate(flops=0, bytes_accessed=2 * size, transcendentals=0),
        name="bring",
    )(where, *arrays)


def norm_kernel(
    hidden_hbm, gain_hbm, adapter_hbm, slot_hbm,
    sent_ref, hidden_ref, gain_ref, adapter_ref, slot_ref, sems,
):
    copies = [
        pltpu.make_async_copy(source, target, sems.at[k])
        for k, (source, target) in enumerate(
            (
                (adapter_hbm, adapter_ref),
                (slot_hbm, slot_ref),
                (hidden_hbm, hidden_ref),
                (gain_hbm, gain_ref),
            )
        )
    ]
    for copy in copies:
        copy.start()
    rows, width = hidden_ref.shape
    copies[2].wait()
    values = hidden_ref[...].astype(jnp.float32)
    factor = lax.rsqrt(jnp.mean(values * values, axis=-1, keepdims=True) + norm_eps)
    copies[3].wait()
    sent_ref[:, :width] = (values * factor * gain_ref[...]).astype(jnp.bfloat16)
    copies[0].wait()
    copies[1].wait()
    row = lax.broadcasted_iota(jnp.int32, (rows, LANES), 0)
    lane = lax.broadcasted_iota(jnp.int32, (rows, LANES), 1)
    marks = jnp.zeros((rows, LANES), jnp.int32)
    for r in range(rows):
        slot = slot_ref[adapter_ref[r]]
        digit = jnp.where(lane == 0, slot // 32, jnp.where(lane == 1, slot % 32, 0))
        marks = jnp.where(row == r, digit, marks)
    sent_ref[:, width:] = marks.astype(jnp.float32).astype(jnp.bfloat16)


def norm_and_marks(hidden, gain, request_adapter, adapter_slot):
    rows, width = hidden.shape
    return pl.pallas_call(
        norm_kernel,
        in_specs=[pl.BlockSpec(memory_space=pl.ANY)] * 4,
        out_specs=whole_block((rows, width + LANES)),
        out_shape=jax.ShapeDtypeStruct((rows, width + LANES), jnp.bfloat16),
        scratch_shapes=[
            pltpu.VMEM(hidden.shape, jnp.bfloat16),
            pltpu.VMEM((1, width), jnp.float32),
            pltpu.SMEM(request_adapter.shape, jnp.int32),
            pltpu.SMEM(adapter_slot.shape, jnp.int32),
            pltpu.SemaphoreType.DMA((4,)),
        ],
        compiler_params=pltpu.CompilerParams(vmem_limit_bytes=NORM_VMEM),
        name="norm_and_marks",
    )(hidden, gain.reshape(1, width), request_adapter, adapter_slot)


def by_rank(factor):
    return factor.transpose(0, 2, 1).reshape(-1, factor.shape[1])


def permuted(block, offset):
    count = pool_size()
    return lax.ppermute(block, "pool", [(i, i ^ offset) for i in range(count)])


def in_order(upper, own, other, axis):
    return jnp.concatenate(
        [jnp.where(upper, other, own), jnp.where(upper, own, other)], axis=axis
    )


def scatter_chips(pair_sums, query_width):
    me = lax.axis_index("pool")
    chips, local, width = pair_sums.shape
    blocks = pair_sums.reshape(2, chips // 2, local, width)
    other = permuted(blocks[1], 2)
    own = blocks[0]
    query = own[..., :query_width] + other[..., :query_width]
    keyval = in_order((me & 2) != 0, own[..., query_width:], other[..., query_width:], -1)
    line = jnp.concatenate([query, keyval], axis=-1)
    parts = [line[0]] + [permuted(line[k], 4 * k) for k in (1, 2, 3)]
    query = sum(part[:, :query_width] for part in parts).astype(jnp.bfloat16)
    pieces = [part[:, query_width:].astype(jnp.bfloat16) for part in parts]
    low, high = (me & 4) != 0, (me & 8) != 0
    near = in_order(low, pieces[0], pieces[1], -1)
    far = in_order(low, pieces[2], pieces[3], -1)
    return query, in_order(high, near, far, -1)


def scatter_output(pair_sums):
    chips, local, width = pair_sums.shape
    blocks = pair_sums.reshape(2, chips // 2, local, width)
    line = blocks[0] + permuted(blocks[1], 2)
    return line[0] + sum(permuted(line[k], 4 * k) for k in (1, 2, 3))


def body(
    hidden,
    gain,
    query_weight,
    key_value_weight,
    output_weight,
    query_down_factor,
    query_up_factor,
    output_down_factor,
    output_up_factor,
    key_cache,
    value_cache,
    lengths,
    request_adapter,
    adapter_slot,
):
    count = pool_size()
    own_slots = query_down_factor.shape[0]
    local_rows = hidden.shape[0]
    col_width = query_weight.shape[1]

    aligned = (
        count == 16 and col_width % LANES == 0 and key_value_weight.shape[1] % LANES == 0
    )
    if aligned:
        sent = norm_and_marks(hidden, gain, request_adapter, adapter_slot)
    else:
        normalized_input = norm_rows(hidden, gain)
        slot_ids = lookup_slots(request_adapter, adapter_slot)
        digits = jnp.stack([slot_ids // 32, slot_ids % 32], axis=1).astype(jnp.bfloat16)
        sent = jnp.concatenate([normalized_input, jnp.pad(digits, ((0, 0), (0, 126)))], axis=1)
    first_slot = lax.axis_index("pool") * own_slots
    where = jnp.stack([lax.axis_index("pool"), first_slot]).astype(jnp.int32)
    if aligned:

        def bring_query(rows):
            now, _ = lax.optimization_barrier((where, rows))
            return bring(
                now,
                [query_weight],
            )

        gathered, (query_near,) = gather_rows(sent, bring_query)
    else:
        gathered = gather_rows(sent)
    gathered_rows = gathered[:, :MODEL_WIDTH]
    all_digits = gathered[:, MODEL_WIDTH : MODEL_WIDTH + 2].astype(jnp.int32)
    slot_ids = all_digits[:, 0] * 32 + all_digits[:, 1]
    request_total = gathered_rows.shape[0]

    owner_mask = (
        slot_ids[:, None] == first_slot + jnp.arange(own_slots, dtype=jnp.int32)[None, :]
    )
    bf_zero = jnp.zeros((), jnp.bfloat16)

    query_width = MODEL_WIDTH
    if aligned:
        kept, given = query_halves(
            where,
            gathered,
            query_near,
            key_value_weight,
            by_rank(query_down_factor),
            query_up_factor.reshape(own_slots * ADAPTER_RANK, -1),
            count,
            local_rows,
        )
        query_rows, keyval_rows = scatter_chips(kept + swap_cores(given), query_width)
    else:
        query_shrunk = owner_shrunk(gathered_rows, query_down_factor, owner_mask)
        lifted_rows = jnp.where(owner_mask[:, :, None], query_shrunk[:, None, :], bf_zero).reshape(
            request_total, own_slots * ADAPTER_RANK
        )
        query_delta = adapter_scale * jnp.dot(
            lifted_rows,
            query_up_factor.reshape(own_slots * ADAPTER_RANK, -1),
            preferred_element_type=jnp.float32,
        )
        kept_delta, given_delta = core_halves(query_delta)
        received_delta = swap_cores(given_delta)
        base = jnp.concatenate(
            [
                jnp.dot(gathered_rows, query_weight, preferred_element_type=jnp.float32),
                jnp.dot(gathered_rows, key_value_weight, preferred_element_type=jnp.float32),
            ],
            axis=1,
        )
        kept_base, given_base = core_halves(base)
        received_base = swap_cores(given_base)
        pair_query = pair_columns(kept_base[:, :, :col_width], received_base[:, :, :col_width])
        pair_keyval = pair_columns(kept_base[:, :, col_width:], received_base[:, :, col_width:])
        pair_delta = kept_delta + received_delta
        first_column = (lax.axis_index("pool") // 2) * (2 * col_width)
        there = lax.dynamic_slice_in_dim(pair_delta, first_column, 2 * col_width, 2)
        pair_delta = lax.dynamic_update_slice_in_dim(pair_delta, there + pair_query, first_column, 2)
        leaving = jnp.concatenate([pair_delta, pair_keyval], axis=2)
        arrived = exchange_chips(leaving)
        query_rows = jnp.sum(arrived[:, :, :query_width], axis=0).astype(jnp.bfloat16)
        keyval_rows = arrived[:, :, query_width:].astype(jnp.bfloat16)
        keyval_rows = keyval_rows.reshape(count // 2, local_rows, 2, -1)
        keyval_rows = keyval_rows.transpose(1, 0, 2, 3).reshape(local_rows, -1)

    attention_output = attend(query_rows, keyval_rows, key_cache, value_cache, lengths)
    if aligned:

        def bring_output(rows):
            now, _ = lax.optimization_barrier((where, rows))
            return bring(now, [output_weight])

        every_row, (output_near,) = gather_rows(attention_output, bring_output)
    else:
        every_row = gather_rows(attention_output)
    if aligned:
        kept, given = output_halves(
            where,
            every_row,
            gathered,
            output_near,
            by_rank(output_down_factor),
            output_up_factor.reshape(own_slots * ADAPTER_RANK, -1),
            count,
            local_rows,
        )
    else:
        out_width = output_weight.shape[0]
        columns = lax.dynamic_slice_in_dim(every_row, lax.axis_index("pool") * out_width, out_width, 1)
        output_shrunk = owner_shrunk(every_row, output_down_factor, owner_mask)
        lifted_rows = jnp.where(owner_mask[:, :, None], output_shrunk[:, None, :], bf_zero).reshape(
            request_total, own_slots * ADAPTER_RANK
        )
        up_rows = output_up_factor.reshape(own_slots * ADAPTER_RANK, MODEL_WIDTH)
        partial = jnp.dot(
            columns, output_weight, preferred_element_type=jnp.float32
        ) + adapter_scale * jnp.dot(lifted_rows, up_rows, preferred_element_type=jnp.float32)
        kept, given = core_halves(partial)
    if aligned:
        return scatter_output(kept + swap_cores(given)).astype(jnp.bfloat16)
    arrived = exchange_chips(kept + swap_cores(given))
    return jnp.sum(arrived, axis=0).astype(jnp.bfloat16)


def solution(mesh):
    placed = (
        P(("groups", "pool"), None),
        P(),
        P(None, "pool"),
        P(None, "pool"),
        P("pool", None),
        P(("groups", "pool"), None, None),
        P(("groups", "pool"), None, None),
        P(("groups", "pool"), None, None),
        P(("groups", "pool"), None, None),
        P(("groups", "pool"), None, None),
        P(("groups", "pool"), None, None),
        P(("groups", "pool")),
        P(("groups", "pool")),
        P("groups"),
    )
    return jax.shard_map(
        body, mesh=mesh, in_specs=placed, out_specs=P(("groups", "pool"), None), check_vma=False
    )
```

```python
import jax
import jax.numpy as jnp
from jax import lax
from jax.experimental import pallas as pl
from jax.experimental.pallas import tpu as pltpu
from jax.sharding import PartitionSpec as P

MODEL_WIDTH = 8192
H = 64
KVH = 8
HEAD_WIDTH = 128
ADAPTER_RANK = 16
CACHE = 512
DKV = 1024


adapter_scale = 0.5
norm_eps = 1e-05


def norm_rows(hidden, gain):
    values = hidden.astype(jnp.float32)
    factor = lax.rsqrt(jnp.mean(values * values, axis=-1, keepdims=True) + norm_eps)
    return (values * factor * gain).astype(jnp.bfloat16)


def lookup_slots(all_ids, adapter_slot):
    table_size = adapter_slot.shape[0]
    matches = all_ids[:, None] == jnp.arange(table_size, dtype=jnp.int32)[None, :]
    return jnp.sum(jnp.where(matches, adapter_slot[None, :], 0), axis=1)


def attend(query_rows, keyval_rows, key_cache, value_cache, lengths):
    group_size = H // KVH
    local_rows = query_rows.shape[0]
    heads_q = query_rows.reshape(local_rows, KVH, group_size, HEAD_WIDTH)
    new_keys = keyval_rows[:, :DKV].reshape(local_rows, KVH, HEAD_WIDTH)
    new_values = keyval_rows[:, DKV:].reshape(local_rows, KVH, HEAD_WIDTH)
    cached_keys = key_cache.reshape(local_rows, CACHE, KVH, HEAD_WIDTH)
    cached_values = value_cache.reshape(local_rows, CACHE, KVH, HEAD_WIDTH)
    factor = HEAD_WIDTH ** (-0.5)
    scores = (
        jnp.einsum("rkgd,rckd->rkgc", heads_q, cached_keys, preferred_element_type=jnp.float32)
        * factor
    )
    own_score = (
        jnp.einsum("rkgd,rkd->rkg", heads_q, new_keys, preferred_element_type=jnp.float32) * factor
    )
    in_cache = (jnp.arange(CACHE, dtype=jnp.int32)[None, :] < lengths[:, None])[:, None, None, :]
    scores = jnp.where(in_cache, scores, -1e30)
    highest = jnp.maximum(jnp.max(scores, axis=-1), own_score)
    cached_exp = jnp.where(in_cache, jnp.exp(scores - highest[..., None]), 0.0)
    own_exp = jnp.exp(own_score - highest)
    softmax_sum = jnp.sum(cached_exp, axis=-1) + own_exp
    cached_weight = (cached_exp / softmax_sum[..., None]).astype(jnp.bfloat16)
    own_weight = (own_exp / softmax_sum).astype(jnp.bfloat16)
    mixture = jnp.einsum(
        "rkgc,rckd->rkgd", cached_weight, cached_values, preferred_element_type=jnp.float32
    )
    mixture = (
        mixture
        + own_weight.astype(jnp.float32)[..., None] * new_values.astype(jnp.float32)[:, :, None, :]
    )
    return mixture.reshape(local_rows, KVH * group_size * HEAD_WIDTH).astype(jnp.bfloat16)


def owner_shrunk(rows, down_factor, owner_mask):
    partial = jnp.einsum("we,bey->wby", rows, down_factor, preferred_element_type=jnp.float32)
    return jnp.sum(jnp.where(owner_mask[:, :, None], partial, 0.0), axis=1).astype(jnp.bfloat16)


def pool_size():
    return lax.axis_size("pool")


def exchange_quads(rows, step):
    count = pool_size()
    me = lax.axis_index("pool")
    parts = [rows] + [
        lax.ppermute(rows, "pool", [(i, i ^ (k * step)) for i in range(count)]) for k in (1, 2, 3)
    ]
    low = (me & step) != 0
    high = (me & (2 * step)) != 0
    swapped = [
        jnp.where(low, parts[1], parts[0]),
        jnp.where(low, parts[0], parts[1]),
        jnp.where(low, parts[3], parts[2]),
        jnp.where(low, parts[2], parts[3]),
    ]
    return jnp.concatenate(
        [
            jnp.where(high, swapped[2], swapped[0]),
            jnp.where(high, swapped[3], swapped[1]),
            jnp.where(high, swapped[0], swapped[2]),
            jnp.where(high, swapped[1], swapped[3]),
        ],
        axis=0,
    )


def exchange_pair(rows, step):
    count = pool_size()
    upper = (lax.axis_index("pool") & step) != 0
    other = lax.ppermute(rows, "pool", [(i, i ^ step) for i in range(count)])
    return jnp.concatenate([jnp.where(upper, other, rows), jnp.where(upper, rows, other)], axis=0)


def gather_rows(rows, beside=None):
    count = pool_size()
    step = 4
    held = None if beside is None else beside(rows)
    while step < count:
        if beside is not None:
            rows = jnp.concatenate([rows] + [permuted(rows, k * step) for k in (1, 2, 3)], axis=0)
            step *= 4
        elif step * 4 <= count:
            rows = exchange_quads(rows, step)
            step *= 4
        else:
            rows = exchange_pair(rows, step)
            step *= 2
    if held is not None:
        rows, held = lax.optimization_barrier((rows, held))
    fours = [[4 * k + j for j in range(4)] for k in range(count // 4)]
    rows = lax.all_gather(rows, "pool", axis=0, axis_index_groups=fours, tiled=True)
    return rows if beside is None else (rows, held)


def core_halves(partial):
    count = pool_size()
    width = partial.shape[-1]
    blocks = partial.reshape(2, 2, count // 4, -1, width)
    odd = (lax.axis_index("pool") & 1) != 0
    keep = jnp.where(odd, blocks[:, 1], blocks[:, 0])
    give = jnp.where(odd, blocks[:, 0], blocks[:, 1])
    return (
        keep.transpose(1, 0, 2, 3).reshape(count // 2, -1, width),
        give.transpose(1, 0, 2, 3).reshape(count // 2, -1, width),
    )


def swap_cores(block):
    count = pool_size()
    return lax.ppermute(block, "pool", [(i, i ^ 1) for i in range(count)])


def exchange_chips(blocks):
    count = pool_size()
    same_core = [[2 * k + c for k in range(count // 2)] for c in range(2)]
    return lax.all_to_all(blocks, "pool", 0, 0, tiled=True, axis_index_groups=same_core)


def pair_columns(kept, received):
    odd = (lax.axis_index("pool") & 1) != 0
    return jnp.concatenate(
        [jnp.where(odd, received, kept), jnp.where(odd, kept, received)], axis=-1
    )


CHUNKS = 8
NORM_VMEM = 57000 * 1024
LANES = 128
KERNEL_VMEM = 24 * 1024 * 1024
BRING_VMEM = 40 * 1024 * 1024


def whole_block(shape):
    return pl.BlockSpec(shape, lambda: (0,) * len(shape))


def own_lift(rows_ref, down_ref, marks_ref, first_slot):
    ranks = down_ref.shape[0]
    width = down_ref.shape[1]
    step = width // CHUNKS
    total = None
    for k in range(CHUNKS):
        part = lax.dot_general(
            rows_ref[:, k * step : (k + 1) * step],
            down_ref[:, k * step : (k + 1) * step],
            (((1,), (1,)), ((), ())),
            preferred_element_type=jnp.float32,
        )
        total = part if total is None else total + part
    marks = marks_ref[...].astype(jnp.float32)
    slots = (marks[:, 0:1] * 32.0 + marks[:, 1:2]).astype(jnp.int32)
    place = lax.broadcasted_iota(jnp.int32, total.shape, 1) // ADAPTER_RANK + first_slot
    return jnp.where(slots == place, total, 0.0).astype(jnp.bfloat16)


def split_store(values, odd, place, kept_ref, given_ref, first, add):
    width = values.shape[1]
    size = values.shape[0] // 4
    local = kept_ref.shape[1]
    spot = pl.ds(first, width)
    for y in range(2):
        even_rows = values[2 * y * size : (2 * y + 1) * size]
        odd_rows = values[(2 * y + 1) * size : (2 * y + 2) * size]
        kept = jnp.where(odd, odd_rows, even_rows)
        given = jnp.where(odd, even_rows, odd_rows)
        for z in range(size // local):
            k = place(z, y)
            kept_piece = kept[z * local : (z + 1) * local]
            given_piece = given[z * local : (z + 1) * local]
            if add:
                kept_piece = kept_piece + kept_ref[k, :, spot]
                given_piece = given_piece + given_ref[k, :, spot]
            kept_ref[k, :, spot] = kept_piece
            given_ref[k, :, spot] = given_piece


def query_kernel(
    where_ref, rows_ref, marks_ref, query_vmem, keyval_vmem, down_vmem, up_vmem,
    kept_ref, given_ref,
):
    me = where_ref[0]
    odd = (me % 2) == 1
    far = kept_ref.shape[0] // 2

    def place(z, y):
        return jnp.bitwise_xor((me // 2) % 2, y) * far + z

    width = down_vmem.shape[1]
    step = width // CHUNKS
    lifted = own_lift(rows_ref, down_vmem, marks_ref, where_ref[1])
    for k in range(CHUNKS):
        spot = slice(k * step, (k + 1) * step)
        delta = adapter_scale * jnp.dot(
            lifted, up_vmem[:, spot], preferred_element_type=jnp.float32
        )
        split_store(delta, odd, place, kept_ref, given_ref, k * step, False)
    query = None
    for k in range(CHUNKS):
        spot = slice(k * step, (k + 1) * step)
        part = jnp.dot(rows_ref[:, spot], query_vmem[spot], preferred_element_type=jnp.float32)
        query = part if query is None else query + part
    columns = query.shape[1]
    split_store(
        query, odd, place, kept_ref, given_ref, pl.multiple_of(me * columns, LANES), True
    )
    keyval = None
    for k in range(CHUNKS):
        spot = slice(k * step, (k + 1) * step)
        part = jnp.dot(rows_ref[:, spot], keyval_vmem[spot], preferred_element_type=jnp.float32)
        keyval = part if keyval is None else keyval + part
    none = jnp.zeros_like(keyval)
    both = jnp.concatenate([jnp.where(odd, none, keyval), jnp.where(odd, keyval, none)], axis=1)
    split_store(both, odd, place, kept_ref, given_ref, width, False)


def query_halves(where, gathered, query_weight, key_value_weight, down, up, count, local_rows):
    rows = gathered.shape[0]
    width, columns = query_weight.shape
    keyval_columns = key_value_weight.shape[1]
    ranks = down.shape[0]
    sent = jax.ShapeDtypeStruct(
        (count // 2, local_rows, width + 2 * keyval_columns), jnp.float32
    )
    return pl.pallas_call(
        query_kernel,
        in_specs=[
            pl.BlockSpec(memory_space=pltpu.SMEM),
            whole_block((rows, width)),
            whole_block((rows, LANES)),
        ]
        + [pl.BlockSpec(memory_space=pltpu.VMEM)] * 4,
        out_specs=[whole_block(sent.shape)] * 2,
        out_shape=[sent, sent],
        compiler_params=pltpu.CompilerParams(vmem_limit_bytes=KERNEL_VMEM),
        name="query_halves",
    )(where, gathered[:, :width], gathered[:, width:], query_weight, key_value_weight, down, up)


def output_kernel(
    where_ref, rows_ref, marks_ref, output_vmem, down_vmem, up_vmem, kept_ref, given_ref
):
    me = where_ref[0]
    odd = (me % 2) == 1

    def place(z, y):
        return 2 * jnp.bitwise_xor(me // 4, z) + y

    depth, width = output_vmem.shape
    step = width // CHUNKS
    lifted = own_lift(rows_ref, down_vmem, marks_ref, where_ref[1])
    columns = rows_ref[:, pl.ds(pl.multiple_of(me * depth, LANES), depth)]
    for k in range(CHUNKS):
        spot = slice(k * step, (k + 1) * step)
        part = jnp.dot(columns, output_vmem[:, spot], preferred_element_type=jnp.float32)
        part = part + adapter_scale * jnp.dot(
            lifted, up_vmem[:, spot], preferred_element_type=jnp.float32
        )
        split_store(part, odd, place, kept_ref, given_ref, k * step, False)


def output_halves(where, every_row, gathered, output_weight, down, up, count, local_rows):
    rows = every_row.shape[0]
    depth, width = output_weight.shape
    ranks = down.shape[0]
    sent = jax.ShapeDtypeStruct((count // 2, local_rows, width), jnp.float32)
    return pl.pallas_call(
        output_kernel,
        in_specs=[
            pl.BlockSpec(memory_space=pltpu.SMEM),
            whole_block((rows, width)),
            whole_block((rows, LANES)),
        ]
        + [pl.BlockSpec(memory_space=pltpu.VMEM)] * 3,
        out_specs=[whole_block(sent.shape)] * 2,
        out_shape=[sent, sent],
        compiler_params=pltpu.CompilerParams(vmem_limit_bytes=KERNEL_VMEM),
        name="output_halves",
    )(where, every_row, gathered[:, width:], output_weight, down, up)


def bring_kernel(*refs):
    count = (len(refs) - 2) // 2
    sources, targets, sems = refs[1 : count + 1], refs[count + 1 : -1], refs[-1]
    copies = []
    for source, target in zip(sources, targets):
        step = source.shape[0] // 4
        for k in range(4):
            spot = pl.ds(k * step, step)
            copies.append(
                pltpu.make_async_copy(source.at[spot], target.at[spot], sems.at[len(copies)])
            )
    for copy in copies:
        copy.start()
    for copy in copies:
        copy.wait()


def bring(where, arrays):
    size = sum(2 * array.size for array in arrays)
    return pl.pallas_call(
        bring_kernel,
        in_specs=[pl.BlockSpec(memory_space=pltpu.SMEM)]
        + [pl.BlockSpec(memory_space=pl.ANY)] * len(arrays),
        out_specs=[pl.BlockSpec(memory_space=pltpu.VMEM)] * len(arrays),
        out_shape=[jax.ShapeDtypeStruct(array.shape, array.dtype) for array in arrays],
        scratch_shapes=[pltpu.SemaphoreType.DMA((4 * len(arrays),))],
        compiler_params=pltpu.CompilerParams(vmem_limit_bytes=BRING_VMEM),
        cost_estimate=pl.CostEstimate(flops=0, bytes_accessed=2 * size, transcendentals=0),
        name="bring",
    )(where, *arrays)


def norm_kernel(
    hidden_hbm, gain_hbm, adapter_hbm, slot_hbm,
    sent_ref, hidden_ref, gain_ref, adapter_ref, slot_ref, sems,
):
    copies = [
        pltpu.make_async_copy(source, target, sems.at[k])
        for k, (source, target) in enumerate(
            (
                (adapter_hbm, adapter_ref),
                (slot_hbm, slot_ref),
                (hidden_hbm, hidden_ref),
                (gain_hbm, gain_ref),
            )
        )
    ]
    for copy in copies:
        copy.start()
    rows, width = hidden_ref.shape
    copies[2].wait()
    values = hidden_ref[...].astype(jnp.float32)
    factor = lax.rsqrt(jnp.mean(values * values, axis=-1, keepdims=True) + norm_eps)
    copies[3].wait()
    sent_ref[:, :width] = (values * factor * gain_ref[...]).astype(jnp.bfloat16)
    copies[0].wait()
    copies[1].wait()
    row = lax.broadcasted_iota(jnp.int32, (rows, LANES), 0)
    lane = lax.broadcasted_iota(jnp.int32, (rows, LANES), 1)
    marks = jnp.zeros((rows, LANES), jnp.int32)
    for r in range(rows):
        slot = slot_ref[adapter_ref[r]]
        digit = jnp.where(lane == 0, slot // 32, jnp.where(lane == 1, slot % 32, 0))
        marks = jnp.where(row == r, digit, marks)
    sent_ref[:, width:] = marks.astype(jnp.float32).astype(jnp.bfloat16)


def norm_and_marks(hidden, gain, request_adapter, adapter_slot):
    rows, width = hidden.shape
    return pl.pallas_call(
        norm_kernel,
        in_specs=[pl.BlockSpec(memory_space=pl.ANY)] * 4,
        out_specs=whole_block((rows, width + LANES)),
        out_shape=jax.ShapeDtypeStruct((rows, width + LANES), jnp.bfloat16),
        scratch_shapes=[
            pltpu.VMEM(hidden.shape, jnp.bfloat16),
            pltpu.VMEM((1, width), jnp.float32),
            pltpu.SMEM(request_adapter.shape, jnp.int32),
            pltpu.SMEM(adapter_slot.shape, jnp.int32),
            pltpu.SemaphoreType.DMA((4,)),
        ],
        compiler_params=pltpu.CompilerParams(vmem_limit_bytes=NORM_VMEM),
        name="norm_and_marks",
    )(hidden, gain.reshape(1, width), request_adapter, adapter_slot)


def by_rank(factor):
    return factor.transpose(0, 2, 1).reshape(-1, factor.shape[1])


def permuted(block, offset):
    count = pool_size()
    return lax.ppermute(block, "pool", [(i, i ^ offset) for i in range(count)])


def in_order(upper, own, other, axis):
    return jnp.concatenate(
        [jnp.where(upper, other, own), jnp.where(upper, own, other)], axis=axis
    )


def scatter_chips(pair_sums, query_width):
    me = lax.axis_index("pool")
    chips, local, width = pair_sums.shape
    blocks = pair_sums.reshape(2, chips // 2, local, width)
    other = permuted(blocks[1], 2)
    own = blocks[0]
    query = own[..., :query_width] + other[..., :query_width]
    keyval = in_order((me & 2) != 0, own[..., query_width:], other[..., query_width:], -1)
    line = jnp.concatenate([query, keyval], axis=-1)
    parts = [line[0]] + [permuted(line[k], 4 * k) for k in (1, 2, 3)]
    query = sum(part[:, :query_width] for part in parts).astype(jnp.bfloat16)
    pieces = [part[:, query_width:].astype(jnp.bfloat16) for part in parts]
    low, high = (me & 4) != 0, (me & 8) != 0
    near = in_order(low, pieces[0], pieces[1], -1)
    far = in_order(low, pieces[2], pieces[3], -1)
    return query, in_order(high, near, far, -1)


def body(
    hidden,
    gain,
    query_weight,
    key_value_weight,
    output_weight,
    query_down_factor,
    query_up_factor,
    output_down_factor,
    output_up_factor,
    key_cache,
    value_cache,
    lengths,
    request_adapter,
    adapter_slot,
):
    count = pool_size()
    own_slots = query_down_factor.shape[0]
    local_rows = hidden.shape[0]
    col_width = query_weight.shape[1]

    aligned = (
        count == 16 and col_width % LANES == 0 and key_value_weight.shape[1] % LANES == 0
    )
    if aligned:
        sent = norm_and_marks(hidden, gain, request_adapter, adapter_slot)
    else:
        normalized_input = norm_rows(hidden, gain)
        slot_ids = lookup_slots(request_adapter, adapter_slot)
        digits = jnp.stack([slot_ids // 32, slot_ids % 32], axis=1).astype(jnp.bfloat16)
        sent = jnp.concatenate([normalized_input, jnp.pad(digits, ((0, 0), (0, 126)))], axis=1)
    first_slot = lax.axis_index("pool") * own_slots
    where = jnp.stack([lax.axis_index("pool"), first_slot]).astype(jnp.int32)
    if aligned:

        def bring_query(rows):
            now, _ = lax.optimization_barrier((where, rows))
            return bring(
                now,
                [query_weight],
            )

        gathered, (query_near,) = gather_rows(sent, bring_query)
    else:
        gathered = gather_rows(sent)
    gathered_rows = gathered[:, :MODEL_WIDTH]
    all_digits = gathered[:, MODEL_WIDTH : MODEL_WIDTH + 2].astype(jnp.int32)
    slot_ids = all_digits[:, 0] * 32 + all_digits[:, 1]
    request_total = gathered_rows.shape[0]

    owner_mask = (
        slot_ids[:, None] == first_slot + jnp.arange(own_slots, dtype=jnp.int32)[None, :]
    )
    bf_zero = jnp.zeros((), jnp.bfloat16)

    query_width = MODEL_WIDTH
    if aligned:
        kept, given = query_halves(
            where,
            gathered,
            query_near,
            key_value_weight,
            by_rank(query_down_factor),
            query_up_factor.reshape(own_slots * ADAPTER_RANK, -1),
            count,
            local_rows,
        )
        query_rows, keyval_rows = scatter_chips(kept + swap_cores(given), query_width)
    else:
        query_shrunk = owner_shrunk(gathered_rows, query_down_factor, owner_mask)
        lifted_rows = jnp.where(owner_mask[:, :, None], query_shrunk[:, None, :], bf_zero).reshape(
            request_total, own_slots * ADAPTER_RANK
        )
        query_delta = adapter_scale * jnp.dot(
            lifted_rows,
            query_up_factor.reshape(own_slots * ADAPTER_RANK, -1),
            preferred_element_type=jnp.float32,
        )
        kept_delta, given_delta = core_halves(query_delta)
        received_delta = swap_cores(given_delta)
        base = jnp.concatenate(
            [
                jnp.dot(gathered_rows, query_weight, preferred_element_type=jnp.float32),
                jnp.dot(gathered_rows, key_value_weight, preferred_element_type=jnp.float32),
            ],
            axis=1,
        )
        kept_base, given_base = core_halves(base)
        received_base = swap_cores(given_base)
        pair_query = pair_columns(kept_base[:, :, :col_width], received_base[:, :, :col_width])
        pair_keyval = pair_columns(kept_base[:, :, col_width:], received_base[:, :, col_width:])
        pair_delta = kept_delta + received_delta
        first_column = (lax.axis_index("pool") // 2) * (2 * col_width)
        there = lax.dynamic_slice_in_dim(pair_delta, first_column, 2 * col_width, 2)
        pair_delta = lax.dynamic_update_slice_in_dim(pair_delta, there + pair_query, first_column, 2)
        leaving = jnp.concatenate([pair_delta, pair_keyval], axis=2)
        arrived = exchange_chips(leaving)
        query_rows = jnp.sum(arrived[:, :, :query_width], axis=0).astype(jnp.bfloat16)
        keyval_rows = arrived[:, :, query_width:].astype(jnp.bfloat16)
        keyval_rows = keyval_rows.reshape(count // 2, local_rows, 2, -1)
        keyval_rows = keyval_rows.transpose(1, 0, 2, 3).reshape(local_rows, -1)

    attention_output = attend(query_rows, keyval_rows, key_cache, value_cache, lengths)
    if aligned:

        def bring_output(rows):
            now, _ = lax.optimization_barrier((where, rows))
            return bring(now, [output_weight])

        every_row, (output_near,) = gather_rows(attention_output, bring_output)
    else:
        every_row = gather_rows(attention_output)
    if aligned:
        kept, given = output_halves(
            where,
            every_row,
            gathered,
            output_near,
            by_rank(output_down_factor),
            output_up_factor.reshape(own_slots * ADAPTER_RANK, -1),
            count,
            local_rows,
        )
    else:
        out_width = output_weight.shape[0]
        columns = lax.dynamic_slice_in_dim(every_row, lax.axis_index("pool") * out_width, out_width, 1)
        output_shrunk = owner_shrunk(every_row, output_down_factor, owner_mask)
        lifted_rows = jnp.where(owner_mask[:, :, None], output_shrunk[:, None, :], bf_zero).reshape(
            request_total, own_slots * ADAPTER_RANK
        )
        up_rows = output_up_factor.reshape(own_slots * ADAPTER_RANK, MODEL_WIDTH)
        partial = jnp.dot(
            columns, output_weight, preferred_element_type=jnp.float32
        ) + adapter_scale * jnp.dot(lifted_rows, up_rows, preferred_element_type=jnp.float32)
        kept, given = core_halves(partial)
    pair_sums = (kept + swap_cores(given)).astype(jnp.bfloat16)
    arrived = exchange_chips(pair_sums).astype(jnp.float32)
    return jnp.sum(arrived, axis=0).astype(jnp.bfloat16)


def solution(mesh):
    placed = (
        P(("groups", "pool"), None),
        P(),
        P(None, "pool"),
        P(None, "pool"),
        P("pool", None),
        P(("groups", "pool"), None, None),
        P(("groups", "pool"), None, None),
        P(("groups", "pool"), None, None),
        P(("groups", "pool"), None, None),
        P(("groups", "pool"), None, None),
        P(("groups", "pool"), None, None),
        P(("groups", "pool")),
        P(("groups", "pool")),
        P("groups"),
    )
    return jax.shard_map(
        body, mesh=mesh, in_specs=placed, out_specs=P(("groups", "pool"), None), check_vma=False
    )
```
